32 devices in a mesh: row: 8 (over y, x, core), col: 4 (over z).
Axes of the slice: x: 2, y: 2, z: 4, core: 2. Of those that a mesh axis runs over, the one named last changes fastest.
Arguments:
- fine_input: bfloat16 [1, 256, 512, 256], P(None, 'row', 'col'), may hold values from -6 to 6
- coarse_feat: bfloat16 [1, 64, 128, 256], P(None, ('row', 'col')), may hold values from -6 to 6
- conv_weight: bfloat16 [3, 3, 256, 256], replicated, may hold values from -0.125 to 0.125
- step_scale: float32 [1000, 256], replicated, may hold values from 0.5 to 2
- timesteps: int32 [1], replicated, may hold values from 0 to 999
- cotangent: bfloat16 [1, 256, 512, 256], P(None, 'row', 'col'), may hold values from -6 to 6
Outputs:
- grad_fine: bfloat16 [1, 256, 512, 256], P(None, 'row', 'col')
- grad_coarse: bfloat16 [1, 64, 128, 256], P(None, ('row', 'col'))
- grad_weight: float32 [3, 3, 256, 256], replicated
The draws below stay inside these ranges and needn't reach their ends.
All inputs are finite; a program needn't handle non-finite values.
Results may differ from the reference program's by a relative error of at most 0.013.
Values may be sent and summed in bfloat16 or wider, within the bound.
No kernel may reach another device: no remote copies, remote signals or barrier semaphores. Data moves between devices by JAX's collectives and lax.ppermute only.
A program may use at most 128 MiB of HBM per device.

```python
import math
import jax
import jax.numpy as jnp
from jax import lax

C = 256
TSTEPS = 1000
FR = 1
HF = 256
WF = 512
HC = 64
WC = 128


def shard_levels(rng, extent, split, smallest, top_value):
    def one(axis_at, blocks):
        heights = jax.random.uniform(jax.random.fold_in(jax.random.fold_in(rng, 6), axis_at), (blocks,), jnp.float32, smallest / len(split), top_value / len(split))
        return jnp.repeat(jnp.exp(heights), extent[axis_at] // blocks).reshape((-1,) + (1,) * (len(extent) - axis_at - 1))

    loudness = one(*split[0])
    for cut in split[1:]:
        loudness = loudness * one(*cut)
    return loudness


def centred(own_key, extent, width, most, cuts=(), kind=jnp.bfloat16):
    entries = width * jax.random.normal(own_key, extent, jnp.float32)
    if cuts:
        entries = entries * shard_levels(own_key, extent, cuts, -0.22, 0.18)
    return jnp.clip(entries, -most, most).astype(kind)


def setup_inputs(seed: int = 0) -> dict:
    arg_keys = jax.random.split(jax.random.key(seed), 7)
    fine_input = centred(arg_keys[0], (FR, HF, WF, C), 1.0, 6.0, ((1, 8), (2, 4)))
    coarse_feat = centred(arg_keys[1], (FR, HC, WC, C), 1.0, 6.0, ((1, 32),))
    conv_weight = centred(arg_keys[2], (3, 3, C, C), (9 * C) ** -0.5, 0.125)
    step_scale = jnp.clip(jnp.exp(jax.random.uniform(arg_keys[3], (TSTEPS, C), jnp.float32, math.log(0.5), math.log(2.0))), 0.5, 2.0)
    timesteps = jax.random.randint(arg_keys[4], (FR,), 0, TSTEPS).astype(jnp.int32)
    cotangent = centred(arg_keys[5], (FR, HF, WF, C), 1.0, 6.0, ((1, 8), (2, 4)))
    return dict(fine_input=fine_input, coarse_feat=coarse_feat, conv_weight=conv_weight, step_scale=step_scale, timesteps=timesteps, cotangent=cotangent)


def reference(fine_input, coarse_feat, conv_weight, step_scale, timesteps, cotangent):
    upper = jnp.repeat(jnp.repeat(coarse_feat.astype(jnp.float32), 4, axis=1), 4, axis=2)
    hidden = fine_input.astype(jnp.float32) + upper
    sig = jax.nn.sigmoid(hidden)
    act = (hidden * sig).astype(jnp.bfloat16)
    onehot = (timesteps[:, None] == jnp.arange(TSTEPS, dtype=jnp.int32)[None, :]).astype(jnp.float32)
    picked = jnp.dot(onehot, step_scale, precision=lax.Precision.HIGHEST)
    dpre = (cotangent.astype(jnp.float32) * picked[:, None, None, :]).astype(jnp.bfloat16)
    pad_act = jnp.pad(act, ((0, 0), (1, 1), (1, 1), (0, 0)))
    pad_grad = jnp.pad(dpre, ((0, 0), (1, 1), (1, 1), (0, 0)))
    flat_grad = dpre.reshape(-1, C)
    rows_w = []
    dact = jnp.zeros((FR * HF * WF, C), jnp.float32)
    for i in range(3):
        taps = []
        for j in range(3):
            window = pad_act[:, i:i + HF, j:j + WF, :].reshape(-1, C)
            taps.append(lax.dot_general(window, flat_grad, (((0,), (0,)), ((), ())), preferred_element_type=jnp.float32))
            moved = pad_grad[:, 2 - i:2 - i + HF, 2 - j:2 - j + WF, :].reshape(-1, C)
            dact = dact + lax.dot_general(moved, conv_weight[i, j], (((1,), (1,)), ((), ())), preferred_element_type=jnp.float32)
        rows_w.append(jnp.stack(taps))
    grad_weight = jnp.stack(rows_w) / jnp.sqrt(jnp.float32(FR * HF * WF))
    dhidden = dact.reshape(FR, HF, WF, C) * sig * (1.0 + hidden * (1.0 - sig))
    grad_fine = dhidden.astype(jnp.bfloat16)
    grad_coarse = dhidden.reshape(FR, HC, 4, WC, 4, C).sum(axis=(2, 4)).astype(jnp.bfloat16)
    return (grad_fine, grad_coarse, grad_weight)
```

```python
import functools
import jax
import jax.numpy as jnp
from jax import lax
from jax.experimental import pallas as pl
from jax.experimental.pallas import tpu as pltpu
from jax.sharding import PartitionSpec as P

BF = jnp.bfloat16
F32 = jnp.float32
MB = 1024 * 1024
START_MIB = 53.7
LOAD_MIB = 50


def smem():
    return pl.BlockSpec(memory_space=pltpu.SMEM)


def vmem():
    return pl.BlockSpec(memory_space=pltpu.VMEM)


def params(mib):
    return pltpu.CompilerParams(vmem_limit_bytes=int(mib * MB))


def cost(flops, nbytes):
    return pl.CostEstimate(flops=flops, bytes_accessed=nbytes, transcendentals=0)


def hbm():
    return pl.BlockSpec(memory_space=pltpu.HBM)


def place():
    row = lax.axis_index("row")
    return lax.rem(row, 2), row // 2, lax.axis_index("col")


def start_kernel(n, cot, coarse, ahead, behind, *refs):
    blocks, (rough, high, low, sems) = refs[: n - 2], refs[n - 2 :]
    _, _, me = place()
    cr, _, ch = rough.shape
    rows, width, _ = cot.shape
    cols = rough.shape[1] // n
    pairs = (coarse, rough), (cot.at[:, width - 16 :, :], high), (cot.at[:, :16, :], low)
    copies = [pltpu.make_async_copy(*pair, sems.at[k]) for k, pair in enumerate(pairs)]
    for c in copies:
        c.start()
    copies[0].wait()
    outs = [blocks[0], ahead, *blocks[1:], behind]
    for s, out in enumerate(outs):
        start = pl.multiple_of(lax.rem(me + s, n) * cols, cols)
        for j in range(cr):
            out[j * cols : (j + 1) * cols, :] = rough[j, pl.ds(start, cols), :]
    r = lax.broadcasted_iota(jnp.int32, (rows, rows * 16), 0)
    p = lax.broadcasted_iota(jnp.int32, (rows, rows * 16), 1)
    for out, edge, pick, c in ((ahead, high, 15, copies[1]), (behind, low, 0, copies[2])):
        c.wait()
        sel = jnp.where(p == r * 16 + pick, 1.0, 0.0).astype(BF)
        col = jnp.dot(sel, edge[...].reshape(rows * 16, ch), preferred_element_type=F32)
        out[cr * cols :, :] = col.astype(BF)


def load_kernel(steps, cot, scales, near, scale, table, sems):
    rows = cot.shape[0]
    parts = sems.shape[0] - 1
    tall = rows // parts
    at = pl.multiple_of(steps[0] // 8 * 8, 8)
    pairs = [(scales.at[pl.ds(at, 8)], table)]
    pairs += [(cot.at[pl.ds(k * tall, tall)], near.at[pl.ds(k * tall, tall)]) for k in range(parts)]
    copies = [pltpu.make_async_copy(*pair, sems.at[k]) for k, pair in enumerate(pairs)]
    for c in copies:
        c.start()
    for c in copies:
        c.wait()
    scale[...] = table[pl.ds(lax.rem(steps[0], 8), 1), :]


def edge_kernel(n, offset, scale, cot, from_left, from_right, t_out, b_out, left, right):
    _, _, me = place()
    rows, width, _ = cot.shape
    sides = ((left, from_left, me > 0), (right, from_right, me < n - 1))
    for side, block, inside in sides:
        col = (block[offset:, :].astype(F32) * scale[...]).astype(BF).astype(F32)
        side[...] = jnp.where(inside, col, 0.0)
    idx = lax.broadcasted_iota(jnp.int32, (16, left.shape[1]), 0)
    for out, k in ((t_out, 0), (b_out, rows - 1)):
        out[:width, :] = (cot[k].astype(F32) * scale[...]).astype(BF)
        two = jnp.where(idx == 1, right[k : k + 1, :], 0.0)
        out[width:, :] = jnp.where(idx == 0, left[k : k + 1, :], two).astype(BF)


def gate(fine, coarse_row):
    width = fine.shape[1]
    cols = coarse_row.shape[0]
    a = lax.broadcasted_iota(jnp.int32, (width, cols), 0)
    b = lax.broadcasted_iota(jnp.int32, (width, cols), 1)
    up = jnp.where(a // (width // cols) == b, 1.0, 0.0).astype(BF)
    upper = jnp.dot(up, coarse_row, preferred_element_type=F32)
    hidden = fine.astype(F32) + upper[None]
    sig = 0.5 * jnp.tanh(0.5 * hidden) + 0.5
    return hidden, sig


def spread(moved, slot, rounded, left, right):
    width = rounded.shape[0]
    row = rounded.astype(F32)
    idx = lax.broadcasted_iota(jnp.int32, row.shape, 0)
    moved[0, slot] = jnp.where(idx == 0, left, pltpu.roll(row, 1, 0)).astype(BF)
    moved[1, slot] = rounded
    moved[2, slot] = jnp.where(idx == width - 1, right, pltpu.roll(row, width - 1, 0)).astype(BF)


def prepare_kernel(n, cr, scale, fine, cot, left, right, *refs):
    blocks, (act_t, moved, strip) = refs[:n], refs[n:]
    _, _, me = place()
    rows, width, ch = cot.shape
    cols = strip.shape[1]
    for s in range(n):
        src = lax.rem(me + n - s, n)
        for j in range(cr):
            strip[src * cr + j] = blocks[s][j * cols : (j + 1) * cols, :]

    def group(g, _):
        for q in range(4):
            r = g * 4 + q
            rounded = (cot[r].astype(F32) * scale[...]).astype(BF)
            spread(moved, r + 1, rounded, left[pl.ds(r, 1), :], right[pl.ds(r, 1), :])
        hidden, sig = gate(fine[pl.ds(g * 4, 4)], strip[g])
        act = (hidden * sig).astype(BF).reshape(4 * width, ch)
        act_t[:, pl.ds(pl.multiple_of(g * 4 * width, 4 * width), 4 * width)] = act.T
        return 0

    lax.fori_loop(0, rows // 4, group, 0)


def weight_kernel(act_t, above, below, moved_in, keep, send, moved):
    core, plane, z = place()
    _, rows, width, ch = moved.shape
    rows -= 2
    planes, zs, depth, half = keep.shape
    for slot, halo in ((0, above), (rows + 1, below)):
        ends = halo[width:, :].astype(F32)
        spread(moved, slot, halo[:width, :], ends[0:1], ends[1:2])
    step = ch // (planes * zs)
    z = lax.rem(z, zs)

    def tap(t, _):
        i, j = t // 3, lax.rem(t, 3)
        window = moved[2 - j, pl.ds(2 - i, rows)].reshape(rows * width, ch)
        acc = jnp.dot(act_t[...], window, preferred_element_type=F32)
        low, high = acc[:, :half], acc[:, half:]
        mine = jnp.where(core == 0, low, high).astype(BF)
        other = jnp.where(core == 0, high, low).astype(BF)
        at = pl.multiple_of(t * step, step)
        for p in range(planes):
            for c in range(zs):
                b = (p * zs + c) * step
                keep[p ^ plane, c ^ z, pl.ds(at, step), :] = mine[b : b + step]
                send[p ^ plane, c ^ z, pl.ds(at, step), :] = other[b : b + step]
        return 0

    lax.fori_loop(0, 9, tap, 0)


def input_kernel(first, size, n, after, moved, fine, strip, weight, *refs):
    gf, gc, fines, pooled, sems = refs[-5:]
    _, _, me = place()
    cr = strip.shape[0] // n
    _, width, ch = fine.shape
    cols = strip.shape[1]
    wide = jnp.concatenate([weight[t] for t in range(9)], axis=1)
    copies = []
    for g in range(size):
        k = ((n - 1 - (first + g) // cr) ^ me) * cr + (first + g) % cr
        r = 4 * k
        taps = [
            moved[2 - t % 3, pl.ds(2 - t // 3 + r, 4)].reshape(4 * width, ch) for t in range(9)
        ]
        dact = lax.dot_general(
            jnp.concatenate(taps, axis=1),
            wide,
            (((1,), (1,)), ((), ())),
            preferred_element_type=F32,
        ).reshape(4, width, ch)
        hidden, sig = gate(fine[pl.ds(r, 4)], strip[k])
        dhidden = dact * sig * (1.0 + hidden * (1.0 - sig))
        fines[g] = dhidden.astype(BF)
        tall = dhidden[0] + dhidden[1] + dhidden[2] + dhidden[3]
        for h in range(ch // 128):
            pooled[...] = tall[:, 128 * h : 128 * h + 128]
            every = [pooled[pl.ds(k, cols, stride=width // cols), :] for k in range(width // cols)]
            gc[g, :, 128 * h : 128 * h + 128] = functools.reduce(jnp.add, every).astype(BF)
        copies.append(pltpu.make_async_copy(fines.at[g], gf.at[pl.ds(r, 4)], sems.at[g]))
        copies[-1].start()
    for c in copies:
        c.wait()


def finish_kernel(norm, zs, spots, n, *refs):
    pieces, parts = refs[: len(spots)], refs[len(spots) : len(spots) + n]
    scratch, sems = refs[-2:]
    out = refs[-3] if not n else refs[-4]
    core, plane, me = place()
    planes = lax.axis_size("row") // 2
    ch = out.shape[1]
    half = ch // 2
    tall = ch // planes
    step = tall // zs
    z = lax.rem(me, zs)
    copies = []
    for k, (flip, s, first) in enumerate(spots):
        lanes = pl.ds(pl.multiple_of((core ^ flip) * half, half), half)
        for c in range(pieces[k].shape[0]):
            x = pieces[k][c].astype(F32) * norm
            for t in range(9):
                scratch[k, c, t] = x[t * step : (t + 1) * step]
            b = pl.multiple_of((plane ^ s) * tall + ((first + c) ^ z) * step, step)
            copies.append(
                pltpu.make_async_copy(
                    scratch.at[k, c], out.at[:, pl.ds(b, step), lanes], sems.at[k, c]
                )
            )
            copies[-1].start()
    if n:
        coarse = refs[-3]
        cols = parts[0].shape[1]
        for s in range(n):
            start = pl.multiple_of((me ^ s) * cols, cols)
            coarse[:, pl.ds(start, cols), :] = parts[s][...]
    for c in copies:
        c.wait()


def xor_pairs(count, bit):
    return [(i, i ^ bit) for i in range(count)]


def per_device(fine_input, coarse_feat, conv_weight, step_scale, timesteps, cotangent):
    _, rows, width, ch = fine_input.shape
    n = lax.axis_size("col")
    nrow = lax.axis_size("row")
    planes = nrow // 2
    cr = coarse_feat.shape[1]
    cols = width // 4
    fine, cot, coarse = fine_input[0], cotangent[0], coarse_feat[0]
    weight = conv_weight.reshape(9, ch, ch)

    def shape(*dims, dtype=BF):
        return jax.ShapeDtypeStruct(dims, dtype)

    block, packed = shape(cr * cols, ch), shape(cr * cols + rows, ch)
    ahead, behind, *blocks = pl.pallas_call(
        functools.partial(start_kernel, n),
        out_shape=[packed, packed] + [block] * (n - 2),
        in_specs=[hbm(), hbm()],
        out_specs=[vmem()] * n,
        scratch_shapes=[
            pltpu.VMEM(coarse.shape, BF),
            pltpu.VMEM((rows, 16, ch), BF),
            pltpu.VMEM((rows, 16, ch), BF),
            pltpu.SemaphoreType.DMA((3,)),
        ],
        compiler_params=params(START_MIB),
        cost_estimate=cost(1 << 20, 1 << 20),
        name="start",
    )(cot, coarse)
    cot, scale = pl.pallas_call(
        load_kernel,
        out_shape=[shape(*cot.shape), shape(1, ch, dtype=F32)],
        in_specs=[smem(), hbm(), hbm()],
        out_specs=[vmem()] * 2,
        scratch_shapes=[pltpu.VMEM((8, ch), F32), pltpu.SemaphoreType.DMA((9,))],
        compiler_params=params(LOAD_MIB),
        cost_estimate=cost(1 << 20, 4 << 20),
        name="load",
    )(timesteps, cot, step_scale)

    def turn(x, s):
        return lax.ppermute(x, "col", [(i, (i + s) % n) for i in range(n)])

    from_left, from_right = turn(ahead, 1), turn(behind, n - 1)
    blocks = [blocks[0], from_left]+[turn(blocks[s - 1], s) for s in range(2, n - 1)] + [from_right]

    halo, side = shape(width + 16, ch), shape(rows, ch, dtype=F32)
    top, bottom, left, right = pl.pallas_call(
        functools.partial(edge_kernel, n, cr * cols),
        out_shape=[halo, halo, side, side],
        in_specs=[vmem()] * 4,
        out_specs=[vmem()] * 4,
        compiler_params=params(4),
        cost_estimate=cost(1 << 18, 1 << 19),
        name="edges",
    )(scale, cot, from_left, from_right)
    row_up = [(i, i + 1) for i in range(nrow - 1)]
    above = lax.ppermute(bottom, "row", row_up)
    below = lax.ppermute(top, "row", [(j, i) for i, j in row_up])

    groups = rows // 4
    act_t, moved, strip = pl.pallas_call(
        functools.partial(prepare_kernel, n, cr),
        out_shape=[
            shape(ch, rows * width),
            shape(3, rows + 2, width, ch),
            shape(groups, cols, ch),
        ],
        in_specs=[vmem()] * (5 + n),
        out_specs=[vmem()] * 3,
        compiler_params=params(8),
        cost_estimate=cost(1 << 32, 4 << 20),
        name="prepare",
    )(scale, fine, cot, left, right, *blocks)

    halves = n // 2
    aligned = ch // (planes * halves) % 16 == 0
    zs = halves if aligned else 1
    depth = 9 * ch // (planes * zs)
    half = ch // 2
    part = shape(planes, zs, depth, half)
    keep, send, moved = pl.pallas_call(
        weight_kernel,
        out_shape=[part, part, shape(*moved.shape)],
        in_specs=[vmem()] * 4,
        out_specs=[vmem()] * 3,
        input_output_aliases={3: 2},
        compiler_params=params(8),
        cost_estimate=cost(2 * 9 * rows * width * ch * ch, 8 << 20),
        name="weight_grad",
    )(act_t, above, below, moved)

    done, pooled, made = [], [], 0

    def input_piece(size, after):
        nonlocal done, made
        *done, gc = pl.pallas_call(
            functools.partial(input_kernel, made, size, n),
            out_shape=[shape(rows, width, ch), shape(size, cols, ch)],
            in_specs=[pl.BlockSpec(memory_space=pl.ANY)]
            + [vmem()] * 4
            + [pl.BlockSpec(memory_space=pl.ANY) for _ in done],
            out_specs=[pl.BlockSpec(memory_space=pl.ANY), vmem()],
            input_output_aliases={5: 0} if done else {},
            scratch_shapes=[
                pltpu.VMEM((size, 4, width, ch), BF),
                pltpu.VMEM((width, 128), F32),
                pltpu.SemaphoreType.DMA((size,)),
            ],
            compiler_params=params(12),
            cost_estimate=cost(2 * 9 * 4 * size * width * ch * ch, 4 << 20),
            name="input_grad",
        )(after, moved, fine, strip, weight, *done)
        pooled.append(gc)
        made += size

    def beside(got, size, after):
        nonlocal done, pooled
        if size:
            input_piece(size, after)
            got, done, pooled = lax.optimization_barrier((got, done, pooled))
        return got

    parts = {}

    def pooled_strip(s):
        rows_done = [x[g : g + 1] for x in pooled for g in range(x.shape[0])]
        return jnp.concatenate(rows_done[(n - 1 - s) * cr : (n - s) * cr])

    def send_pooled(got, limit):
        nonlocal parts
        ready = [s for s in range(n - 1, 0, -1) if s not in parts and (n - s) * cr <= made]
        for s in ready[:limit]:
            parts[s] = col_swap(pooled_strip(s), s)
        if ready:
            got, parts = lax.optimization_barrier((got, parts))
        return got

    def add(*terms):
        return functools.reduce(jnp.add, [t.astype(F32) for t in terms]).astype(BF)

    def core_swap(x):
        return lax.ppermute(x, "row", xor_pairs(nrow, 1))

    def plane_swap(x, s):
        return lax.ppermute(x, "row", xor_pairs(nrow, 2 * s))

    def col_swap(x, s):
        return lax.ppermute(x, "col", xor_pairs(n, s))

    sizes = piece_sizes(rows // 4)
    total = add(keep, *beside([core_swap(send)], sizes[0], send))
    got = [plane_swap(total[s], s) for s in range(1, planes)]
    total = add(total[0], *beside(got, sizes[1], total))
    if not aligned:
        order = jnp.arange(halves) ^ (lax.axis_index("col") % halves)
        total = total.reshape(halves, depth // halves, half)[order]
    bit = halves // 2
    while bit:
        got = [col_swap(total[bit:], bit)]
        if bit == 1:
            got = send_pooled(got, n // 2)
        total = add(total[:bit], *got)
        bit //= 2
    got = [col_swap(total, halves)]
    got = send_pooled(got, n)
    total = add(total, *beside(got, sizes[2], total))
    bit = 1
    while bit < (halves // 2 if aligned else halves):
        total = jnp.concatenate([total, col_swap(total, bit)])
        bit *= 2
    if not aligned:
        total = total[order].reshape(1, depth, half)
    ways = list(range(planes - 1, 0, -1))
    near = [total] + [plane_swap(total, s) for s in ways]
    waves = [near] + ([[col_swap(x, bit) for x in near]] if aligned else [])
    missing = [s for s in range(1, n) if s not in parts]
    parts.update({s: col_swap(pooled_strip(s), s) for s in missing})
    parts[0] = pooled_strip(0)
    pixels = rows * nrow * width * n

    def finish(out, pieces, spots, parts=()):
        coarse = [shape(cr, n * cols, ch)] if parts else []
        count, tall = len(pieces), pieces[0].shape[0]
        return pl.pallas_call(
            functools.partial(finish_kernel, float(pixels) ** -0.5, zs, spots, len(parts)),
            out_shape=[shape(9, ch, ch, dtype=F32)] + coarse,
            in_specs=[vmem()] * (count + len(parts)) + [hbm() for _ in out],
            out_specs=[hbm()] + [vmem() for _ in coarse],
            input_output_aliases={count + len(parts): 0} if out else {},
            scratch_shapes=[
                pltpu.VMEM((count, tall, 9, depth // 9, half), F32),
                pltpu.SemaphoreType.DMA((count, tall)),
            ],
            compiler_params=params(8),
            cost_estimate=cost(1 << 20, 4 << 20),
            name="finish",
        )(*pieces, *parts, *out)

    *out, grad_coarse = finish([], near[:1], ((0, 0, 0),), [parts[s] for s in range(n)])
    for k, wave in enumerate(waves):
        final = k + 1 == len(waves)
        spots = [(s, k * total.shape[0]) for s in [0] + ways]
        heads = wave[:-1] if final else wave
        swapped = core_swap(jnp.stack(heads))
        others = [swapped[i] for i in range(len(heads))]
        here = list(zip(wave, spots))[1 if k == 0 else 0 :]
        there = list(zip(others, spots))
        pieces = [x for x, _ in here + there]
        places = [(0, *spot) for _, spot in here] + [(1, *spot) for _, spot in there]
        out = finish(out, pieces, tuple(places))
        if final:
            out = finish(out, [core_swap(wave[-1])], ((1, *spots[-1]),))
    return (done[0][None], grad_coarse[None], out[0].reshape(3, 3, ch, ch))


def piece_sizes(groups):
    sizes = [groups // 8, groups * 5 // 8]
    return sizes + [groups - sum(sizes)]


def solution(mesh):
    return jax.shard_map(
        per_device,
        mesh=mesh,
        in_specs=(
            P(None, "row", "col", None),
            P(None, ("row", "col"), None, None),
            P(),
            P(),
            P(),
            P(None, "row", "col", None),
        ),
        out_specs=(P(None, "row", "col", None), P(None, ("row", "col"), None, None), P()),
        check_vma=False,
    )
```

```python
import functools
import jax
import jax.numpy as jnp
from jax import lax
from jax.experimental import pallas as pl
from jax.experimental.pallas import tpu as pltpu
from jax.sharding import PartitionSpec as P

BF = jnp.bfloat16
F32 = jnp.float32
MB = 1024 * 1024
START_MIB = 53.7


def smem():
    return pl.BlockSpec(memory_space=pltpu.SMEM)


def vmem():
    return pl.BlockSpec(memory_space=pltpu.VMEM)


def params(mib):
    return pltpu.CompilerParams(vmem_limit_bytes=int(mib * MB))


def cost(flops, nbytes):
    return pl.CostEstimate(flops=flops, bytes_accessed=nbytes, transcendentals=0)


def hbm():
    return pl.BlockSpec(memory_space=pltpu.HBM)


def place():
    row = lax.axis_index("row")
    return lax.rem(row, 2), row // 2, lax.axis_index("col")


def is_edge(s):
    return s & (s + 1) == 0


def start_kernel(n, cot, coarse, *refs):
    outs, (rough, low, high, sems) = refs[:n], refs[n:]
    _, _, me = place()
    cr, _, ch = rough.shape
    rows, width, _ = cot.shape
    cols = rough.shape[1] // n
    pairs = (coarse, rough), (cot.at[:, :16, :], low), (cot.at[:, width - 16 :, :], high)
    copies = [pltpu.make_async_copy(*pair, sems.at[k]) for k, pair in enumerate(pairs)]
    for c in copies:
        c.start()
    copies[0].wait()
    for s, out in enumerate(outs):
        start = pl.multiple_of((me ^ s) * cols, cols)
        for j in range(cr):
            out[j * cols : (j + 1) * cols, :] = rough[j, pl.ds(start, cols), :]
    r = lax.broadcasted_iota(jnp.int32, (rows, rows * 16), 0)
    p = lax.broadcasted_iota(jnp.int32, (rows, rows * 16), 1)
    sides = []
    for c, edge, pick in ((copies[1], low, 0), (copies[2], high, 15)):
        c.wait()
        sel = jnp.where(p == r * 16 + pick, 1.0, 0.0).astype(BF)
        flat = edge[...].reshape(rows * 16, ch)
        sides.append(jnp.dot(sel, flat, preferred_element_type=F32))
    for s in range(1, n):
        if is_edge(s):
            col = jnp.where((me ^ s) > me, sides[1], sides[0])
            outs[s][cr * cols :, :] = col.astype(BF)


def load_kernel(steps, cot, scales, moved, scale):
    rows, width, ch = cot.shape
    by = scales[pl.ds(steps[0], 1), :]
    scale[...] = by
    zero = jnp.zeros((1, ch), F32)

    def group(g, _):
        for q in range(4):
            r = g * 4 + q
            spread(moved, r + 1, (cot[r].astype(F32) * by).astype(BF), zero, zero)
        return 0

    lax.fori_loop(0, rows // 4, group, 0)


def edge_kernel(offset, shifts, scale, moved, *refs):
    blocks, (one, two, left, right) = refs[: len(shifts)], refs[len(shifts) :]
    core, _, me = place()
    _, rows, width, ch = moved.shape
    rows -= 2
    by = scale[...]
    for side, place_of in ((left, me - 1), (right, me + 1)):
        col = jnp.zeros((rows, ch), F32)
        for s, block in zip(shifts, blocks):
            edge = (block[offset:, :].astype(F32) * by).astype(BF).astype(F32)
            col = jnp.where((me ^ s) == place_of, edge, col)
        side[...] = col
    idx = lax.broadcasted_iota(jnp.int32, (16, ch), 0)
    ends = []
    for k in (0, rows - 1):
        tip = jnp.where(idx == 1, right[k : k + 1, :], 0.0)
        tip = jnp.where(idx == 0, left[k : k + 1, :], tip)
        ends.append((moved[1, k + 1].astype(F32), tip))
    (top, top_tip), (bottom, bottom_tip) = ends
    for out, first in ((one, core == 1), (two, core == 0)):
        out[:width, :] = jnp.where(first, top, bottom).astype(BF)
        out[width:, :] = jnp.where(first, top_tip, bottom_tip).astype(BF)


def spread_up(coarse_row, width):
    cols = coarse_row.shape[0]
    a = lax.broadcasted_iota(jnp.int32, (width, cols), 0)
    b = lax.broadcasted_iota(jnp.int32, (width, cols), 1)
    up = jnp.where(a // (width // cols) == b, 1.0, 0.0).astype(BF)
    return jnp.dot(up, coarse_row, preferred_element_type=F32)


def sigmoid(x):
    return 0.5 * jnp.tanh(0.5 * x) + 0.5


def gate(fine, coarse_row):
    hidden = fine.astype(F32) + spread_up(coarse_row, fine.shape[1])[None]
    return hidden, sigmoid(hidden)


def spread(moved, slot, rounded, left, right):
    width = rounded.shape[0]
    row = rounded.astype(F32)
    idx = lax.broadcasted_iota(jnp.int32, row.shape, 0)
    moved[0, slot] = jnp.where(idx == 0, left, pltpu.roll(row, 1, 0)).astype(BF)
    moved[1, slot] = rounded
    moved[2, slot] = jnp.where(idx == width - 1, right, pltpu.roll(row, width - 1, 0)).astype(BF)


def prepare_kernel(n, cr, fine, left, right, moved_in, *refs):
    blocks, (moved, act_t, strip, up) = refs[:n], refs[n:]
    _, _, me = place()
    rows, width, ch = fine.shape
    cols = strip.shape[1]
    for s in range(n):
        for j in range(cr):
            strip[(me ^ s) * cr + j] = blocks[s][j * cols : (j + 1) * cols, :]
    idx = lax.broadcasted_iota(jnp.int32, (16, ch), 0)

    def group(g, _):
        up[...] = spread_up(strip[g], width)
        for q in range(4):
            r = g * 4 + q
            for k, low, pick, side in ((0, 0, 0, left), (2, width - 16, 15, right)):
                tile = moved[k, r + 1, low : low + 16, :].astype(F32)
                tile = jnp.where(idx == pick, side[pl.ds(r, 1), :], tile)
                moved[k, r + 1, low : low + 16, :] = tile.astype(BF)
            hidden = fine[r].astype(F32) + up[...]
            act = (hidden * sigmoid(hidden)).astype(BF)
            act_t[:, pl.ds(pl.multiple_of(r * width, width), width)] = act.T
        return 0

    lax.fori_loop(0, rows // 4, group, 0)


def weight_kernel(act_t, one, two, moved_in, keep, send, moved):
    core, plane, z = place()
    _, rows, width, ch = moved.shape
    rows -= 2
    planes, zs, depth, half = keep.shape
    for slot, first in ((0, core == 1), (rows + 1, core == 0)):
        halo = jnp.where(first, one[...].astype(F32), two[...].astype(F32))
        spread(moved, slot, halo[:width].astype(BF), halo[width : width + 1], halo[width + 1 : width + 2])
    step = ch // (planes * zs)
    z = lax.rem(z, zs)

    def tap(t, _):
        i, j = t // 3, lax.rem(t, 3)
        window = moved[2 - j, pl.ds(2 - i, rows)].reshape(rows * width, ch)
        acc = jnp.dot(act_t[...], window, preferred_element_type=F32)
        low, high = acc[:, :half], acc[:, half:]
        mine = jnp.where(core == 0, low, high).astype(BF)
        other = jnp.where(core == 0, high, low).astype(BF)
        at = pl.multiple_of(t * step, step)
        for p in range(planes):
            for c in range(zs):
                b = (p * zs + c) * step
                keep[p ^ plane, c ^ z, pl.ds(at, step), :] = mine[b : b + step]
                send[p ^ plane, c ^ z, pl.ds(at, step), :] = other[b : b + step]
        return 0

    lax.fori_loop(0, 9, tap, 0)


def strip_order(n):
    return list(range(n - 1, 0, -2)) + list(range(n - 2, -1, -2))


def input_kernel(first, size, n, after, moved, fine, strip, weight, *refs):
    gf, gc, fines, pooled, sems = refs[-5:]
    _, _, me = place()
    cr = strip.shape[0] // n
    _, width, ch = fine.shape
    cols = strip.shape[1]
    wide = jnp.concatenate([weight[t] for t in range(9)], axis=1)
    copies = []
    for g in range(size):
        k = (strip_order(n)[(first + g) // cr] ^ me) * cr + (first + g) % cr
        r = 4 * k
        taps = [
            moved[2 - t % 3, pl.ds(2 - t // 3 + r, 4)].reshape(4 * width, ch) for t in range(9)
        ]
        dact = lax.dot_general(
            jnp.concatenate(taps, axis=1),
            wide,
            (((1,), (1,)), ((), ())),
            preferred_element_type=F32,
        ).reshape(4, width, ch)
        hidden, sig = gate(fine[pl.ds(r, 4)], strip[k])
        dhidden = dact * sig * (1.0 + hidden * (1.0 - sig))
        fines[g] = dhidden.astype(BF)
        tall = dhidden[0] + dhidden[1] + dhidden[2] + dhidden[3]
        for h in range(ch // 128):
            pooled[...] = tall[:, 128 * h : 128 * h + 128]
            every = [pooled[pl.ds(k, cols, stride=width // cols), :] for k in range(width // cols)]
            gc[g, h] = functools.reduce(jnp.add, every).astype(BF)
        copies.append(pltpu.make_async_copy(fines.at[g], gf.at[pl.ds(r, 4)], sems.at[g]))
        copies[-1].start()
    for c in copies:
        c.wait()


def finish_kernel(norm, zs, spots, n, *refs):
    pieces, parts = refs[: len(spots)], refs[len(spots) : len(spots) + n]
    if n:
        out, coarse_out, scratch, sems, coarse, coarse_sem = refs[-6:]
    else:
        out, scratch, sems = refs[-3:]
    core, plane, me = place()
    planes = lax.axis_size("row") // 2
    ch = out.shape[1]
    half = ch // 2
    tall = ch // planes
    step = tall // zs
    z = lax.rem(me, zs)
    copies = []
    for k, (flip, s, first) in enumerate(spots):
        lanes = pl.ds(pl.multiple_of((core ^ flip) * half, half), half)
        for c in range(pieces[k].shape[0]):
            x = pieces[k][c].astype(F32) * norm
            for t in range(9):
                scratch[k, c, t] = x[t * step : (t + 1) * step]
            b = pl.multiple_of((plane ^ s) * tall + ((first + c) ^ z) * step, step)
            copies.append(
                pltpu.make_async_copy(
                    scratch.at[k, c], out.at[:, pl.ds(b, step), lanes], sems.at[k, c]
                )
            )
            copies[-1].start()
    if n:
        cr = coarse.shape[0]
        cols = coarse.shape[1] // n
        for s in range(n):
            start = pl.multiple_of((me ^ s) * cols, cols)
            for j in range(cr):
                for h in range(2):
                    b = (j * 2 + h) * cols
                    coarse[j, pl.ds(start, cols), pl.ds(h * half, half)] = parts[s][b : b + cols]
        copies.append(pltpu.make_async_copy(coarse, coarse_out, coarse_sem.at[0]))
        copies[-1].start()
    for c in copies:
        c.wait()


def xor_pairs(count, bit):
    return [(i, i ^ bit) for i in range(count)]


def per_device(fine_input, coarse_feat, conv_weight, step_scale, timesteps, cotangent):
    _, rows, width, ch = fine_input.shape
    n = lax.axis_size("col")
    nrow = lax.axis_size("row")
    planes = nrow // 2
    cr = coarse_feat.shape[1]
    cols = width // 4
    fine, cot, coarse = fine_input[0], cotangent[0], coarse_feat[0]
    weight = conv_weight.reshape(9, ch, ch)

    def shape(*dims, dtype=BF):
        return jax.ShapeDtypeStruct(dims, dtype)

    def col_swap(x, s):
        return lax.ppermute(x, "col", xor_pairs(n, s))

    blocks = pl.pallas_call(
        functools.partial(start_kernel, n),
        out_shape=[shape(cr * cols + (rows if s and is_edge(s) else 0), ch) for s in range(n)],
        in_specs=[hbm(), hbm()],
        out_specs=[vmem()] * n,
        scratch_shapes=[
            pltpu.VMEM(coarse.shape, BF),
            pltpu.VMEM((rows, 16, ch), BF),
            pltpu.VMEM((rows, 16, ch), BF),
            pltpu.SemaphoreType.DMA((3,)),
        ],
        compiler_params=params(START_MIB),
        cost_estimate=cost(1 << 20, 4 << 20),
        name="start",
    )(cot, coarse)
    blocks = list(blocks)
    moved, scale = pl.pallas_call(
        load_kernel,
        out_shape=[shape(3, rows + 2, width, ch), shape(1, ch, dtype=F32)],
        in_specs=[smem(), vmem(), vmem()],
        out_specs=[vmem()] * 2,
        compiler_params=params(4),
        cost_estimate=cost(1 << 20, 4 << 20),
        name="load",
    )(timesteps, cot, step_scale)

    shifts = [s for s in range(1, n) if is_edge(s)]
    for s in shifts + [s for s in range(1, n) if not is_edge(s)]:
        blocks[s] = col_swap(blocks[s], s)

    halo, side = shape(width + 16, ch), shape(rows, ch, dtype=F32)
    one, two, left, right = pl.pallas_call(
        functools.partial(edge_kernel, cr * cols, shifts),
        out_shape=[halo, halo, side, side],
        in_specs=[vmem()] * (2 + len(shifts)),
        out_specs=[vmem()] * 4,
        compiler_params=params(4),
        cost_estimate=cost(1 << 18, 1 << 19),
        name="edges",
    )(scale, moved, *[blocks[s] for s in shifts])
    one = lax.ppermute(one, "row", xor_pairs(nrow, 1))
    odd = range(1, nrow - 1, 2)
    two = lax.ppermute(two, "row", [(i, i + 1) for i in odd] + [(i + 1, i) for i in odd])

    groups = rows // 4
    moved, act_t, strip = pl.pallas_call(
        functools.partial(prepare_kernel, n, cr),
        out_shape=[shape(*moved.shape), shape(ch, rows * width), shape(groups, cols, ch)],
        in_specs=[vmem()] * (4 + n),
        out_specs=[vmem()] * 3,
        input_output_aliases={3: 0},
        scratch_shapes=[pltpu.VMEM((width, ch), F32)],
        compiler_params=params(8),
        cost_estimate=cost(1 << 32, 4 << 20),
        name="prepare",
    )(fine, left, right, moved, *blocks)

    halves = n // 2
    aligned = ch // (planes * halves) % 16 == 0
    zs = halves if aligned else 1
    depth = 9 * ch // (planes * zs)
    half = ch // 2
    part = shape(planes, zs, depth, half)
    keep, send, moved = pl.pallas_call(
        weight_kernel,
        out_shape=[part, part, shape(*moved.shape)],
        in_specs=[vmem()] * 4,
        out_specs=[vmem()] * 3,
        input_output_aliases={3: 2},
        compiler_params=params(8),
        cost_estimate=cost(2 * 9 * rows * width * ch * ch, 8 << 20),
        name="weight_grad",
    )(act_t, one, two, moved)

    done, pooled, made = [], [], 0

    def input_piece(size, after):
        nonlocal done, made
        *done, gc = pl.pallas_call(
            functools.partial(input_kernel, made, size, n),
            out_shape=[shape(rows, width, ch), shape(size, 2, cols, ch // 2)],
            in_specs=[pl.BlockSpec(memory_space=pl.ANY)]
            + [vmem()] * 4
            + [pl.BlockSpec(memory_space=pl.ANY) for _ in done],
            out_specs=[pl.BlockSpec(memory_space=pl.ANY), vmem()],
            input_output_aliases={5: 0} if done else {},
            scratch_shapes=[
                pltpu.VMEM((size, 4, width, ch), BF),
                pltpu.VMEM((width, 128), F32),
                pltpu.SemaphoreType.DMA((size,)),
            ],
            compiler_params=params(12),
            cost_estimate=cost(2 * 9 * 4 * size * width * ch * ch, 4 << 20),
            name="input_grad",
        )(after, moved, fine, strip, weight, *done)
        pooled.append(gc)
        made += size

    def beside(got, size, after):
        nonlocal done, pooled
        if size:
            input_piece(size, after)
            got, done, pooled = lax.optimization_barrier((got, done, pooled))
        return got

    def pooled_strip(s):
        at = strip_order(n).index(s) * cr
        groups_done = [x[g] for x in pooled for g in range(x.shape[0])]
        return jnp.concatenate([x.reshape(-1, ch // 2) for x in groups_done[at : at + cr]])

    def add(*terms):
        return functools.reduce(jnp.add, [t.astype(F32) for t in terms]).astype(BF)

    def core_swap(x):
        return lax.ppermute(x, "row", xor_pairs(nrow, 1))

    def plane_swap(x, s):
        return lax.ppermute(x, "row", xor_pairs(nrow, 2 * s))

    sizes = piece_sizes(rows // 4)
    total = add(keep, *beside([core_swap(send)], sizes[0], send))
    got = [plane_swap(total[s], s) for s in range(1, planes)]
    total = add(total[0], *beside(got, sizes[1], total))
    if not aligned:
        order = jnp.arange(halves) ^ (lax.axis_index("col") % halves)
        total = total.reshape(halves, depth // halves, half)[order]
    bit = halves // 2
    while bit:
        got = [col_swap(total[bit:], bit)]
        total = add(total[:bit], *beside(got, sizes[2] if bit == 1 else 0, total))
        bit //= 2
    total = add(total, *beside([col_swap(total, halves)], sizes[3], total))

    strips = {s: [(0, pooled_strip(s))] for s in range(n)}

    def hop(bit, extra):
        sent = [(s, src, x) for s in strips if s & bit for src, x in strips[s]]
        got = col_swap(jnp.concatenate(extra + [x for _, _, x in sent]), bit)
        at = sum(x.shape[0] for x in extra)
        head = got[:at]
        for s, src, x in sent:
            strips.pop(s, None)
            strips[s ^ bit].append((src ^ bit, got[at : at + x.shape[0]]))
            at += x.shape[0]
        return head

    bit = 1
    while bit < halves // 2:
        head = hop(bit, [total.reshape(-1, half)])
        total = jnp.concatenate([total, head.reshape(total.shape)])
        bit *= 2
    head = hop(bit, [total.reshape(-1, half)])
    if aligned:
        waves = [total, head.reshape(total.shape)]
    else:
        total = jnp.concatenate([total, head.reshape(total.shape)])
        waves = [total[order].reshape(1, depth, half)]
    ways = list(range(planes - 1, 0, -1))
    waves = [[x] + [plane_swap(x, s) for s in ways] for x in waves]
    if aligned:
        waves[0][1:], waves[1][0] = lax.optimization_barrier((waves[0][1:], waves[1][0]))

    hop(bit * 2, [])
    parts = [x for _, x in sorted(strips[0], key=lambda pair: pair[0])]
    pixels = rows * nrow * width * n

    def finish(out, pieces, spots, parts=()):
        coarse = [shape(cr, n * cols, ch)] if parts else []
        count, tall = len(pieces), pieces[0].shape[0]
        return pl.pallas_call(
            functools.partial(finish_kernel, float(pixels) ** -0.5, zs, spots, len(parts)),
            out_shape=[shape(9, ch, ch, dtype=F32)] + coarse,
            in_specs=[vmem()] * (count + len(parts)) + [hbm() for _ in out],
            out_specs=[hbm()] + [hbm() for _ in coarse],
            input_output_aliases={count + len(parts): 0} if out else {},
            scratch_shapes=[
                pltpu.VMEM((count, tall, 9, depth // 9, half), F32),
                pltpu.SemaphoreType.DMA((count, tall)),
            ]
            + [x for c in coarse for x in (pltpu.VMEM(c.shape, BF), pltpu.SemaphoreType.DMA((1,)))],
            compiler_params=params(8),
            cost_estimate=cost(1 << 20, 4 << 20),
            name="finish",
        )(*pieces, *parts, *out)

    spots = [(s, k * wave[0].shape[0]) for k, wave in enumerate(waves) for s in [0] + ways]
    mine = [x for wave in waves for x in wave]
    other = []
    for wave in waves:
        swapped = core_swap(jnp.stack(wave))
        other += [swapped[i] for i in range(len(wave))]
    out = finish([], mine, tuple((0, *spot) for spot in spots))
    grad_weight, grad_coarse = finish(out, other, tuple((1, *spot) for spot in spots), parts)
    return (done[0][None], grad_coarse[None], grad_weight.reshape(3, 3, ch, ch))


def piece_sizes(groups):
    sizes = [groups // 8, groups * 5 // 8, groups // 8]
    return sizes + [groups - sum(sizes)]


def solution(mesh):
    return jax.shard_map(
        per_device,
        mesh=mesh,
        in_specs=(
            P(None, "row", "col", None),
            P(None, ("row", "col"), None, None),
            P(),
            P(),
            P(),
            P(None, "row", "col", None),
        ),
        out_specs=(P(None, "row", "col", None), P(None, ("row", "col"), None, None), P()),
        check_vma=False,
    )
```

```python
import functools
import jax
import jax.numpy as jnp
from jax import lax
from jax.experimental import pallas as pl
from jax.experimental.pallas import tpu as pltpu
from jax.sharding import PartitionSpec as P

BF = jnp.bfloat16
F32 = jnp.float32
MB = 1024 * 1024
START_MIB = 53.7


def smem():
    return pl.BlockSpec(memory_space=pltpu.SMEM)


def vmem():
    return pl.BlockSpec(memory_space=pltpu.VMEM)


def params(mib):
    return pltpu.CompilerParams(vmem_limit_bytes=int(mib * MB))


def cost(flops, nbytes):
    return pl.CostEstimate(flops=flops, bytes_accessed=nbytes, transcendentals=0)


def hbm():
    return pl.BlockSpec(memory_space=pltpu.HBM)


def place():
    row = lax.axis_index("row")
    return lax.rem(row, 2), row // 2, lax.axis_index("col")


def is_edge(s):
    return s & (s + 1) == 0


def start_kernel(n, cot, coarse, *refs):
    outs, (rough, low, high, sems) = refs[:n], refs[n:]
    _, _, me = place()
    cr, _, ch = rough.shape
    rows, width, _ = cot.shape
    cols = rough.shape[1] // n
    pairs = (coarse, rough), (cot.at[:, :16, :], low), (cot.at[:, width - 16 :, :], high)
    copies = [pltpu.make_async_copy(*pair, sems.at[k]) for k, pair in enumerate(pairs)]
    for c in copies:
        c.start()
    copies[0].wait()
    for s, out in enumerate(outs):
        start = pl.multiple_of((me ^ s) * cols, cols)
        for j in range(cr):
            out[j * cols : (j + 1) * cols, :] = rough[j, pl.ds(start, cols), :]
    r = lax.broadcasted_iota(jnp.int32, (rows, rows * 16), 0)
    p = lax.broadcasted_iota(jnp.int32, (rows, rows * 16), 1)
    sides = []
    for c, edge, pick in ((copies[1], low, 0), (copies[2], high, 15)):
        c.wait()
        sel = jnp.where(p == r * 16 + pick, 1.0, 0.0).astype(BF)
        flat = edge[...].reshape(rows * 16, ch)
        sides.append(jnp.dot(sel, flat, preferred_element_type=F32))
    for s in range(1, n):
        if is_edge(s):
            col = jnp.where((me ^ s) > me, sides[1], sides[0])
            outs[s][cr * cols :, :] = col.astype(BF)


def load_kernel(steps, cot, scales, moved, scale):
    rows, width, ch = cot.shape
    by = scales[pl.ds(steps[0], 1), :]
    scale[...] = by
    zero = jnp.zeros((1, ch), F32)

    def group(g, _):
        for q in range(4):
            r = g * 4 + q
            spread(moved, r + 1, (cot[r].astype(F32) * by).astype(BF), zero, zero)
        return 0

    lax.fori_loop(0, rows // 4, group, 0)


def edge_kernel(offset, shifts, scale, moved, *refs):
    blocks, (one, two, left, right) = refs[: len(shifts)], refs[len(shifts) :]
    core, _, me = place()
    _, rows, width, ch = moved.shape
    rows -= 2
    by = scale[...]
    for side, place_of in ((left, me - 1), (right, me + 1)):
        col = jnp.zeros((rows, ch), F32)
        for s, block in zip(shifts, blocks):
            edge = (block[offset:, :].astype(F32) * by).astype(BF).astype(F32)
            col = jnp.where((me ^ s) == place_of, edge, col)
        side[...] = col
    idx = lax.broadcasted_iota(jnp.int32, (16, ch), 0)
    ends = []
    for k in (0, rows - 1):
        tip = jnp.where(idx == 1, right[k : k + 1, :], 0.0)
        tip = jnp.where(idx == 0, left[k : k + 1, :], tip)
        ends.append((moved[1, k + 1].astype(F32), tip))
    (top, top_tip), (bottom, bottom_tip) = ends
    for out, first in ((one, core == 1), (two, core == 0)):
        out[:width, :] = jnp.where(first, top, bottom).astype(BF)
        out[width:, :] = jnp.where(first, top_tip, bottom_tip).astype(BF)


def spread_up(coarse_row, width):
    cols = coarse_row.shape[0]
    a = lax.broadcasted_iota(jnp.int32, (width, cols), 0)
    b = lax.broadcasted_iota(jnp.int32, (width, cols), 1)
    up = jnp.where(a // (width // cols) == b, 1.0, 0.0).astype(BF)
    return jnp.dot(up, coarse_row, preferred_element_type=F32)


def sigmoid(x):
    return 0.5 * jnp.tanh(0.5 * x) + 0.5


def gate(fine, coarse_row):
    hidden = fine.astype(F32) + spread_up(coarse_row, fine.shape[1])[None]
    return hidden, sigmoid(hidden)


def spread(moved, slot, rounded, left, right):
    width = rounded.shape[0]
    row = rounded.astype(F32)
    idx = lax.broadcasted_iota(jnp.int32, row.shape, 0)
    moved[0, slot] = jnp.where(idx == 0, left, pltpu.roll(row, 1, 0)).astype(BF)
    moved[1, slot] = rounded
    moved[2, slot] = jnp.where(idx == width - 1, right, pltpu.roll(row, width - 1, 0)).astype(BF)


def prepare_kernel(n, cr, fine, left, right, moved_in, *refs):
    blocks, (moved, act_t, strip, sums, mid, up) = refs[:n], refs[n:]
    core, _, me = place()
    rows, width, ch = fine.shape
    cols = strip.shape[1]
    for s in range(n):
        for j in range(cr):
            strip[(me ^ s) * cr + j] = blocks[s][j * cols : (j + 1) * cols, :]
    idx = lax.broadcasted_iota(jnp.int32, (16, ch), 0)

    def patch(r, _):
        for k, low, pick, side in ((0, 0, 0, left), (2, width - 16, 15, right)):
            tile = moved[k, r + 1, low : low + 16, :].astype(F32)
            tile = jnp.where(idx == pick, side[pl.ds(r, 1), :], tile)
            moved[k, r + 1, low : low + 16, :] = tile.astype(BF)
        return 0

    lax.fori_loop(0, rows, patch, 0)
    tall = rows // 4

    def build(c):
        for g in range(c * tall // 4, (c + 1) * tall // 4):
            up[g] = spread_up(strip[g], width)
            for r in range(4 * g, 4 * g + 4):
                hidden = fine[r].astype(F32) + up[g]
                act = (hidden * sigmoid(hidden)).astype(BF)
                act_t[:, r * width : (r + 1) * width] = act.T

    def share(c, first):
        for k in range(5):
            out = mid if k == 4 else sums.at[k]
            got = partial_tap(1 - core, k, c * tall, tall, act_t, moved)
            out[...] = got if first else out[...] + got

    build(1)
    build(2)
    share(1, True)
    build(0)
    share(2, False)
    build(3)


def partial_tap(part, k, row, tall, act_t, moved):
    _, _, width, ch = moved.shape
    half = ch // 2
    lhs = act_t[:, row * width : (row + tall) * width]
    if isinstance(k, int) and k == 4:
        lanes = pl.ds(pl.multiple_of(part * half, half), half)
        window = moved[1, 1 + row : 1 + row + tall, :, lanes]
    else:
        t = part * 5 + k
        window = moved[2 - lax.rem(t, 3), pl.ds(2 - t // 3 + row, tall)]
    return jnp.dot(lhs, window.reshape(tall * width, -1), preferred_element_type=F32)


def weight_taps(part, pieces, act_t, moved, out, sums=None, mid=None):
    _, plane, z = place()
    planes, zs, depth, half = out.shape
    ch = 2 * half
    step = ch // (planes * zs)
    z = lax.rem(z, zs)

    def put(unit, acc):
        at = pl.multiple_of(unit * step, step)
        for p in range(planes):
            for c in range(zs):
                b = (p * zs + c) * step
                out[p ^ plane, c ^ z, pl.ds(at, step), :] = acc[b : b + step].astype(BF)

    def total(k, start):
        got = [partial_tap(part, k, row, tall, act_t, moved) for row, tall in pieces]
        return functools.reduce(jnp.add, got if start is None else [start] + got)

    def tap(k, _):
        acc = total(k, None if sums is None else sums[k])
        put(k, acc[:, :half])
        put(k + 4, acc[:, half:])
        return 0

    lax.fori_loop(0, 4, tap, 0)
    put(8, total(4, None if mid is None else mid[...]))


def other_kernel(act_t, one, two, sums, mid, moved_in, out, moved):
    core, _, _ = place()
    _, rows, width, ch = moved.shape
    for slot, first in ((0, core == 1), (rows - 1, core == 0)):
        halo = jnp.where(first, one[...].astype(F32), two[...].astype(F32))
        left, right = halo[width : width + 1], halo[width + 1 : width + 2]
        spread(moved, slot, halo[:width].astype(BF), left, right)
    tall = (rows - 2) // 4
    weight_taps(1 - core, ((0, tall), (3 * tall, tall)), act_t, moved, out, sums, mid)


def mine_kernel(act_t, moved, out):
    core, _, _ = place()
    weight_taps(core, ((0, moved.shape[1] - 2),), act_t, moved, out)


def strip_order(n):
    return list(range(n - 1, 0, -2)) + list(range(n - 2, -1, -2))


def input_kernel(first, size, n, after, moved, fine, strip, weight, *refs):
    gf, gc, fines, pooled, sems = refs[-5:]
    _, _, me = place()
    cr = strip.shape[0] // n
    _, width, ch = fine.shape
    cols = strip.shape[1]
    wide = jnp.concatenate([weight[t] for t in range(9)], axis=1)
    copies = []
    for g in range(size):
        k = (strip_order(n)[(first + g) // cr] ^ me) * cr + (first + g) % cr
        r = 4 * k
        taps = [
            moved[2 - t % 3, pl.ds(2 - t // 3 + r, 4)].reshape(4 * width, ch) for t in range(9)
        ]
        dact = lax.dot_general(
            jnp.concatenate(taps, axis=1),
            wide,
            (((1,), (1,)), ((), ())),
            preferred_element_type=F32,
        ).reshape(4, width, ch)
        hidden, sig = gate(fine[pl.ds(r, 4)], strip[k])
        dhidden = dact * sig * (1.0 + hidden * (1.0 - sig))
        fines[g] = dhidden.astype(BF)
        tall = dhidden[0] + dhidden[1] + dhidden[2] + dhidden[3]
        for h in range(ch // 128):
            pooled[...] = tall[:, 128 * h : 128 * h + 128]
            every = [pooled[pl.ds(k, cols, stride=width // cols), :] for k in range(width // cols)]
            gc[g, h] = functools.reduce(jnp.add, every).astype(BF)
        copies.append(pltpu.make_async_copy(fines.at[g], gf.at[pl.ds(r, 4)], sems.at[g]))
        copies[-1].start()
    for c in copies:
        c.wait()


def finish_kernel(norm, zs, spots, n, *refs):
    pieces, parts = refs[: len(spots)], refs[len(spots) : len(spots) + n]
    if n:
        out, coarse_out, scratch, sems, coarse, coarse_sem = refs[-6:]
    else:
        out, scratch, sems = refs[-3:]
    core, plane, me = place()
    planes = lax.axis_size("row") // 2
    ch = out.shape[1]
    half = ch // 2
    tall = ch // planes
    step = tall // zs
    z = lax.rem(me, zs)
    copies = []
    for k, (flip, s, first) in enumerate(spots):
        part = core ^ flip
        lanes = pl.ds(pl.multiple_of(part * half, half), half)
        for c in range(pieces[k].shape[0]):
            x = pieces[k][c].astype(F32) * norm
            for t in range(9):
                scratch[k, c, t] = x[t * step : (t + 1) * step]
            b = pl.multiple_of((plane ^ s) * tall + ((first + c) ^ z) * step, step)
            span = pl.ds(b, step)
            taps = pl.ds(part * 5, 4)
            pairs = (
                (scratch.at[k, c, :4], out.at[taps, span, :half]),
                (scratch.at[k, c, 4:8], out.at[taps, span, half:]),
                (scratch.at[k, c, 8], out.at[4, span, lanes]),
            )
            for i, pair in enumerate(pairs):
                copies.append(pltpu.make_async_copy(*pair, sems.at[k, c, i]))
                copies[-1].start()
    if n:
        cr = coarse.shape[0]
        cols = coarse.shape[1] // n
        for s in range(n):
            start = pl.multiple_of((me ^ s) * cols, cols)
            for j in range(cr):
                for h in range(2):
                    b = (j * 2 + h) * cols
                    coarse[j, pl.ds(start, cols), pl.ds(h * half, half)] = parts[s][b : b + cols]
        copies.append(pltpu.make_async_copy(coarse, coarse_out, coarse_sem.at[0]))
        copies[-1].start()
    for c in copies:
        c.wait()


def xor_pairs(count, bit):
    return [(i, i ^ bit) for i in range(count)]


def per_device(fine_input, coarse_feat, conv_weight, step_scale, timesteps, cotangent):
    _, rows, width, ch = fine_input.shape
    n = lax.axis_size("col")
    nrow = lax.axis_size("row")
    planes = nrow // 2
    cr = coarse_feat.shape[1]
    cols = width // 4
    fine, cot, coarse = fine_input[0], cotangent[0], coarse_feat[0]
    weight = conv_weight.reshape(9, ch, ch)

    def shape(*dims, dtype=BF):
        return jax.ShapeDtypeStruct(dims, dtype)

    def col_swap(x, s):
        return lax.ppermute(x, "col", xor_pairs(n, s))

    blocks = pl.pallas_call(
        functools.partial(start_kernel, n),
        out_shape=[shape(cr * cols + (rows if s and is_edge(s) else 0), ch) for s in range(n)],
        in_specs=[hbm(), hbm()],
        out_specs=[vmem()] * n,
        scratch_shapes=[
            pltpu.VMEM(coarse.shape, BF),
            pltpu.VMEM((rows, 16, ch), BF),
            pltpu.VMEM((rows, 16, ch), BF),
            pltpu.SemaphoreType.DMA((3,)),
        ],
        compiler_params=params(START_MIB),
        cost_estimate=cost(1 << 31, 4 << 20),
        name="start",
    )(cot, coarse)
    blocks = list(blocks)
    moved, scale = pl.pallas_call(
        load_kernel,
        out_shape=[shape(3, rows + 2, width, ch), shape(1, ch, dtype=F32)],
        in_specs=[smem(), vmem(), vmem()],
        out_specs=[vmem()] * 2,
        compiler_params=params(4),
        cost_estimate=cost(1 << 20, 4 << 20),
        name="load",
    )(timesteps, cot, step_scale)

    shifts = [s for s in range(1, n) if is_edge(s)]
    for s in shifts + [s for s in range(1, n) if not is_edge(s)]:
        blocks[s] = col_swap(blocks[s], s)

    halo, side = shape(width + 16, ch), shape(rows, ch, dtype=F32)
    one, two, left, right = pl.pallas_call(
        functools.partial(edge_kernel, cr * cols, shifts),
        out_shape=[halo, halo, side, side],
        in_specs=[vmem()] * (2 + len(shifts)),
        out_specs=[vmem()] * 4,
        compiler_params=params(4),
        cost_estimate=cost(1 << 18, 1 << 19),
        name="edges",
    )(scale, moved, *[blocks[s] for s in shifts])
    odd = range(1, nrow - 1, 2)
    two = lax.ppermute(two, "row", [(i, i + 1) for i in odd] + [(i + 1, i) for i in odd])
    one = lax.ppermute(one, "row", xor_pairs(nrow, 1))

    groups = rows // 4
    moved, act_t, strip, sums, mid = pl.pallas_call(
        functools.partial(prepare_kernel, n, cr),
        out_shape=[
            shape(*moved.shape),
            shape(ch, rows * width),
            shape(groups, cols, ch),
            shape(4, ch, ch, dtype=F32),
            shape(ch, ch // 2, dtype=F32),
        ],
        in_specs=[vmem()] * (4 + n),
        out_specs=[vmem()] * 5,
        input_output_aliases={3: 0},
        scratch_shapes=[pltpu.VMEM((groups, width, ch), F32)],
        compiler_params=params(12),
        cost_estimate=cost(1 << 32, 4 << 20),
        name="prepare",
    )(fine, left, right, moved, *blocks)

    halves = n // 2
    aligned = ch // (planes * halves) % 16 == 0
    zs = halves if aligned else 1
    depth = 9 * ch // (planes * zs)
    half = ch // 2
    part = shape(planes, zs, depth, half)
    send, moved = pl.pallas_call(
        other_kernel,
        out_shape=[part, shape(*moved.shape)],
        in_specs=[vmem()] * 6,
        out_specs=[vmem()] * 2,
        input_output_aliases={5: 1},
        compiler_params=params(8),
        cost_estimate=cost(9 * rows * width * ch * ch // 2, 8 << 20),
        name="weight_other",
    )(act_t, one, two, sums, mid, moved)
    keep = pl.pallas_call(
        mine_kernel,
        out_shape=part,
        in_specs=[vmem()] * 2,
        out_specs=vmem(),
        compiler_params=params(8),
        cost_estimate=cost(9 * rows * width * ch * ch, 8 << 20),
        name="weight_mine",
    )(act_t, moved)

    done, pooled, made = [], [], 0

    def input_piece(size, after):
        nonlocal done, made
        *done, gc = pl.pallas_call(
            functools.partial(input_kernel, made, size, n),
            out_shape=[shape(rows, width, ch), shape(size, 2, cols, ch // 2)],
            in_specs=[pl.BlockSpec(memory_space=pl.ANY)]
            + [vmem()] * 4
            + [pl.BlockSpec(memory_space=pl.ANY) for _ in done],
            out_specs=[pl.BlockSpec(memory_space=pl.ANY), vmem()],
            input_output_aliases={5: 0} if done else {},
            scratch_shapes=[
                pltpu.VMEM((size, 4, width, ch), BF),
                pltpu.VMEM((width, 128), F32),
                pltpu.SemaphoreType.DMA((size,)),
            ],
            compiler_params=params(12),
            cost_estimate=cost(2 * 9 * 4 * size * width * ch * ch, 4 << 20),
            name="input_grad",
        )(after, moved, fine, strip, weight, *done)
        pooled.append(gc)
        made += size

    def beside(got, size, after):
        nonlocal done, pooled
        if size:
            input_piece(size, after)
            got, done, pooled = lax.optimization_barrier((got, done, pooled))
        return got

    def pooled_strip(s):
        at = strip_order(n).index(s) * cr
        groups_done = [x[g] for x in pooled for g in range(x.shape[0])]
        return jnp.concatenate([x.reshape(-1, ch // 2) for x in groups_done[at : at + cr]])

    def add(*terms):
        return functools.reduce(jnp.add, [t.astype(F32) for t in terms]).astype(BF)

    def core_swap(x):
        return lax.ppermute(x, "row", xor_pairs(nrow, 1))

    def plane_swap(x, s):
        return lax.ppermute(x, "row", xor_pairs(nrow, 2 * s))

    sizes = piece_sizes(rows // 4)
    total = add(keep, core_swap(send))
    got = [plane_swap(total[s], s) for s in range(1, planes)]
    total = add(total[0], *beside(got, sizes[0], total))
    if not aligned:
        order = jnp.arange(halves) ^ (lax.axis_index("col") % halves)
        total = total.reshape(halves, depth // halves, half)[order]
    bit = halves // 2
    while bit:
        got = [col_swap(total[bit:], bit)]
        total = add(total[:bit], *beside(got, sizes[1] if bit == 1 else 0, total))
        bit //= 2
    total = add(total, *beside([col_swap(total, halves)], sizes[2], total))

    strips = {s: [(0, pooled_strip(s))] for s in range(n)}

    def hop(bit, extra):
        sent = [(s, src, x) for s in strips if s & bit for src, x in strips[s]]
        return sent, col_swap(jnp.concatenate(extra + [x for _, _, x in sent]), bit)

    def land(bit, sent, got, at):
        for s, src, x in sent:
            strips.pop(s, None)
            strips[s ^ bit].append((src ^ bit, got[at : at + x.shape[0]]))
            at += x.shape[0]

    def ride(bit, total):
        sent, got = hop(bit, [total.reshape(-1, half)])
        at = total.size // half
        land(bit, sent, got, at)
        return got[:at].reshape(total.shape)

    bit = 1
    while bit < halves // 2:
        total = jnp.concatenate([total, ride(bit, total)])
        bit *= 2
    came = ride(bit, total)
    if aligned:
        waves = [total, came]
    else:
        total = jnp.concatenate([total, came])
        waves = [total[order].reshape(1, depth, half)]
    ways = list(range(1, planes))
    waves = [[x] + [plane_swap(x, s) for s in ways] for x in waves]
    if aligned:
        waves[0][1:], waves[1][0] = lax.optimization_barrier((waves[0][1:], waves[1][0]))

    sent, hopped = hop(bit * 2, [])
    pixels = rows * nrow * width * n

    def finish(out, pieces, spots, parts=()):
        coarse = [shape(cr, n * cols, ch)] if parts else []
        count, tall = len(pieces), pieces[0].shape[0]
        return pl.pallas_call(
            functools.partial(finish_kernel, float(pixels) ** -0.5, zs, spots, len(parts)),
            out_shape=[shape(9, ch, ch, dtype=F32)] + coarse,
            in_specs=[vmem()] * (count + len(parts)) + [hbm() for _ in out],
            out_specs=[hbm()] + [hbm() for _ in coarse],
            input_output_aliases={count + len(parts): 0} if out else {},
            scratch_shapes=[
                pltpu.VMEM((count, tall, 9, depth // 9, half), F32),
                pltpu.SemaphoreType.DMA((count, tall, 3)),
            ]
            + [x for c in coarse for x in (pltpu.VMEM(c.shape, BF), pltpu.SemaphoreType.DMA((1,)))],
            compiler_params=params(8),
            cost_estimate=cost(1 << 20, 4 << 20),
            name="finish",
        )(*pieces, *parts, *out)

    spots = [(s, k * wave[0].shape[0]) for k, wave in enumerate(waves) for s in [0] + ways]
    mine = [x for wave in waves for x in wave]
    other = []
    for wave in waves:
        swapped = core_swap(jnp.stack(wave))
        other += [swapped[i] for i in range(len(wave))]
    out = finish([], mine, tuple((0, *spot) for spot in spots))
    last, out = lax.optimization_barrier((hopped, out))
    land(bit * 2, sent, last, 0)
    parts = [x for _, x in sorted(strips[0], key=lambda pair: pair[0])]
    grad_weight, grad_coarse = finish(out, other, tuple((1, *spot) for spot in spots), parts)
    return (done[0][None], grad_coarse[None], grad_weight.reshape(3, 3, ch, ch))


def piece_sizes(groups):
    sizes = [groups * 3 // 4, groups // 8]
    return sizes + [groups - sum(sizes)]


def solution(mesh):
    return jax.shard_map(
        per_device,
        mesh=mesh,
        in_specs=(
            P(None, "row", "col", None),
            P(None, ("row", "col"), None, None),
            P(),
            P(),
            P(),
            P(None, "row", "col", None),
        ),
        out_specs=(P(None, "row", "col", None), P(None, ("row", "col"), None, None), P()),
        check_vma=False,
    )
```

```python
import functools
import jax
import jax.numpy as jnp
from jax import lax
from jax.experimental import pallas as pl
from jax.experimental.pallas import tpu as pltpu
from jax.sharding import PartitionSpec as P

BF = jnp.bfloat16
F32 = jnp.float32
MB = 1024 * 1024
START_MIB = 53.7


def smem():
    return pl.BlockSpec(memory_space=pltpu.SMEM)


def vmem():
    return pl.BlockSpec(memory_space=pltpu.VMEM)


def params(mib):
    return pltpu.CompilerParams(vmem_limit_bytes=int(mib * MB))


def cost(flops, nbytes):
    return pl.CostEstimate(flops=flops, bytes_accessed=nbytes, transcendentals=0)


def hbm():
    return pl.BlockSpec(memory_space=pltpu.HBM)


def place():
    row = lax.axis_index("row")
    return lax.rem(row, 2), row // 2, lax.axis_index("col")


def is_edge(s):
    return s & (s + 1) == 0


def start_kernel(n, cot, coarse, *refs):
    outs, (rough, low, high, sems) = refs[:n], refs[n:]
    _, _, me = place()
    cr, _, ch = rough.shape
    rows, width, _ = cot.shape
    cols = rough.shape[1] // n
    pairs = (coarse, rough), (cot.at[:, :16, :], low), (cot.at[:, width - 16 :, :], high)
    copies = [pltpu.make_async_copy(*pair, sems.at[k]) for k, pair in enumerate(pairs)]
    for c in copies:
        c.start()
    copies[0].wait()
    for s, out in enumerate(outs):
        start = pl.multiple_of((me ^ s) * cols, cols)
        for j in range(cr):
            out[j * cols : (j + 1) * cols, :] = rough[j, pl.ds(start, cols), :]
    r = lax.broadcasted_iota(jnp.int32, (rows, rows * 16), 0)
    p = lax.broadcasted_iota(jnp.int32, (rows, rows * 16), 1)
    sides = []
    for c, edge, pick in ((copies[1], low, 0), (copies[2], high, 15)):
        c.wait()
        sel = jnp.where(p == r * 16 + pick, 1.0, 0.0).astype(BF)
        flat = edge[...].reshape(rows * 16, ch)
        sides.append(jnp.dot(sel, flat, preferred_element_type=F32))
    for s in range(1, n):
        if is_edge(s):
            col = jnp.where((me ^ s) > me, sides[1], sides[0])
            outs[s][cr * cols :, :] = col.astype(BF)


def load_kernel(steps, cot, scales, moved, scale):
    rows, width, ch = cot.shape
    by = scales[pl.ds(steps[0], 1), :]
    scale[...] = by
    zero = jnp.zeros((1, ch), F32)

    def group(g, _):
        for q in range(4):
            r = g * 4 + q
            spread(moved, r + 1, (cot[r].astype(F32) * by).astype(BF), zero, zero)
        return 0

    lax.fori_loop(0, rows // 4, group, 0)


def edge_kernel(offset, shifts, scale, moved, *refs):
    blocks, (one, two, left, right) = refs[: len(shifts)], refs[len(shifts) :]
    core, _, me = place()
    _, rows, width, ch = moved.shape
    rows -= 2
    by = scale[...]
    for side, place_of in ((left, me - 1), (right, me + 1)):
        col = jnp.zeros((rows, ch), F32)
        for s, block in zip(shifts, blocks):
            edge = (block[offset:, :].astype(F32) * by).astype(BF).astype(F32)
            col = jnp.where((me ^ s) == place_of, edge, col)
        side[...] = col
    idx = lax.broadcasted_iota(jnp.int32, (16, ch), 0)
    ends = []
    for k in (0, rows - 1):
        tip = jnp.where(idx == 1, right[k : k + 1, :], 0.0)
        tip = jnp.where(idx == 0, left[k : k + 1, :], tip)
        ends.append((moved[1, k + 1].astype(F32), tip))
    (top, top_tip), (bottom, bottom_tip) = ends
    for out, first in ((one, core == 1), (two, core == 0)):
        out[:width, :] = jnp.where(first, top, bottom).astype(BF)
        out[width:, :] = jnp.where(first, top_tip, bottom_tip).astype(BF)


def spread_up(coarse_row, width):
    cols = coarse_row.shape[0]
    a = lax.broadcasted_iota(jnp.int32, (width, cols), 0)
    b = lax.broadcasted_iota(jnp.int32, (width, cols), 1)
    up = jnp.where(a // (width // cols) == b, 1.0, 0.0).astype(BF)
    return jnp.dot(up, coarse_row, preferred_element_type=F32)


def sigmoid(x):
    return 0.5 * jnp.tanh(0.5 * x) + 0.5


def gate(fine, coarse_row):
    hidden = fine.astype(F32) + spread_up(coarse_row, fine.shape[1])[None]
    return hidden, sigmoid(hidden)


def spread(moved, slot, rounded, left, right):
    width = rounded.shape[0]
    row = rounded.astype(F32)
    idx = lax.broadcasted_iota(jnp.int32, row.shape, 0)
    moved[0, slot] = jnp.where(idx == 0, left, pltpu.roll(row, 1, 0)).astype(BF)
    moved[1, slot] = rounded
    moved[2, slot] = jnp.where(idx == width - 1, right, pltpu.roll(row, width - 1, 0)).astype(BF)


def prepare_kernel(n, cr, fine, left, right, moved_in, *refs):
    blocks, (moved, act_t, strip, sums, up) = refs[:n], refs[n:]
    core, _, me = place()
    rows, width, ch = fine.shape
    cols = strip.shape[1]
    for s in range(n):
        for j in range(cr):
            strip[(me ^ s) * cr + j] = blocks[s][j * cols : (j + 1) * cols, :]
    idx = lax.broadcasted_iota(jnp.int32, (16, ch), 0)

    def patch(r, _):
        for k, low, pick, side in ((0, 0, 0, left), (2, width - 16, 15, right)):
            tile = moved[k, r + 1, low : low + 16, :].astype(F32)
            tile = jnp.where(idx == pick, side[pl.ds(r, 1), :], tile)
            moved[k, r + 1, low : low + 16, :] = tile.astype(BF)
        return 0

    lax.fori_loop(0, rows, patch, 0)
    last = rows // 4 - 1

    def build(g):
        up[g] = spread_up(strip[g], width)
        for r in range(4 * g, 4 * g + 4):
            hidden = fine[r].astype(F32) + up[g]
            act = (hidden * sigmoid(hidden)).astype(BF)
            act_t[:, r * width : (r + 1) * width] = act.T

    def share(g):
        for k in range(5):
            got = partial_tap(1 - core, k, 4 * g, 4, act_t, moved)
            sums[k] = got if g == 1 else sums[k] + got

    build(1)
    for g in range(1, last):
        build(g + 1 if g + 1 < last else 0)
        share(g)
    build(last)


def partial_tap(part, k, row, tall, act_t, moved):
    _, _, width, ch = moved.shape
    lhs = act_t[:, row * width : (row + tall) * width]
    t = 4 if isinstance(k, int) and k == 4 else part * 5 + k
    window = moved[2 - lax.rem(t, 3), pl.ds(2 - t // 3 + row, tall)]
    return jnp.dot(lhs, window.reshape(tall * width, ch), preferred_element_type=F32)


def weight_taps(part, act_t, moved, out, sums):
    _, plane, z = place()
    planes, zs, depth, half = out.shape
    rows = moved.shape[1] - 2
    ch = 2 * half
    step = ch // (planes * zs)
    z = lax.rem(z, zs)

    def put(unit, acc):
        at = pl.multiple_of(unit * step, step)
        for p in range(planes):
            for c in range(zs):
                b = (p * zs + c) * step
                out[p ^ plane, c ^ z, pl.ds(at, step), :] = acc[b : b + step].astype(BF)

    def total(k):
        if sums is None:
            return partial_tap(part, k, 0, rows, act_t, moved)
        first = partial_tap(part, k, 0, 4, act_t, moved)
        return sums[k] + first + partial_tap(part, k, rows - 4, 4, act_t, moved)

    def tap(k, _):
        acc = total(k)
        put(k, acc[:, :half])
        put(k + 4, acc[:, half:])
        return 0

    lax.fori_loop(0, 4, tap, 0)
    return put, total


def other_kernel(act_t, two, one, sums, moved_in, out, rest, moved):
    core, _, _ = place()
    _, rows, width, ch = moved.shape
    for slot, first in ((0, core == 1), (rows - 1, core == 0)):
        halo = jnp.where(first, one[...].astype(F32), two[...].astype(F32))
        left, right = halo[width : width + 1], halo[width + 1 : width + 2]
        spread(moved, slot, halo[:width].astype(BF), left, right)
    put, total = weight_taps(1 - core, act_t, moved, out, sums)
    middle = total(4)
    low, high = middle[:, : ch // 2], middle[:, ch // 2 :]
    put(8, jnp.where(core == 1, low, high))
    rest[...] = jnp.where(core == 1, high, low)


def mine_kernel(act_t, rest, moved, out):
    core, _, _ = place()
    put, _ = weight_taps(core, act_t, moved, out, None)
    put(8, rest[...])


def strip_order(n):
    return list(range(n - 1, 0, -2)) + list(range(n - 2, -1, -2))


def input_kernel(first, size, n, after, moved, fine, strip, weight, *refs):
    gf, gc, fines, pooled, sems = refs[-5:]
    _, _, me = place()
    cr = strip.shape[0] // n
    _, width, ch = fine.shape
    cols = strip.shape[1]
    wide = jnp.concatenate([weight[t] for t in range(9)], axis=1)
    copies = []
    for g in range(size):
        k = (strip_order(n)[(first + g) // cr] ^ me) * cr + (first + g) % cr
        r = 4 * k
        taps = [
            moved[2 - t % 3, pl.ds(2 - t // 3 + r, 4)].reshape(4 * width, ch) for t in range(9)
        ]
        dact = lax.dot_general(
            jnp.concatenate(taps, axis=1),
            wide,
            (((1,), (1,)), ((), ())),
            preferred_element_type=F32,
        ).reshape(4, width, ch)
        hidden, sig = gate(fine[pl.ds(r, 4)], strip[k])
        dhidden = dact * sig * (1.0 + hidden * (1.0 - sig))
        fines[g] = dhidden.astype(BF)
        tall = dhidden[0] + dhidden[1] + dhidden[2] + dhidden[3]
        for h in range(ch // 128):
            pooled[...] = tall[:, 128 * h : 128 * h + 128]
            every = [pooled[pl.ds(k, cols, stride=width // cols), :] for k in range(width // cols)]
            gc[g, h] = functools.reduce(jnp.add, every).astype(BF)
        copies.append(pltpu.make_async_copy(fines.at[g], gf.at[pl.ds(r, 4)], sems.at[g]))
        copies[-1].start()
    for c in copies:
        c.wait()


def finish_kernel(norm, zs, spots, n, *refs):
    pieces, parts = refs[: len(spots)], refs[len(spots) : len(spots) + n]
    if n:
        out, coarse_out, scratch, sems, coarse, coarse_sem = refs[-6:]
    else:
        out, scratch, sems = refs[-3:]
    core, plane, me = place()
    planes = lax.axis_size("row") // 2
    ch = out.shape[1]
    half = ch // 2
    tall = ch // planes
    step = tall // zs
    z = lax.rem(me, zs)
    copies = []
    for k, (flip, s, first) in enumerate(spots):
        part = core ^ flip
        lanes = pl.ds(pl.multiple_of(part * half, half), half)
        for c in range(pieces[k].shape[0]):
            x = pieces[k][c].astype(F32) * norm
            for t in range(9):
                scratch[k, c, t] = x[t * step : (t + 1) * step]
            b = pl.multiple_of((plane ^ s) * tall + ((first + c) ^ z) * step, step)
            span = pl.ds(b, step)
            taps = pl.ds(part * 5, 4)
            pairs = (
                (scratch.at[k, c, :4], out.at[taps, span, :half]),
                (scratch.at[k, c, 4:8], out.at[taps, span, half:]),
                (scratch.at[k, c, 8], out.at[4, span, lanes]),
            )
            for i, pair in enumerate(pairs):
                copies.append(pltpu.make_async_copy(*pair, sems.at[k, c, i]))
                copies[-1].start()
    if n:
        cr = coarse.shape[0]
        cols = coarse.shape[1] // n
        for s in range(n):
            start = pl.multiple_of((me ^ s) * cols, cols)
            for j in range(cr):
                for h in range(2):
                    b = (j * 2 + h) * cols
                    coarse[j, pl.ds(start, cols), pl.ds(h * half, half)] = parts[s][b : b + cols]
        copies.append(pltpu.make_async_copy(coarse, coarse_out, coarse_sem.at[0]))
        copies[-1].start()
    for c in copies:
        c.wait()


def xor_pairs(count, bit):
    return [(i, i ^ bit) for i in range(count)]


def per_device(fine_input, coarse_feat, conv_weight, step_scale, timesteps, cotangent):
    _, rows, width, ch = fine_input.shape
    n = lax.axis_size("col")
    nrow = lax.axis_size("row")
    planes = nrow // 2
    cr = coarse_feat.shape[1]
    cols = width // 4
    fine, cot, coarse = fine_input[0], cotangent[0], coarse_feat[0]
    weight = conv_weight.reshape(9, ch, ch)

    def shape(*dims, dtype=BF):
        return jax.ShapeDtypeStruct(dims, dtype)

    def col_swap(x, s):
        return lax.ppermute(x, "col", xor_pairs(n, s))

    blocks = pl.pallas_call(
        functools.partial(start_kernel, n),
        out_shape=[shape(cr * cols + (rows if s and is_edge(s) else 0), ch) for s in range(n)],
        in_specs=[hbm(), hbm()],
        out_specs=[vmem()] * n,
        scratch_shapes=[
            pltpu.VMEM(coarse.shape, BF),
            pltpu.VMEM((rows, 16, ch), BF),
            pltpu.VMEM((rows, 16, ch), BF),
            pltpu.SemaphoreType.DMA((3,)),
        ],
        compiler_params=params(START_MIB),
        cost_estimate=cost(1 << 31, 4 << 20),
        name="start",
    )(cot, coarse)
    blocks = list(blocks)
    moved, scale = pl.pallas_call(
        load_kernel,
        out_shape=[shape(3, rows + 2, width, ch), shape(1, ch, dtype=F32)],
        in_specs=[smem(), vmem(), vmem()],
        out_specs=[vmem()] * 2,
        compiler_params=params(4),
        cost_estimate=cost(1 << 20, 4 << 20),
        name="load",
    )(timesteps, cot, step_scale)

    shifts = [s for s in range(n - 1, 0, -1) if is_edge(s)]
    for s in shifts + [s for s in range(1, n) if not is_edge(s)]:
        blocks[s] = col_swap(blocks[s], s)

    halo, side = shape(width + 16, ch), shape(rows, ch, dtype=F32)
    one, two, left, right = pl.pallas_call(
        functools.partial(edge_kernel, cr * cols, shifts),
        out_shape=[halo, halo, side, side],
        in_specs=[vmem()] * (2 + len(shifts)),
        out_specs=[vmem()] * 4,
        compiler_params=params(4),
        cost_estimate=cost(1 << 18, 1 << 19),
        name="edges",
    )(scale, moved, *[blocks[s] for s in shifts])
    odd = range(1, nrow - 1, 2)
    two = lax.ppermute(two, "row", [(i, i + 1) for i in odd] + [(i + 1, i) for i in odd])
    one = lax.ppermute(one, "row", xor_pairs(nrow, 1))

    groups = rows // 4
    moved, act_t, strip, sums = pl.pallas_call(
        functools.partial(prepare_kernel, n, cr),
        out_shape=[
            shape(*moved.shape),
            shape(ch, rows * width),
            shape(groups, cols, ch),
            shape(5, ch, ch, dtype=F32),
        ],
        in_specs=[vmem()] * (4 + n),
        out_specs=[vmem()] * 4,
        input_output_aliases={3: 0},
        scratch_shapes=[pltpu.VMEM((groups, width, ch), F32)],
        compiler_params=params(12),
        cost_estimate=cost(1 << 32, 4 << 20),
        name="prepare",
    )(fine, left, right, moved, *blocks)

    halves = n // 2
    aligned = ch // (planes * halves) % 16 == 0
    zs = halves if aligned else 1
    depth = 9 * ch // (planes * zs)
    half = ch // 2
    part = shape(planes, zs, depth, half)
    send, rest, moved = pl.pallas_call(
        other_kernel,
        out_shape=[part, shape(ch, half, dtype=F32), shape(*moved.shape)],
        in_specs=[vmem()] * 5,
        out_specs=[vmem()] * 3,
        input_output_aliases={4: 2},
        compiler_params=params(8),
        cost_estimate=cost(9 * rows * width * ch * ch // 4, 8 << 20),
        name="weight_other",
    )(act_t, two, one, sums, moved)
    keep = pl.pallas_call(
        mine_kernel,
        out_shape=part,
        in_specs=[vmem()] * 3,
        out_specs=vmem(),
        compiler_params=params(8),
        cost_estimate=cost(8 * rows * width * ch * ch, 8 << 20),
        name="weight_mine",
    )(act_t, rest, moved)

    done, pooled, made = [], [], 0

    def input_piece(size, after):
        nonlocal done, made
        *done, gc = pl.pallas_call(
            functools.partial(input_kernel, made, size, n),
            out_shape=[shape(rows, width, ch), shape(size, 2, cols, ch // 2)],
            in_specs=[pl.BlockSpec(memory_space=pl.ANY)]
            + [vmem()] * 4
            + [pl.BlockSpec(memory_space=pl.ANY) for _ in done],
            out_specs=[pl.BlockSpec(memory_space=pl.ANY), vmem()],
            input_output_aliases={5: 0} if done else {},
            scratch_shapes=[
                pltpu.VMEM((size, 4, width, ch), BF),
                pltpu.VMEM((width, 128), F32),
                pltpu.SemaphoreType.DMA((size,)),
            ],
            compiler_params=params(12),
            cost_estimate=cost(2 * 9 * 4 * size * width * ch * ch, 4 << 20),
            name="input_grad",
        )(after, moved, fine, strip, weight, *done)
        pooled.append(gc)
        made += size

    def beside(got, size, after):
        nonlocal done, pooled
        if size:
            input_piece(size, after)
            got, done, pooled = lax.optimization_barrier((got, done, pooled))
        return got

    def pooled_strip(s):
        at = strip_order(n).index(s) * cr
        groups_done = [x[g] for x in pooled for g in range(x.shape[0])]
        return jnp.concatenate([x.reshape(-1, ch // 2) for x in groups_done[at : at + cr]])

    def add(*terms):
        return functools.reduce(jnp.add, [t.astype(F32) for t in terms]).astype(BF)

    def core_swap(x):
        return lax.ppermute(x, "row", xor_pairs(nrow, 1))

    def plane_swap(x, s):
        return lax.ppermute(x, "row", xor_pairs(nrow, 2 * s))

    sizes = piece_sizes(rows // 4)
    total = add(keep, core_swap(send))
    got = [plane_swap(total[s], s) for s in range(1, planes)]
    total = add(total[0], *beside(got, sizes[0], total))
    if not aligned:
        order = jnp.arange(halves) ^ (lax.axis_index("col") % halves)
        total = total.reshape(halves, depth // halves, half)[order]
    bit = halves // 2
    while bit:
        got = [col_swap(total[bit:], bit)]
        total = add(total[:bit], *beside(got, sizes[1] if bit == 1 else 0, total))
        bit //= 2
    total = add(total, *beside([col_swap(total, halves)], sizes[2], total))

    strips = {s: [(0, pooled_strip(s))] for s in range(n)}

    def hop(bit, extra):
        sent = [(s, src, x) for s in strips if s & bit for src, x in strips[s]]
        return sent, col_swap(jnp.concatenate(extra + [x for _, _, x in sent]), bit)

    def land(bit, sent, got, at):
        for s, src, x in sent:
            strips.pop(s, None)
            strips[s ^ bit].append((src ^ bit, got[at : at + x.shape[0]]))
            at += x.shape[0]

    def ride(bit, total):
        sent, got = hop(bit, [total.reshape(-1, half)])
        at = total.size // half
        land(bit, sent, got, at)
        return got[:at].reshape(total.shape)

    bit = 1
    while bit < halves // 2:
        total = jnp.concatenate([total, ride(bit, total)])
        bit *= 2
    came = ride(bit, total)
    if aligned:
        waves = [total, came]
    else:
        total = jnp.concatenate([total, came])
        waves = [total[order].reshape(1, depth, half)]
    ways = list(range(1, planes))
    waves = [[x] + [plane_swap(x, s) for s in ways] for x in waves]
    if aligned:
        waves[0][1:], waves[1][0] = lax.optimization_barrier((waves[0][1:], waves[1][0]))

    sent, hopped = hop(bit * 2, [])
    pixels = rows * nrow * width * n

    def finish(out, pieces, spots, parts=()):
        coarse = [shape(cr, n * cols, ch)] if parts else []
        count, tall = len(pieces), pieces[0].shape[0]
        return pl.pallas_call(
            functools.partial(finish_kernel, float(pixels) ** -0.5, zs, spots, len(parts)),
            out_shape=[shape(9, ch, ch, dtype=F32)] + coarse,
            in_specs=[vmem()] * (count + len(parts)) + [hbm() for _ in out],
            out_specs=[hbm()] + [hbm() for _ in coarse],
            input_output_aliases={count + len(parts): 0} if out else {},
            scratch_shapes=[
                pltpu.VMEM((count, tall, 9, depth // 9, half), F32),
                pltpu.SemaphoreType.DMA((count, tall, 3)),
            ]
            + [x for c in coarse for x in (pltpu.VMEM(c.shape, BF), pltpu.SemaphoreType.DMA((1,)))],
            compiler_params=params(8),
            cost_estimate=cost(1 << 20, 4 << 20),
            name="finish",
        )(*pieces, *parts, *out)

    spots = [(s, k * wave[0].shape[0]) for k, wave in enumerate(waves) for s in [0] + ways]
    mine = [x for wave in waves for x in wave]
    other = []
    for wave in waves:
        swapped = core_swap(jnp.stack(wave))
        other += [swapped[i] for i in range(len(wave))]
    out = finish([], mine, tuple((0, *spot) for spot in spots))
    last, out = lax.optimization_barrier((hopped, out))
    land(bit * 2, sent, last, 0)
    parts = [x for _, x in sorted(strips[0], key=lambda pair: pair[0])]
    grad_weight, grad_coarse = finish(out, other, tuple((1, *spot) for spot in spots), parts)
    return (done[0][None], grad_coarse[None], grad_weight.reshape(3, 3, ch, ch))


def piece_sizes(groups):
    sizes = [groups * 3 // 4, groups // 8]
    return sizes + [groups - sum(sizes)]


def solution(mesh):
    return jax.shard_map(
        per_device,
        mesh=mesh,
        in_specs=(
            P(None, "row", "col", None),
            P(None, ("row", "col"), None, None),
            P(),
            P(),
            P(),
            P(None, "row", "col", None),
        ),
        out_specs=(P(None, "row", "col", None), P(None, ("row", "col"), None, None), P()),
        check_vma=False,
    )
```

```python
import functools
import jax
import jax.numpy as jnp
from jax import lax
from jax.experimental import pallas as pl
from jax.experimental.pallas import tpu as pltpu
from jax.sharding import PartitionSpec as P

BF = jnp.bfloat16
F32 = jnp.float32
MB = 1024 * 1024
START_MIB = 53.7


def smem():
    return pl.BlockSpec(memory_space=pltpu.SMEM)


def vmem():
    return pl.BlockSpec(memory_space=pltpu.VMEM)


def params(mib):
    return pltpu.CompilerParams(vmem_limit_bytes=int(mib * MB))


def cost(flops, nbytes):
    return pl.CostEstimate(flops=flops, bytes_accessed=nbytes, transcendentals=0)


def hbm():
    return pl.BlockSpec(memory_space=pltpu.HBM)


def place():
    row = lax.axis_index("row")
    return lax.rem(row, 2), row // 2, lax.axis_index("col")


def is_edge(s):
    return s & (s + 1) == 0


def start_kernel(n, cot, coarse, *refs):
    outs, (rough, low, high, sems) = refs[:n], refs[n:]
    _, _, me = place()
    cr, _, ch = rough.shape
    rows, width, _ = cot.shape
    cols = rough.shape[1] // n
    pairs = (coarse, rough), (cot.at[:, :16, :], low), (cot.at[:, width - 16 :, :], high)
    copies = [pltpu.make_async_copy(*pair, sems.at[k]) for k, pair in enumerate(pairs)]
    for c in copies:
        c.start()
    copies[0].wait()
    for s, out in enumerate(outs):
        start = pl.multiple_of((me ^ s) * cols, cols)
        for j in range(cr):
            out[j * cols : (j + 1) * cols, :] = rough[j, pl.ds(start, cols), :]
    r = lax.broadcasted_iota(jnp.int32, (rows, rows * 16), 0)
    p = lax.broadcasted_iota(jnp.int32, (rows, rows * 16), 1)
    sides = []
    for c, edge, pick in ((copies[1], low, 0), (copies[2], high, 15)):
        c.wait()
        sel = jnp.where(p == r * 16 + pick, 1.0, 0.0).astype(BF)
        flat = edge[...].reshape(rows * 16, ch)
        sides.append(jnp.dot(sel, flat, preferred_element_type=F32))
    for s in range(1, n):
        if is_edge(s):
            col = jnp.where((me ^ s) > me, sides[1], sides[0])
            outs[s][cr * cols :, :] = col.astype(BF)


def load_kernel(steps, cot, scales, moved, scale):
    rows, width, ch = cot.shape
    by = scales[pl.ds(steps[0], 1), :]
    scale[...] = by
    zero = jnp.zeros((1, ch), F32)

    def group(g, _):
        for q in range(4):
            r = g * 4 + q
            spread(moved, r + 1, (cot[r].astype(F32) * by).astype(BF), zero, zero)
        return 0

    lax.fori_loop(0, rows // 4, group, 0)


def edge_kernel(offset, shifts, scale, moved, *refs):
    blocks, (one, two, left, right) = refs[: len(shifts)], refs[len(shifts) :]
    core, _, me = place()
    _, rows, width, ch = moved.shape
    rows -= 2
    by = scale[...]
    for side, place_of in ((left, me - 1), (right, me + 1)):
        col = jnp.zeros((rows, ch), F32)
        for s, block in zip(shifts, blocks):
            edge = (block[offset:, :].astype(F32) * by).astype(BF).astype(F32)
            col = jnp.where((me ^ s) == place_of, edge, col)
        side[...] = col
    idx = lax.broadcasted_iota(jnp.int32, (16, ch), 0)
    ends = []
    for k in (0, rows - 1):
        tip = jnp.where(idx == 1, right[k : k + 1, :], 0.0)
        tip = jnp.where(idx == 0, left[k : k + 1, :], tip)
        ends.append((moved[1, k + 1].astype(F32), tip))
    (top, top_tip), (bottom, bottom_tip) = ends
    for out, first in ((one, core == 1), (two, core == 0)):
        out[:width, :] = jnp.where(first, top, bottom).astype(BF)
        out[width:, :] = jnp.where(first, top_tip, bottom_tip).astype(BF)


def spread_up(coarse_row, width):
    cols = coarse_row.shape[0]
    a = lax.broadcasted_iota(jnp.int32, (width, cols), 0)
    b = lax.broadcasted_iota(jnp.int32, (width, cols), 1)
    up = jnp.where(a // (width // cols) == b, 1.0, 0.0).astype(BF)
    return jnp.dot(up, coarse_row, preferred_element_type=F32)


def sigmoid(x):
    return 0.5 * jnp.tanh(0.5 * x) + 0.5


def gate(fine, coarse_row):
    hidden = fine.astype(F32) + spread_up(coarse_row, fine.shape[1])[None]
    return hidden, sigmoid(hidden)


def spread(moved, slot, rounded, left, right):
    width = rounded.shape[0]
    row = rounded.astype(F32)
    idx = lax.broadcasted_iota(jnp.int32, row.shape, 0)
    moved[0, slot] = jnp.where(idx == 0, left, pltpu.roll(row, 1, 0)).astype(BF)
    moved[1, slot] = rounded
    moved[2, slot] = jnp.where(idx == width - 1, right, pltpu.roll(row, width - 1, 0)).astype(BF)


def prepare_kernel(n, cr, fine, left, right, moved_in, *refs):
    blocks, (moved, act_t, strip, sums, up) = refs[:n], refs[n:]
    core, _, me = place()
    rows, width, ch = fine.shape
    cols = strip.shape[1]
    for s in range(n):
        for j in range(cr):
            strip[(me ^ s) * cr + j] = blocks[s][j * cols : (j + 1) * cols, :]
    idx = lax.broadcasted_iota(jnp.int32, (16, ch), 0)

    def patch(r, _):
        for k, low, pick, side in ((0, 0, 0, left), (2, width - 16, 15, right)):
            tile = moved[k, r + 1, low : low + 16, :].astype(F32)
            tile = jnp.where(idx == pick, side[pl.ds(r, 1), :], tile)
            moved[k, r + 1, low : low + 16, :] = tile.astype(BF)
        return 0

    lax.fori_loop(0, rows, patch, 0)
    last = rows // 4 - 1

    def build(g):
        up[g] = spread_up(strip[g], width)
        for r in range(4 * g, 4 * g + 4):
            hidden = fine[r].astype(F32) + up[g]
            act = (hidden * sigmoid(hidden)).astype(BF)
            act_t[:, r * width : (r + 1) * width] = act.T

    def share(g):
        for k in range(5):
            got = partial_tap(1 - core, k, 4 * g, 4, act_t, moved)
            sums[k] = got if g == 1 else sums[k] + got

    build(1)
    for g in range(1, last):
        build(g + 1 if g + 1 < last else 0)
        share(g)
    build(last)


def partial_tap(part, k, row, tall, act_t, moved):
    _, _, width, ch = moved.shape
    lhs = act_t[:, row * width : (row + tall) * width]
    t = 4 if isinstance(k, int) and k == 4 else part * 5 + k
    window = moved[2 - lax.rem(t, 3), pl.ds(2 - t // 3 + row, tall)]
    return jnp.dot(lhs, window.reshape(tall * width, ch), preferred_element_type=F32)


def weight_taps(part, act_t, moved, out, sums):
    _, plane, z = place()
    planes, zs, depth, half = out.shape
    rows = moved.shape[1] - 2
    ch = 2 * half
    step = ch // (planes * zs)
    z = lax.rem(z, zs)

    def put(unit, acc):
        at = pl.multiple_of(unit * step, step)
        for p in range(planes):
            for c in range(zs):
                b = (p * zs + c) * step
                out[p ^ plane, c ^ z, pl.ds(at, step), :] = acc[b : b + step].astype(BF)

    def total(k):
        if sums is None:
            return partial_tap(part, k, 0, rows, act_t, moved)
        first = partial_tap(part, k, 0, 4, act_t, moved)
        return sums[k] + first + partial_tap(part, k, rows - 4, 4, act_t, moved)

    def tap(k, _):
        acc = total(k)
        put(k, acc[:, :half])
        put(k + 4, acc[:, half:])
        return 0

    lax.fori_loop(0, 4, tap, 0)
    return put, total


def other_kernel(act_t, two, one, sums, moved_in, out, rest, moved):
    core, _, _ = place()
    _, rows, width, ch = moved.shape
    row = lax.axis_index("row")
    outer = (row == 0) | (row == lax.axis_size("row") - 1)
    next_chip = jnp.where(outer, 0.0, two[...].astype(F32))
    for slot, first in ((0, core == 1), (rows - 1, core == 0)):
        halo = jnp.where(first, one[...].astype(F32), next_chip)
        left, right = halo[width : width + 1], halo[width + 1 : width + 2]
        spread(moved, slot, halo[:width].astype(BF), left, right)
    put, total = weight_taps(1 - core, act_t, moved, out, sums)
    middle = total(4)
    low, high = middle[:, : ch // 2], middle[:, ch // 2 :]
    put(8, jnp.where(core == 1, low, high))
    rest[...] = jnp.where(core == 1, high, low)


def mine_kernel(act_t, rest, moved, out):
    core, _, _ = place()
    put, _ = weight_taps(core, act_t, moved, out, None)
    put(8, rest[...])


def strip_order(n):
    return list(range(n - 1, 0, -2)) + list(range(n - 2, -1, -2))


def input_kernel(first, size, n, after, moved, fine, strip, weight, *refs):
    gf, gc, fines, pooled, sems = refs[-5:]
    _, _, me = place()
    cr = strip.shape[0] // n
    _, width, ch = fine.shape
    cols = strip.shape[1]
    wide = jnp.concatenate([weight[t] for t in range(9)], axis=1)
    copies = []
    for g in range(size):
        k = (strip_order(n)[(first + g) // cr] ^ me) * cr + (first + g) % cr
        r = 4 * k
        taps = [
            moved[2 - t % 3, pl.ds(2 - t // 3 + r, 4)].reshape(4 * width, ch) for t in range(9)
        ]
        dact = lax.dot_general(
            jnp.concatenate(taps, axis=1),
            wide,
            (((1,), (1,)), ((), ())),
            preferred_element_type=F32,
        ).reshape(4, width, ch)
        hidden, sig = gate(fine[pl.ds(r, 4)], strip[k])
        dhidden = dact * sig * (1.0 + hidden * (1.0 - sig))
        fines[g] = dhidden.astype(BF)
        tall = dhidden[0] + dhidden[1] + dhidden[2] + dhidden[3]
        for h in range(ch // 128):
            pooled[...] = tall[:, 128 * h : 128 * h + 128]
            every = [pooled[pl.ds(k, cols, stride=width // cols), :] for k in range(width // cols)]
            gc[g, h] = functools.reduce(jnp.add, every).astype(BF)
        copies.append(pltpu.make_async_copy(fines.at[g], gf.at[pl.ds(r, 4)], sems.at[g]))
        copies[-1].start()
    for c in copies:
        c.wait()


def finish_kernel(norm, zs, spots, n, *refs):
    pieces, parts = refs[: len(spots)], refs[len(spots) : len(spots) + n]
    if n:
        out, coarse_out, scratch, sems, coarse, coarse_sem = refs[-6:]
    else:
        out, scratch, sems = refs[-3:]
    core, plane, me = place()
    planes = lax.axis_size("row") // 2
    ch = out.shape[1]
    half = ch // 2
    tall = ch // planes
    step = tall // zs
    z = lax.rem(me, zs)
    copies = []
    for k, (flip, s, first) in enumerate(spots):
        part = core ^ flip
        lanes = pl.ds(pl.multiple_of(part * half, half), half)
        for c in range(pieces[k].shape[0]):
            x = pieces[k][c].astype(F32) * norm
            for t in range(9):
                scratch[k, c, t] = x[t * step : (t + 1) * step]
            b = pl.multiple_of((plane ^ s) * tall + ((first + c) ^ z) * step, step)
            span = pl.ds(b, step)
            taps = pl.ds(part * 5, 4)
            pairs = (
                (scratch.at[k, c, :4], out.at[taps, span, :half]),
                (scratch.at[k, c, 4:8], out.at[taps, span, half:]),
                (scratch.at[k, c, 8], out.at[4, span, lanes]),
            )
            for i, pair in enumerate(pairs):
                copies.append(pltpu.make_async_copy(*pair, sems.at[k, c, i]))
                copies[-1].start()
    if n:
        cr = coarse.shape[0]
        cols = coarse.shape[1] // n
        for s in range(n):
            start = pl.multiple_of((me ^ s) * cols, cols)
            for j in range(cr):
                for h in range(2):
                    b = (j * 2 + h) * cols
                    coarse[j, pl.ds(start, cols), pl.ds(h * half, half)] = parts[s][b : b + cols]
        copies.append(pltpu.make_async_copy(coarse, coarse_out, coarse_sem.at[0]))
        copies[-1].start()
    for c in copies:
        c.wait()


def xor_pairs(count, bit):
    return [(i, i ^ bit) for i in range(count)]


def per_device(fine_input, coarse_feat, conv_weight, step_scale, timesteps, cotangent):
    _, rows, width, ch = fine_input.shape
    n = lax.axis_size("col")
    nrow = lax.axis_size("row")
    planes = nrow // 2
    cr = coarse_feat.shape[1]
    cols = width // 4
    fine, cot, coarse = fine_input[0], cotangent[0], coarse_feat[0]
    weight = conv_weight.reshape(9, ch, ch)

    def shape(*dims, dtype=BF):
        return jax.ShapeDtypeStruct(dims, dtype)

    def col_swap(x, s):
        return lax.ppermute(x, "col", xor_pairs(n, s))

    blocks = pl.pallas_call(
        functools.partial(start_kernel, n),
        out_shape=[shape(cr * cols + (rows if s and is_edge(s) else 0), ch) for s in range(n)],
        in_specs=[hbm(), hbm()],
        out_specs=[vmem()] * n,
        scratch_shapes=[
            pltpu.VMEM(coarse.shape, BF),
            pltpu.VMEM((rows, 16, ch), BF),
            pltpu.VMEM((rows, 16, ch), BF),
            pltpu.SemaphoreType.DMA((3,)),
        ],
        compiler_params=params(START_MIB),
        cost_estimate=cost(1 << 31, 4 << 20),
        name="start",
    )(cot, coarse)
    blocks = list(blocks)
    moved, scale = pl.pallas_call(
        load_kernel,
        out_shape=[shape(3, rows + 2, width, ch), shape(1, ch, dtype=F32)],
        in_specs=[smem(), vmem(), vmem()],
        out_specs=[vmem()] * 2,
        compiler_params=params(4),
        cost_estimate=cost(1 << 20, 4 << 20),
        name="load",
    )(timesteps, cot, step_scale)

    shifts = [s for s in range(n - 1, 0, -1) if is_edge(s)]
    for s in shifts + [s for s in range(1, n) if not is_edge(s)]:
        blocks[s] = col_swap(blocks[s], s)

    halo, side = shape(width + 16, ch), shape(rows, ch, dtype=F32)
    one, two, left, right = pl.pallas_call(
        functools.partial(edge_kernel, cr * cols, shifts),
        out_shape=[halo, halo, side, side],
        in_specs=[vmem()] * (2 + len(shifts)),
        out_specs=[vmem()] * 4,
        compiler_params=params(4),
        cost_estimate=cost(1 << 18, 1 << 19),
        name="edges",
    )(scale, moved, *[blocks[s] for s in shifts])
    odd = range(1, nrow, 2)
    two = lax.ppermute(
        two, "row", [(i, (i + 1) % nrow) for i in odd] + [((i + 1) % nrow, i) for i in odd]
    )
    one = lax.ppermute(one, "row", xor_pairs(nrow, 1))

    groups = rows // 4
    moved, act_t, strip, sums = pl.pallas_call(
        functools.partial(prepare_kernel, n, cr),
        out_shape=[
            shape(*moved.shape),
            shape(ch, rows * width),
            shape(groups, cols, ch),
            shape(5, ch, ch, dtype=F32),
        ],
        in_specs=[vmem()] * (4 + n),
        out_specs=[vmem()] * 4,
        input_output_aliases={3: 0},
        scratch_shapes=[pltpu.VMEM((groups, width, ch), F32)],
        compiler_params=params(12),
        cost_estimate=cost(1 << 32, 4 << 20),
        name="prepare",
    )(fine, left, right, moved, *blocks)

    halves = n // 2
    aligned = ch // (planes * halves) % 16 == 0
    zs = halves if aligned else 1
    depth = 9 * ch // (planes * zs)
    half = ch // 2
    part = shape(planes, zs, depth, half)
    send, rest, moved = pl.pallas_call(
        other_kernel,
        out_shape=[part, shape(ch, half, dtype=F32), shape(*moved.shape)],
        in_specs=[vmem()] * 5,
        out_specs=[vmem()] * 3,
        input_output_aliases={4: 2},
        compiler_params=params(8),
        cost_estimate=cost(9 * rows * width * ch * ch // 4, 8 << 20),
        name="weight_other",
    )(act_t, two, one, sums, moved)
    keep = pl.pallas_call(
        mine_kernel,
        out_shape=part,
        in_specs=[vmem()] * 3,
        out_specs=vmem(),
        compiler_params=params(8),
        cost_estimate=cost(8 * rows * width * ch * ch, 8 << 20),
        name="weight_mine",
    )(act_t, rest, moved)

    done, pooled, made = [], [], 0

    def input_piece(size, after):
        nonlocal done, made
        *done, gc = pl.pallas_call(
            functools.partial(input_kernel, made, size, n),
            out_shape=[shape(rows, width, ch), shape(size, 2, cols, ch // 2)],
            in_specs=[pl.BlockSpec(memory_space=pl.ANY)]
            + [vmem()] * 4
            + [pl.BlockSpec(memory_space=pl.ANY) for _ in done],
            out_specs=[pl.BlockSpec(memory_space=pl.ANY), vmem()],
            input_output_aliases={5: 0} if done else {},
            scratch_shapes=[
                pltpu.VMEM((size, 4, width, ch), BF),
                pltpu.VMEM((width, 128), F32),
                pltpu.SemaphoreType.DMA((size,)),
            ],
            compiler_params=params(12),
            cost_estimate=cost(2 * 9 * 4 * size * width * ch * ch, 4 << 20),
            name="input_grad",
        )(after, moved, fine, strip, weight, *done)
        pooled.append(gc)
        made += size

    def beside(got, size, after):
        nonlocal done, pooled
        if size:
            input_piece(size, after)
            got, done, pooled = lax.optimization_barrier((got, done, pooled))
        return got

    def pooled_strip(s):
        at = strip_order(n).index(s) * cr
        groups_done = [x[g] for x in pooled for g in range(x.shape[0])]
        return jnp.concatenate([x.reshape(-1, ch // 2) for x in groups_done[at : at + cr]])

    def add(*terms):
        return functools.reduce(jnp.add, [t.astype(F32) for t in terms]).astype(BF)

    def core_swap(x):
        return lax.ppermute(x, "row", xor_pairs(nrow, 1))

    def plane_swap(x, s):
        return lax.ppermute(x, "row", xor_pairs(nrow, 2 * s))

    sizes = piece_sizes(rows // 4)
    total = add(keep, core_swap(send))
    got = [plane_swap(total[s], s) for s in range(1, planes)]
    total = add(total[0], *beside(got, sizes[0], total))
    if not aligned:
        order = jnp.arange(halves) ^ (lax.axis_index("col") % halves)
        total = total.reshape(halves, depth // halves, half)[order]
    bit = halves // 2
    while bit:
        got = [col_swap(total[bit:], bit)]
        total = add(total[:bit], *beside(got, sizes[1] if bit == 1 else 0, total))
        bit //= 2
    total = add(total, *beside([col_swap(total, halves)], sizes[2], total))

    strips = {s: [(0, pooled_strip(s))] for s in range(n)}

    def hop(bit, extra):
        sent = [(s, src, x) for s in strips if s & bit for src, x in strips[s]]
        return sent, col_swap(jnp.concatenate(extra + [x for _, _, x in sent]), bit)

    def land(bit, sent, got, at):
        for s, src, x in sent:
            strips.pop(s, None)
            strips[s ^ bit].append((src ^ bit, got[at : at + x.shape[0]]))
            at += x.shape[0]

    def ride(bit, total):
        sent, got = hop(bit, [total.reshape(-1, half)])
        at = total.size // half
        land(bit, sent, got, at)
        return got[:at].reshape(total.shape)

    bit = 1
    while bit < halves // 2:
        total = jnp.concatenate([total, ride(bit, total)])
        bit *= 2
    came = ride(bit, total)
    if aligned:
        waves = [total, came]
    else:
        total = jnp.concatenate([total, came])
        waves = [total[order].reshape(1, depth, half)]
    ways = list(range(1, planes))
    waves = [[x] + [plane_swap(x, s) for s in ways] for x in waves]
    if aligned:
        waves[0][1:], waves[1][0] = lax.optimization_barrier((waves[0][1:], waves[1][0]))

    sent, hopped = hop(bit * 2, [])
    pixels = rows * nrow * width * n

    def finish(out, pieces, spots, parts=()):
        coarse = [shape(cr, n * cols, ch)] if parts else []
        count, tall = len(pieces), pieces[0].shape[0]
        return pl.pallas_call(
            functools.partial(finish_kernel, float(pixels) ** -0.5, zs, spots, len(parts)),
            out_shape=[shape(9, ch, ch, dtype=F32)] + coarse,
            in_specs=[vmem()] * (count + len(parts)) + [hbm() for _ in out],
            out_specs=[hbm()] + [hbm() for _ in coarse],
            input_output_aliases={count + len(parts): 0} if out else {},
            scratch_shapes=[
                pltpu.VMEM((count, tall, 9, depth // 9, half), F32),
                pltpu.SemaphoreType.DMA((count, tall, 3)),
            ]
            + [x for c in coarse for x in (pltpu.VMEM(c.shape, BF), pltpu.SemaphoreType.DMA((1,)))],
            compiler_params=params(8),
            cost_estimate=cost(1 << 20, 4 << 20),
            name="finish",
        )(*pieces, *parts, *out)

    out, others, spots = [], [], ()
    for k, wave in enumerate(waves):
        if k:
            wave[1:], out = lax.optimization_barrier((wave[1:], out))
        swapped = core_swap(jnp.stack(wave))
        here = [(s, k * wave[0].shape[0]) for s in [0] + ways]
        places = [(0, *spot) for spot in here] + [(1, *spot) for spot in spots]
        out = finish(out, wave + others, tuple(places))
        others, spots = [swapped[i] for i in range(len(wave))], here
    last, out = lax.optimization_barrier((hopped, out))
    land(bit * 2, sent, last, 0)
    parts = [x for _, x in sorted(strips[0], key=lambda pair: pair[0])]
    grad_weight, grad_coarse = finish(out, others, tuple((1, *spot) for spot in spots), parts)
    return (done[0][None], grad_coarse[None], grad_weight.reshape(3, 3, ch, ch))


def piece_sizes(groups):
    sizes = [groups * 3 // 4, groups // 8]
    return sizes + [groups - sum(sizes)]


def solution(mesh):
    return jax.shard_map(
        per_device,
        mesh=mesh,
        in_specs=(
            P(None, "row", "col", None),
            P(None, ("row", "col"), None, None),
            P(),
            P(),
            P(),
            P(None, "row", "col", None),
        ),
        out_specs=(P(None, "row", "col", None), P(None, ("row", "col"), None, None), P()),
        check_vma=False,
    )
```

```python
import functools
import jax
import jax.numpy as jnp
from jax import lax
from jax.experimental import pallas as pl
from jax.experimental.pallas import tpu as pltpu
from jax.sharding import PartitionSpec as P

BF = jnp.bfloat16
F32 = jnp.float32
MB = 1024 * 1024
START_MIB = 53.7


def smem():
    return pl.BlockSpec(memory_space=pltpu.SMEM)


def vmem():
    return pl.BlockSpec(memory_space=pltpu.VMEM)


def params(mib):
    return pltpu.CompilerParams(vmem_limit_bytes=int(mib * MB))


def cost(flops, nbytes):
    return pl.CostEstimate(flops=flops, bytes_accessed=nbytes, transcendentals=0)


def hbm():
    return pl.BlockSpec(memory_space=pltpu.HBM)


def place():
    row = lax.axis_index("row")
    return lax.rem(row, 2), row // 2, lax.axis_index("col")


def is_edge(s):
    return s & (s + 1) == 0


def start_kernel(n, cot, coarse, *refs):
    outs, (rough, low, high, sems) = refs[:n], refs[n:]
    _, _, me = place()
    cr, _, ch = rough.shape
    rows, width, _ = cot.shape
    cols = rough.shape[1] // n
    pairs = (coarse, rough), (cot.at[:, :16, :], low), (cot.at[:, width - 16 :, :], high)
    copies = [pltpu.make_async_copy(*pair, sems.at[k]) for k, pair in enumerate(pairs)]
    for c in copies:
        c.start()
    copies[0].wait()
    for s, out in enumerate(outs):
        start = pl.multiple_of((me ^ s) * cols, cols)
        for j in range(cr):
            out[j * cols : (j + 1) * cols, :] = rough[j, pl.ds(start, cols), :]
    r = lax.broadcasted_iota(jnp.int32, (rows, rows * 16), 0)
    p = lax.broadcasted_iota(jnp.int32, (rows, rows * 16), 1)
    sides = []
    for c, edge, pick in ((copies[1], low, 0), (copies[2], high, 15)):
        c.wait()
        sel = jnp.where(p == r * 16 + pick, 1.0, 0.0).astype(BF)
        flat = edge[...].reshape(rows * 16, ch)
        sides.append(jnp.dot(sel, flat, preferred_element_type=F32))
    for s in range(1, n):
        if is_edge(s):
            col = jnp.where((me ^ s) > me, sides[1], sides[0])
            outs[s][cr * cols :, :] = col.astype(BF)


def load_kernel(steps, cot, scales, moved, scale):
    rows, width, ch = cot.shape
    by = scales[pl.ds(steps[0], 1), :]
    scale[...] = by
    zero = jnp.zeros((1, ch), F32)

    def group(g, _):
        for q in range(4):
            r = g * 4 + q
            spread(moved, r + 1, (cot[r].astype(F32) * by).astype(BF), zero, zero)
        return 0

    lax.fori_loop(0, rows // 4, group, 0)


def edge_kernel(offset, shifts, scale, moved, *refs):
    blocks, (one, two, left, right) = refs[: len(shifts)], refs[len(shifts) :]
    core, _, me = place()
    _, rows, width, ch = moved.shape
    rows -= 2
    by = scale[...]
    for side, place_of in ((left, me - 1), (right, me + 1)):
        col = jnp.zeros((rows, ch), F32)
        for s, block in zip(shifts, blocks):
            edge = (block[offset:, :].astype(F32) * by).astype(BF).astype(F32)
            col = jnp.where((me ^ s) == place_of, edge, col)
        side[...] = col
    idx = lax.broadcasted_iota(jnp.int32, (16, ch), 0)
    ends = []
    for k in (0, rows - 1):
        tip = jnp.where(idx == 1, right[k : k + 1, :], 0.0)
        tip = jnp.where(idx == 0, left[k : k + 1, :], tip)
        ends.append((moved[1, k + 1].astype(F32), tip))
    (top, top_tip), (bottom, bottom_tip) = ends
    for out, first in ((one, core == 1), (two, core == 0)):
        out[:width, :] = jnp.where(first, top, bottom).astype(BF)
        out[width:, :] = jnp.where(first, top_tip, bottom_tip).astype(BF)


def spread_up(coarse_row, width):
    cols = coarse_row.shape[0]
    a = lax.broadcasted_iota(jnp.int32, (width, cols), 0)
    b = lax.broadcasted_iota(jnp.int32, (width, cols), 1)
    up = jnp.where(a // (width // cols) == b, 1.0, 0.0).astype(BF)
    return jnp.dot(up, coarse_row, preferred_element_type=F32)


def sigmoid(x):
    return 0.5 * jnp.tanh(0.5 * x) + 0.5


def gate(fine, coarse_row):
    hidden = fine.astype(F32) + spread_up(coarse_row, fine.shape[1])[None]
    return hidden, sigmoid(hidden)


def spread(moved, slot, rounded, left, right):
    width = rounded.shape[0]
    row = rounded.astype(F32)
    idx = lax.broadcasted_iota(jnp.int32, row.shape, 0)
    moved[0, slot] = jnp.where(idx == 0, left, pltpu.roll(row, 1, 0)).astype(BF)
    moved[1, slot] = rounded
    moved[2, slot] = jnp.where(idx == width - 1, right, pltpu.roll(row, width - 1, 0)).astype(BF)


def prepare_kernel(n, cr, fine, left, right, moved_in, *refs):
    blocks, (moved, act_t, strip, sums, up) = refs[:n], refs[n:]
    core, _, me = place()
    rows, width, ch = fine.shape
    cols = strip.shape[1]
    for s in range(n):
        for j in range(cr):
            strip[(me ^ s) * cr + j] = blocks[s][j * cols : (j + 1) * cols, :]
    idx = lax.broadcasted_iota(jnp.int32, (16, ch), 0)

    def patch(r, _):
        for k, low, pick, side in ((0, 0, 0, left), (2, width - 16, 15, right)):
            tile = moved[k, r + 1, low : low + 16, :].astype(F32)
            tile = jnp.where(idx == pick, side[pl.ds(r, 1), :], tile)
            moved[k, r + 1, low : low + 16, :] = tile.astype(BF)
        return 0

    lax.fori_loop(0, rows, patch, 0)
    last = rows // 4 - 1

    def build(g):
        up[g] = spread_up(strip[g], width)
        for r in range(4 * g, 4 * g + 4):
            hidden = fine[r].astype(F32) + up[g]
            act = (hidden * sigmoid(hidden)).astype(BF)
            act_t[:, r * width : (r + 1) * width] = act.T

    def share(g):
        for k in range(5):
            got = partial_tap(1 - core, k, 4 * g, 4, act_t, moved)
            sums[k] = got if g == 1 else sums[k] + got

    build(1)
    for g in range(1, last):
        build(g + 1 if g + 1 < last else 0)
        share(g)
    build(last)


def partial_tap(part, k, row, tall, act_t, moved):
    _, _, width, ch = moved.shape
    lhs = act_t[:, row * width : (row + tall) * width]
    t = 4 if isinstance(k, int) and k == 4 else part * 5 + k
    window = moved[2 - lax.rem(t, 3), pl.ds(2 - t // 3 + row, tall)]
    return jnp.dot(lhs, window.reshape(tall * width, ch), preferred_element_type=F32)


def weight_taps(part, act_t, moved, out, sums):
    _, plane, z = place()
    planes, zs, depth, half = out.shape
    rows = moved.shape[1] - 2
    ch = 2 * half
    step = ch // (planes * zs)
    z = lax.rem(z, zs)

    def put(unit, acc):
        at = pl.multiple_of(unit * step, step)
        for p in range(planes):
            for c in range(zs):
                b = (p * zs + c) * step
                out[p ^ plane, c ^ z, pl.ds(at, step), :] = acc[b : b + step].astype(BF)

    def total(k):
        if sums is None:
            return partial_tap(part, k, 0, rows, act_t, moved)
        first = partial_tap(part, k, 0, 4, act_t, moved)
        return sums[k] + first + partial_tap(part, k, rows - 4, 4, act_t, moved)

    def tap(k, _):
        acc = total(k)
        put(k, acc[:, :half])
        put(k + 4, acc[:, half:])
        return 0

    lax.fori_loop(0, 4, tap, 0)
    return put, total


def other_kernel(act_t, two, one, sums, moved_in, out, rest, moved):
    core, _, _ = place()
    _, rows, width, ch = moved.shape
    row = lax.axis_index("row")
    outer = (row == 0) | (row == lax.axis_size("row") - 1)
    next_chip = jnp.where(outer, 0.0, two[...].astype(F32))
    for slot, first in ((0, core == 1), (rows - 1, core == 0)):
        halo = jnp.where(first, one[...].astype(F32), next_chip)
        left, right = halo[width : width + 1], halo[width + 1 : width + 2]
        spread(moved, slot, halo[:width].astype(BF), left, right)
    put, total = weight_taps(1 - core, act_t, moved, out, sums)
    middle = total(4)
    low, high = middle[:, : ch // 2], middle[:, ch // 2 :]
    put(8, jnp.where(core == 1, low, high))
    rest[...] = jnp.where(core == 1, high, low)


def mine_kernel(act_t, rest, moved, out):
    core, _, _ = place()
    put, _ = weight_taps(core, act_t, moved, out, None)
    put(8, rest[...])


def strip_order(n):
    return list(range(n - 1, -1, -1))


def input_kernel(first, size, n, after, moved, fine, strip, weight, *refs):
    gf, gc, fines, pooled, sems = refs[-5:]
    _, _, me = place()
    cr = strip.shape[0] // n
    _, width, ch = fine.shape
    cols = strip.shape[1]
    wide = jnp.concatenate([weight[t] for t in range(9)], axis=1)
    copies = []
    for g in range(size):
        k = (strip_order(n)[(first + g) // cr] ^ me) * cr + (first + g) % cr
        r = 4 * k
        taps = [
            moved[2 - t % 3, pl.ds(2 - t // 3 + r, 4)].reshape(4 * width, ch) for t in range(9)
        ]
        dact = lax.dot_general(
            jnp.concatenate(taps, axis=1),
            wide,
            (((1,), (1,)), ((), ())),
            preferred_element_type=F32,
        ).reshape(4, width, ch)
        hidden, sig = gate(fine[pl.ds(r, 4)], strip[k])
        dhidden = dact * sig * (1.0 + hidden * (1.0 - sig))
        fines[g] = dhidden.astype(BF)
        tall = dhidden[0] + dhidden[1] + dhidden[2] + dhidden[3]
        for h in range(ch // 128):
            pooled[...] = tall[:, 128 * h : 128 * h + 128]
            every = [pooled[pl.ds(k, cols, stride=width // cols), :] for k in range(width // cols)]
            gc[g, h] = functools.reduce(jnp.add, every).astype(BF)
        copies.append(pltpu.make_async_copy(fines.at[g], gf.at[pl.ds(r, 4)], sems.at[g]))
        copies[-1].start()
    for c in copies:
        c.wait()


def finish_kernel(norm, zs, spots, n, *refs):
    pieces, parts = refs[: len(spots)], refs[len(spots) : len(spots) + n]
    if n:
        out, coarse_out, scratch, sems, coarse, coarse_sem = refs[-6:]
    else:
        out, scratch, sems = refs[-3:]
    core, plane, me = place()
    planes = lax.axis_size("row") // 2
    ch = out.shape[1]
    half = ch // 2
    tall = ch // planes
    step = tall // zs
    z = lax.rem(me, zs)
    copies = []
    for k, (flip, s, first) in enumerate(spots):
        part = core ^ flip
        lanes = pl.ds(pl.multiple_of(part * half, half), half)
        for c in range(pieces[k].shape[0]):
            x = pieces[k][c].astype(F32) * norm
            for t in range(9):
                scratch[k, c, t] = x[t * step : (t + 1) * step]
            b = pl.multiple_of((plane ^ s) * tall + ((first + c) ^ z) * step, step)
            span = pl.ds(b, step)
            taps = pl.ds(part * 5, 4)
            pairs = (
                (scratch.at[k, c, :4], out.at[taps, span, :half]),
                (scratch.at[k, c, 4:8], out.at[taps, span, half:]),
                (scratch.at[k, c, 8], out.at[4, span, lanes]),
            )
            for i, pair in enumerate(pairs):
                copies.append(pltpu.make_async_copy(*pair, sems.at[k, c, i]))
                copies[-1].start()
    if n:
        cr = coarse.shape[0]
        cols = coarse.shape[1] // n
        for s in range(n):
            start = pl.multiple_of((me ^ s) * cols, cols)
            for j in range(cr):
                for h in range(2):
                    b = (j * 2 + h) * cols
                    coarse[j, pl.ds(start, cols), pl.ds(h * half, half)] = parts[s][b : b + cols]
        copies.append(pltpu.make_async_copy(coarse, coarse_out, coarse_sem.at[0]))
        copies[-1].start()
    for c in copies:
        c.wait()


def xor_pairs(count, bit):
    return [(i, i ^ bit) for i in range(count)]


def per_device(fine_input, coarse_feat, conv_weight, step_scale, timesteps, cotangent):
    _, rows, width, ch = fine_input.shape
    n = lax.axis_size("col")
    nrow = lax.axis_size("row")
    planes = nrow // 2
    cr = coarse_feat.shape[1]
    cols = width // 4
    fine, cot, coarse = fine_input[0], cotangent[0], coarse_feat[0]
    weight = conv_weight.reshape(9, ch, ch)

    def shape(*dims, dtype=BF):
        return jax.ShapeDtypeStruct(dims, dtype)

    def col_swap(x, s):
        return lax.ppermute(x, "col", xor_pairs(n, s))

    blocks = pl.pallas_call(
        functools.partial(start_kernel, n),
        out_shape=[shape(cr * cols + (rows if s and is_edge(s) else 0), ch) for s in range(n)],
        in_specs=[hbm(), hbm()],
        out_specs=[vmem()] * n,
        scratch_shapes=[
            pltpu.VMEM(coarse.shape, BF),
            pltpu.VMEM((rows, 16, ch), BF),
            pltpu.VMEM((rows, 16, ch), BF),
            pltpu.SemaphoreType.DMA((3,)),
        ],
        compiler_params=params(START_MIB),
        cost_estimate=cost(1 << 31, 4 << 20),
        name="start",
    )(cot, coarse)
    blocks = list(blocks)
    moved, scale = pl.pallas_call(
        load_kernel,
        out_shape=[shape(3, rows + 2, width, ch), shape(1, ch, dtype=F32)],
        in_specs=[smem(), vmem(), vmem()],
        out_specs=[vmem()] * 2,
        compiler_params=params(4),
        cost_estimate=cost(1 << 20, 4 << 20),
        name="load",
    )(timesteps, cot, step_scale)

    shifts = [s for s in range(n - 1, 0, -1) if is_edge(s)]
    for s in shifts + [s for s in range(1, n) if not is_edge(s)]:
        blocks[s] = col_swap(blocks[s], s)

    halo, side = shape(width + 16, ch), shape(rows, ch, dtype=F32)
    one, two, left, right = pl.pallas_call(
        functools.partial(edge_kernel, cr * cols, shifts),
        out_shape=[halo, halo, side, side],
        in_specs=[vmem()] * (2 + len(shifts)),
        out_specs=[vmem()] * 4,
        compiler_params=params(4),
        cost_estimate=cost(1 << 18, 1 << 19),
        name="edges",
    )(scale, moved, *[blocks[s] for s in shifts])
    odd = range(1, nrow, 2)
    two = lax.ppermute(
        two, "row", [(i, (i + 1) % nrow) for i in odd] + [((i + 1) % nrow, i) for i in odd]
    )
    one = lax.ppermute(one, "row", xor_pairs(nrow, 1))

    groups = rows // 4
    moved, act_t, strip, sums = pl.pallas_call(
        functools.partial(prepare_kernel, n, cr),
        out_shape=[
            shape(*moved.shape),
            shape(ch, rows * width),
            shape(groups, cols, ch),
            shape(5, ch, ch, dtype=F32),
        ],
        in_specs=[vmem()] * (4 + n),
        out_specs=[vmem()] * 4,
        input_output_aliases={3: 0},
        scratch_shapes=[pltpu.VMEM((groups, width, ch), F32)],
        compiler_params=params(12),
        cost_estimate=cost(1 << 32, 4 << 20),
        name="prepare",
    )(fine, left, right, moved, *blocks)

    halves = n // 2
    aligned = ch // (planes * halves) % 16 == 0
    zs = halves if aligned else 1
    depth = 9 * ch // (planes * zs)
    half = ch // 2
    part = shape(planes, zs, depth, half)
    send, rest, moved = pl.pallas_call(
        other_kernel,
        out_shape=[part, shape(ch, half, dtype=F32), shape(*moved.shape)],
        in_specs=[vmem()] * 5,
        out_specs=[vmem()] * 3,
        input_output_aliases={4: 2},
        compiler_params=params(8),
        cost_estimate=cost(9 * rows * width * ch * ch // 4, 8 << 20),
        name="weight_other",
    )(act_t, two, one, sums, moved)
    keep = pl.pallas_call(
        mine_kernel,
        out_shape=part,
        in_specs=[vmem()] * 3,
        out_specs=vmem(),
        compiler_params=params(8),
        cost_estimate=cost(8 * rows * width * ch * ch, 8 << 20),
        name="weight_mine",
    )(act_t, rest, moved)

    done, pooled, made = [], [], 0

    def input_piece(size, after):
        nonlocal done, made
        *done, gc = pl.pallas_call(
            functools.partial(input_kernel, made, size, n),
            out_shape=[shape(rows, width, ch), shape(size, 2, cols, ch // 2)],
            in_specs=[pl.BlockSpec(memory_space=pl.ANY)]
            + [vmem()] * 4
            + [pl.BlockSpec(memory_space=pl.ANY) for _ in done],
            out_specs=[pl.BlockSpec(memory_space=pl.ANY), vmem()],
            input_output_aliases={5: 0} if done else {},
            scratch_shapes=[
                pltpu.VMEM((size, 4, width, ch), BF),
                pltpu.VMEM((width, 128), F32),
                pltpu.SemaphoreType.DMA((size,)),
            ],
            compiler_params=params(12),
            cost_estimate=cost(2 * 9 * 4 * size * width * ch * ch, 4 << 20),
            name="input_grad",
        )(after, moved, fine, strip, weight, *done)
        pooled.append(gc)
        made += size

    def beside(got, size, after):
        nonlocal done, pooled
        if size:
            input_piece(size, after)
            got, done, pooled = lax.optimization_barrier((got, done, pooled))
        return got

    def pooled_strip(s):
        at = strip_order(n).index(s) * cr
        groups_done = [x[g] for x in pooled for g in range(x.shape[0])]
        return jnp.concatenate([x.reshape(-1, ch // 2) for x in groups_done[at : at + cr]])

    def add(*terms):
        return functools.reduce(jnp.add, [t.astype(F32) for t in terms]).astype(BF)

    def core_swap(x):
        return lax.ppermute(x, "row", xor_pairs(nrow, 1))

    def plane_swap(x, s):
        return lax.ppermute(x, "row", xor_pairs(nrow, 2 * s))

    held = {s: [] for s in range(n)}

    def hop(bit, extra):
        sent = []
        for s in [s for s in held if s & bit]:
            sent += [(s, src, x) for src, x in held.pop(s) + [(0, pooled_strip(s))]]
        return sent, col_swap(jnp.concatenate(extra + [x for _, _, x in sent]), bit)

    def land(bit, sent, got, at):
        for s, src, x in sent:
            held[s ^ bit].append((src ^ bit, got[at : at + x.shape[0]]))
            at += x.shape[0]

    def ride(bit, total):
        sent, got = hop(bit, [total.reshape(-1, half)])
        at = total.size // half
        land(bit, sent, got, at)
        return got[:at].reshape(total.shape)

    sizes = piece_sizes(rows // 4)
    total = add(keep, core_swap(send))
    got = [plane_swap(total[s], s) for s in range(1, planes)]
    total = add(total[0], *beside(got, sizes[0], total))
    if not aligned:
        order = jnp.arange(halves) ^ (lax.axis_index("col") % halves)
        total = total.reshape(halves, depth // halves, half)[order]
    bit = halves // 2
    while bit:
        got = [col_swap(total[bit:], bit)]
        if bit == halves // 2:
            sent, far = hop(halves, [])
        total = add(total[:bit], *beside(got, sizes[1] if bit == 1 else 0, total))
        bit //= 2
    got = beside([col_swap(total, halves)], sizes[2], total)
    total = add(total, *got)
    land(halves, sent, far, 0)

    bit = 1
    while bit < halves // 2:
        total = jnp.concatenate([total, ride(bit, total)])
        bit *= 2
    came = ride(bit, total)
    if aligned:
        waves = [total, came]
    else:
        total = jnp.concatenate([total, came])
        waves = [total[order].reshape(1, depth, half)]
    ways = list(range(1, planes))
    waves = [[x] + [plane_swap(x, s) for s in ways] for x in waves]
    if aligned:
        waves[0][1:], waves[1][0] = lax.optimization_barrier((waves[0][1:], waves[1][0]))

    parts = held[0] + [(0, pooled_strip(0))]
    parts = [x for _, x in sorted(parts, key=lambda pair: pair[0])]
    pixels = rows * nrow * width * n

    def finish(out, pieces, spots, parts=()):
        coarse = [shape(cr, n * cols, ch)] if parts else []
        count, tall = len(pieces), pieces[0].shape[0]
        return pl.pallas_call(
            functools.partial(finish_kernel, float(pixels) ** -0.5, zs, spots, len(parts)),
            out_shape=[shape(9, ch, ch, dtype=F32)] + coarse,
            in_specs=[vmem()] * (count + len(parts)) + [hbm() for _ in out],
            out_specs=[hbm()] + [hbm() for _ in coarse],
            input_output_aliases={count + len(parts): 0} if out else {},
            scratch_shapes=[
                pltpu.VMEM((count, tall, 9, depth // 9, half), F32),
                pltpu.SemaphoreType.DMA((count, tall, 3)),
            ]
            + [x for c in coarse for x in (pltpu.VMEM(c.shape, BF), pltpu.SemaphoreType.DMA((1,)))],
            compiler_params=params(8),
            cost_estimate=cost(1 << 20, 4 << 20),
            name="finish",
        )(*pieces, *parts, *out)

    out, others, spots = [], [], ()
    for k, wave in enumerate(waves):
        if k:
            wave[1:], out = lax.optimization_barrier((wave[1:], out))
        swapped = core_swap(jnp.stack(wave))
        here = [(s, k * wave[0].shape[0]) for s in [0] + ways]
        places = [(0, *spot) for spot in here] + [(1, *spot) for spot in spots]
        out = finish(out, wave + others, tuple(places))
        others, spots = [swapped[i] for i in range(len(wave))], here
    grad_weight, grad_coarse = finish(out, others, tuple((1, *spot) for spot in spots), parts)
    return (done[0][None], grad_coarse[None], grad_weight.reshape(3, 3, ch, ch))


def piece_sizes(groups):
    sizes = [groups * 3 // 4, groups // 8]
    return sizes + [groups - sum(sizes)]


def solution(mesh):
    return jax.shard_map(
        per_device,
        mesh=mesh,
        in_specs=(
            P(None, "row", "col", None),
            P(None, ("row", "col"), None, None),
            P(),
            P(),
            P(),
            P(None, "row", "col", None),
        ),
        out_specs=(P(None, "row", "col", None), P(None, ("row", "col"), None, None), P()),
        check_vma=False,
    )
```

```python
import functools
import jax
import jax.numpy as jnp
from jax import lax
from jax.experimental import pallas as pl
from jax.experimental.pallas import tpu as pltpu
from jax.sharding import PartitionSpec as P

BF = jnp.bfloat16
F32 = jnp.float32
MB = 1024 * 1024
START_MIB = 53.7


def smem():
    return pl.BlockSpec(memory_space=pltpu.SMEM)


def vmem():
    return pl.BlockSpec(memory_space=pltpu.VMEM)


def params(mib):
    return pltpu.CompilerParams(vmem_limit_bytes=int(mib * MB))


def cost(flops, nbytes):
    return pl.CostEstimate(flops=flops, bytes_accessed=nbytes, transcendentals=0)


def hbm():
    return pl.BlockSpec(memory_space=pltpu.HBM)


def place():
    row = lax.axis_index("row")
    return lax.rem(row, 2), row // 2, lax.axis_index("col")


def is_edge(s):
    return s & (s + 1) == 0


def start_kernel(n, cot, coarse, *refs):
    outs, (rough, low, high, sems) = refs[:n], refs[n:]
    _, _, me = place()
    cr, _, ch = rough.shape
    rows, width, _ = cot.shape
    cols = rough.shape[1] // n
    pairs = (coarse, rough), (cot.at[:, :16, :], low), (cot.at[:, width - 16 :, :], high)
    copies = [pltpu.make_async_copy(*pair, sems.at[k]) for k, pair in enumerate(pairs)]
    for c in copies:
        c.start()
    copies[0].wait()
    for s, out in enumerate(outs):
        start = pl.multiple_of((me ^ s) * cols, cols)
        for j in range(cr):
            out[j * cols : (j + 1) * cols, :] = rough[j, pl.ds(start, cols), :]
    r = lax.broadcasted_iota(jnp.int32, (rows, rows * 16), 0)
    p = lax.broadcasted_iota(jnp.int32, (rows, rows * 16), 1)
    sides = []
    for c, edge, pick in ((copies[1], low, 0), (copies[2], high, 15)):
        c.wait()
        sel = jnp.where(p == r * 16 + pick, 1.0, 0.0).astype(BF)
        flat = edge[...].reshape(rows * 16, ch)
        sides.append(jnp.dot(sel, flat, preferred_element_type=F32))
    for s in range(1, n):
        if is_edge(s):
            col = jnp.where((me ^ s) > me, sides[1], sides[0])
            outs[s][cr * cols :, :] = col.astype(BF)


def load_kernel(steps, cot, scales, moved, scale):
    rows, width, ch = cot.shape
    by = scales[pl.ds(steps[0], 1), :]
    scale[...] = by
    zero = jnp.zeros((1, ch), F32)

    def group(g, _):
        for q in range(4):
            r = g * 4 + q
            spread(moved, r + 1, (cot[r].astype(F32) * by).astype(BF), zero, zero)
        return 0

    lax.fori_loop(0, rows // 4, group, 0)


def edge_kernel(offset, shifts, scale, moved, *refs):
    blocks, (one, two, left, right) = refs[: len(shifts)], refs[len(shifts) :]
    core, _, me = place()
    _, rows, width, ch = moved.shape
    rows -= 2
    by = scale[...]
    for side, place_of in ((left, me - 1), (right, me + 1)):
        col = jnp.zeros((rows, ch), F32)
        for s, block in zip(shifts, blocks):
            edge = (block[offset:, :].astype(F32) * by).astype(BF).astype(F32)
            col = jnp.where((me ^ s) == place_of, edge, col)
        side[...] = col
    idx = lax.broadcasted_iota(jnp.int32, (16, ch), 0)
    ends = []
    for k in (0, rows - 1):
        tip = jnp.where(idx == 1, right[k : k + 1, :], 0.0)
        tip = jnp.where(idx == 0, left[k : k + 1, :], tip)
        ends.append((moved[1, k + 1].astype(F32), tip))
    (top, top_tip), (bottom, bottom_tip) = ends
    for out, first in ((one, core == 1), (two, core == 0)):
        out[:width, :] = jnp.where(first, top, bottom).astype(BF)
        out[width:, :] = jnp.where(first, top_tip, bottom_tip).astype(BF)


def spread_up(coarse_row, width):
    cols = coarse_row.shape[0]
    a = lax.broadcasted_iota(jnp.int32, (width, cols), 0)
    b = lax.broadcasted_iota(jnp.int32, (width, cols), 1)
    up = jnp.where(a // (width // cols) == b, 1.0, 0.0).astype(BF)
    return jnp.dot(up, coarse_row, preferred_element_type=F32)


def sigmoid(x):
    return 0.5 * jnp.tanh(0.5 * x) + 0.5


def gate(fine, coarse_row):
    hidden = fine.astype(F32) + spread_up(coarse_row, fine.shape[1])[None]
    return hidden, sigmoid(hidden)


def spread(moved, slot, rounded, left, right):
    width = rounded.shape[0]
    row = rounded.astype(F32)
    idx = lax.broadcasted_iota(jnp.int32, row.shape, 0)
    moved[0, slot] = jnp.where(idx == 0, left, pltpu.roll(row, 1, 0)).astype(BF)
    moved[1, slot] = rounded
    moved[2, slot] = jnp.where(idx == width - 1, right, pltpu.roll(row, width - 1, 0)).astype(BF)


def prepare_kernel(n, cr, fine, left, right, moved_in, *refs):
    blocks, (moved, act_t, strip, sums, up) = refs[:n], refs[n:]
    core, _, me = place()
    rows, width, ch = fine.shape
    cols = strip.shape[1]
    for s in range(n):
        for j in range(cr):
            strip[(me ^ s) * cr + j] = blocks[s][j * cols : (j + 1) * cols, :]
    idx = lax.broadcasted_iota(jnp.int32, (16, ch), 0)

    def patch(r, _):
        for k, low, pick, side in ((0, 0, 0, left), (2, width - 16, 15, right)):
            tile = moved[k, r + 1, low : low + 16, :].astype(F32)
            tile = jnp.where(idx == pick, side[pl.ds(r, 1), :], tile)
            moved[k, r + 1, low : low + 16, :] = tile.astype(BF)
        return 0

    lax.fori_loop(0, rows, patch, 0)
    last = rows // 4 - 1

    def build(g):
        up[g] = spread_up(strip[g], width)
        for r in range(4 * g, 4 * g + 4):
            hidden = fine[r].astype(F32) + up[g]
            act = (hidden * sigmoid(hidden)).astype(BF)
            act_t[:, r * width : (r + 1) * width] = act.T

    def share(g):
        for k in range(5):
            got = partial_tap(1 - core, k, 4 * g, 4, act_t, moved)
            sums[k] = got if g == 1 else sums[k] + got

    build(1)
    for g in range(1, last):
        build(g + 1 if g + 1 < last else 0)
        share(g)
    build(last)


def partial_tap(part, k, row, tall, act_t, moved):
    _, _, width, ch = moved.shape
    lhs = act_t[:, row * width : (row + tall) * width]
    t = 4 if isinstance(k, int) and k == 4 else part * 5 + k
    window = moved[2 - lax.rem(t, 3), pl.ds(2 - t // 3 + row, tall)]
    return jnp.dot(lhs, window.reshape(tall * width, ch), preferred_element_type=F32)


def weight_taps(part, act_t, moved, out, sums):
    _, plane, z = place()
    planes, zs, depth, half = out.shape
    rows = moved.shape[1] - 2
    ch = 2 * half
    step = ch // (planes * zs)
    z = lax.rem(z, zs)

    def put(unit, acc):
        at = pl.multiple_of(unit * step, step)
        for p in range(planes):
            for c in range(zs):
                b = (p * zs + c) * step
                out[p ^ plane, c ^ z, pl.ds(at, step), :] = acc[b : b + step].astype(BF)

    def total(k):
        if sums is None:
            return partial_tap(part, k, 0, rows, act_t, moved)
        first = partial_tap(part, k, 0, 4, act_t, moved)
        return sums[k] + first + partial_tap(part, k, rows - 4, 4, act_t, moved)

    def tap(k, _):
        acc = total(k)
        put(k, acc[:, :half])
        put(k + 4, acc[:, half:])
        return 0

    lax.fori_loop(0, 4, tap, 0)
    return put, total


def other_kernel(act_t, two, one, sums, moved_in, out, rest, moved):
    core, _, _ = place()
    _, rows, width, ch = moved.shape
    row = lax.axis_index("row")
    outer = (row == 0) | (row == lax.axis_size("row") - 1)
    next_chip = jnp.where(outer, 0.0, two[...].astype(F32))
    for slot, first in ((0, core == 1), (rows - 1, core == 0)):
        halo = jnp.where(first, one[...].astype(F32), next_chip)
        left, right = halo[width : width + 1], halo[width + 1 : width + 2]
        spread(moved, slot, halo[:width].astype(BF), left, right)
    put, total = weight_taps(1 - core, act_t, moved, out, sums)
    middle = total(4)
    low, high = middle[:, : ch // 2], middle[:, ch // 2 :]
    put(8, jnp.where(core == 1, low, high))
    rest[...] = jnp.where(core == 1, high, low)


def mine_kernel(act_t, rest, moved, out):
    core, _, _ = place()
    put, _ = weight_taps(core, act_t, moved, out, None)
    put(8, rest[...])


def strip_order(n):
    return list(range(n - 1, -1, -1))


def input_kernel(first, size, n, after, moved, fine, strip, weight, *refs):
    gf, gc, fines, pooled, sems = refs[-5:]
    _, _, me = place()
    cr = strip.shape[0] // n
    _, width, ch = fine.shape
    cols = strip.shape[1]
    wide = jnp.concatenate([weight[t] for t in range(9)], axis=1)
    copies = []
    for g in range(size):
        k = (strip_order(n)[(first + g) // cr] ^ me) * cr + (first + g) % cr
        r = 4 * k
        taps = [
            moved[2 - t % 3, pl.ds(2 - t // 3 + r, 4)].reshape(4 * width, ch) for t in range(9)
        ]
        dact = lax.dot_general(
            jnp.concatenate(taps, axis=1),
            wide,
            (((1,), (1,)), ((), ())),
            preferred_element_type=F32,
        ).reshape(4, width, ch)
        hidden, sig = gate(fine[pl.ds(r, 4)], strip[k])
        dhidden = dact * sig * (1.0 + hidden * (1.0 - sig))
        fines[g] = dhidden.astype(BF)
        tall = dhidden[0] + dhidden[1] + dhidden[2] + dhidden[3]
        for h in range(ch // 128):
            pooled[...] = tall[:, 128 * h : 128 * h + 128]
            every = [pooled[pl.ds(k, cols, stride=width // cols), :] for k in range(width // cols)]
            gc[g, h] = functools.reduce(jnp.add, every).astype(BF)
        copies.append(pltpu.make_async_copy(fines.at[g], gf.at[pl.ds(r, 4)], sems.at[g]))
        copies[-1].start()
    for c in copies:
        c.wait()


def finish_kernel(norm, zs, spots, n, *refs):
    pieces, parts = refs[: len(spots)], refs[len(spots) : len(spots) + n]
    if n:
        out, coarse_out, scratch, sems, coarse, coarse_sem = refs[-6:]
    else:
        out, scratch, sems = refs[-3:]
    core, plane, me = place()
    planes = lax.axis_size("row") // 2
    ch = out.shape[1]
    half = ch // 2
    tall = ch // planes
    step = tall // zs
    z = lax.rem(me, zs)
    copies = []
    for k, (flip, s, first) in enumerate(spots):
        part = core ^ flip
        lanes = pl.ds(pl.multiple_of(part * half, half), half)
        for c in range(pieces[k].shape[0]):
            x = pieces[k][c].astype(F32) * norm
            for t in range(9):
                scratch[k, c, t] = x[t * step : (t + 1) * step]
            b = pl.multiple_of((plane ^ s) * tall + ((first + c) ^ z) * step, step)
            span = pl.ds(b, step)
            taps = pl.ds(part * 5, 4)
            pairs = (
                (scratch.at[k, c, :4], out.at[taps, span, :half]),
                (scratch.at[k, c, 4:8], out.at[taps, span, half:]),
                (scratch.at[k, c, 8], out.at[4, span, lanes]),
            )
            for i, pair in enumerate(pairs):
                copies.append(pltpu.make_async_copy(*pair, sems.at[k, c, i]))
                copies[-1].start()
    if n:
        cr = coarse.shape[0]
        cols = coarse.shape[1] // n
        for s in range(n):
            start = pl.multiple_of((me ^ s) * cols, cols)
            for j in range(cr):
                for h in range(2):
                    b = (j * 2 + h) * cols
                    coarse[j, pl.ds(start, cols), pl.ds(h * half, half)] = parts[s][b : b + cols]
        copies.append(pltpu.make_async_copy(coarse, coarse_out, coarse_sem.at[0]))
        copies[-1].start()
    for c in copies:
        c.wait()


def xor_pairs(count, bit):
    return [(i, i ^ bit) for i in range(count)]


def per_device(fine_input, coarse_feat, conv_weight, step_scale, timesteps, cotangent):
    _, rows, width, ch = fine_input.shape
    n = lax.axis_size("col")
    nrow = lax.axis_size("row")
    planes = nrow // 2
    cr = coarse_feat.shape[1]
    cols = width // 4
    fine, cot, coarse = fine_input[0], cotangent[0], coarse_feat[0]
    weight = conv_weight.reshape(9, ch, ch)

    def shape(*dims, dtype=BF):
        return jax.ShapeDtypeStruct(dims, dtype)

    def col_swap(x, s):
        return lax.ppermute(x, "col", xor_pairs(n, s))

    blocks = pl.pallas_call(
        functools.partial(start_kernel, n),
        out_shape=[shape(cr * cols + (rows if s and is_edge(s) else 0), ch) for s in range(n)],
        in_specs=[hbm(), hbm()],
        out_specs=[vmem()] * n,
        scratch_shapes=[
            pltpu.VMEM(coarse.shape, BF),
            pltpu.VMEM((rows, 16, ch), BF),
            pltpu.VMEM((rows, 16, ch), BF),
            pltpu.SemaphoreType.DMA((3,)),
        ],
        compiler_params=params(START_MIB),
        cost_estimate=cost(1 << 31, 4 << 20),
        name="start",
    )(cot, coarse)
    blocks = list(blocks)
    moved, scale = pl.pallas_call(
        load_kernel,
        out_shape=[shape(3, rows + 2, width, ch), shape(1, ch, dtype=F32)],
        in_specs=[smem(), vmem(), vmem()],
        out_specs=[vmem()] * 2,
        compiler_params=params(4),
        cost_estimate=cost(1 << 20, 4 << 20),
        name="load",
    )(timesteps, cot, step_scale)

    shifts = [s for s in range(n - 1, 0, -1) if is_edge(s)]
    for s in shifts + [s for s in range(1, n) if not is_edge(s)]:
        blocks[s] = col_swap(blocks[s], s)

    halo, side = shape(width + 16, ch), shape(rows, ch, dtype=F32)
    one, two, left, right = pl.pallas_call(
        functools.partial(edge_kernel, cr * cols, shifts),
        out_shape=[halo, halo, side, side],
        in_specs=[vmem()] * (2 + len(shifts)),
        out_specs=[vmem()] * 4,
        compiler_params=params(4),
        cost_estimate=cost(1 << 18, 1 << 19),
        name="edges",
    )(scale, moved, *[blocks[s] for s in shifts])
    odd = range(1, nrow, 2)
    two = lax.ppermute(
        two, "row", [(i, (i + 1) % nrow) for i in odd] + [((i + 1) % nrow, i) for i in odd]
    )
    one = lax.ppermute(one, "row", xor_pairs(nrow, 1))

    groups = rows // 4
    moved, act_t, strip, sums = pl.pallas_call(
        functools.partial(prepare_kernel, n, cr),
        out_shape=[
            shape(*moved.shape),
            shape(ch, rows * width),
            shape(groups, cols, ch),
            shape(5, ch, ch, dtype=F32),
        ],
        in_specs=[vmem()] * (4 + n),
        out_specs=[vmem()] * 4,
        input_output_aliases={3: 0},
        scratch_shapes=[pltpu.VMEM((groups, width, ch), F32)],
        compiler_params=params(12),
        cost_estimate=cost(1 << 32, 4 << 20),
        name="prepare",
    )(fine, left, right, moved, *blocks)

    halves = n // 2
    aligned = ch // (planes * halves) % 16 == 0
    zs = halves if aligned else 1
    depth = 9 * ch // (planes * zs)
    half = ch // 2
    part = shape(planes, zs, depth, half)
    send, rest, moved = pl.pallas_call(
        other_kernel,
        out_shape=[part, shape(ch, half, dtype=F32), shape(*moved.shape)],
        in_specs=[vmem()] * 5,
        out_specs=[vmem()] * 3,
        input_output_aliases={4: 2},
        compiler_params=params(8),
        cost_estimate=cost(9 * rows * width * ch * ch // 4, 8 << 20),
        name="weight_other",
    )(act_t, two, one, sums, moved)
    keep = pl.pallas_call(
        mine_kernel,
        out_shape=part,
        in_specs=[vmem()] * 3,
        out_specs=vmem(),
        compiler_params=params(8),
        cost_estimate=cost(8 * rows * width * ch * ch, 8 << 20),
        name="weight_mine",
    )(act_t, rest, moved)

    done, pooled, made = [], [], 0

    def input_piece(size, after):
        nonlocal done, made
        *done, gc = pl.pallas_call(
            functools.partial(input_kernel, made, size, n),
            out_shape=[shape(rows, width, ch), shape(size, 2, cols, ch // 2)],
            in_specs=[pl.BlockSpec(memory_space=pl.ANY)]
            + [vmem()] * 4
            + [pl.BlockSpec(memory_space=pl.ANY) for _ in done],
            out_specs=[pl.BlockSpec(memory_space=pl.ANY), vmem()],
            input_output_aliases={5: 0} if done else {},
            scratch_shapes=[
                pltpu.VMEM((size, 4, width, ch), BF),
                pltpu.VMEM((width, 128), F32),
                pltpu.SemaphoreType.DMA((size,)),
            ],
            compiler_params=params(12),
            cost_estimate=cost(2 * 9 * 4 * size * width * ch * ch, 4 << 20),
            name="input_grad",
        )(after, moved, fine, strip, weight, *done)
        pooled.append(gc)
        made += size

    def beside(got, size, after):
        nonlocal done, pooled
        if size:
            input_piece(size, after)
            got, done, pooled = lax.optimization_barrier((got, done, pooled))
        return got

    def pooled_strip(s):
        at = strip_order(n).index(s) * cr
        groups_done = [x[g] for x in pooled for g in range(x.shape[0])]
        return jnp.concatenate([x.reshape(-1, ch // 2) for x in groups_done[at : at + cr]])

    def add(*terms):
        return functools.reduce(jnp.add, [t.astype(F32) for t in terms]).astype(BF)

    def core_swap(x):
        return lax.ppermute(x, "row", xor_pairs(nrow, 1))

    def plane_swap(x, s):
        return lax.ppermute(x, "row", xor_pairs(nrow, 2 * s))

    held = {s: [] for s in range(n)}

    def hop(bit, extra):
        sent = []
        for s in [s for s in held if s & bit]:
            sent += [(s, src, x) for src, x in held.pop(s) + [(0, pooled_strip(s))]]
        return sent, col_swap(jnp.concatenate(extra + [x for _, _, x in sent]), bit)

    def land(bit, sent, got, at):
        for s, src, x in sent:
            held[s ^ bit].append((src ^ bit, got[at : at + x.shape[0]]))
            at += x.shape[0]

    def ride(bit, total):
        sent, got = hop(bit, [total.reshape(-1, half)])
        at = total.size // half
        land(bit, sent, got, at)
        return got[:at].reshape(total.shape)

    sizes = piece_sizes(rows // 4)
    total = add(keep, core_swap(send))
    got = [plane_swap(total[s], s) for s in range(1, planes)]
    total = add(total[0], *beside(got, sizes[0], total))
    if not aligned:
        order = jnp.arange(halves) ^ (lax.axis_index("col") % halves)
        total = total.reshape(halves, depth // halves, half)[order]
    bit = halves // 2
    while bit:
        got = [col_swap(total[bit:], bit)]
        if bit == halves // 2:
            sent, far = hop(halves, [])
        total = add(total[:bit], *beside(got, sizes[1] if bit == 1 else 0, total))
        bit //= 2
    got = beside([col_swap(total, halves)], sizes[2], total)
    total = add(total, *got)
    land(halves, sent, far, 0)

    bit = 1
    while bit < halves // 2:
        total = jnp.concatenate([total, ride(bit, total)])
        bit *= 2
    came = ride(bit, total)
    if aligned:
        waves = [total, came]
    else:
        total = jnp.concatenate([total, came])
        waves = [total[order].reshape(1, depth, half)]
    ways = list(range(1, planes))
    waves = [[x] + [plane_swap(x, s) for s in ways] for x in waves]
    if aligned:
        waves[0][1:], waves[1][0] = lax.optimization_barrier((waves[0][1:], waves[1][0]))

    parts = held[0] + [(0, pooled_strip(0))]
    parts = [x for _, x in sorted(parts, key=lambda pair: pair[0])]
    pixels = rows * nrow * width * n

    def finish(out, pieces, spots, parts=()):
        coarse = [shape(cr, n * cols, ch)] if parts else []
        count, tall = len(pieces), pieces[0].shape[0]
        return pl.pallas_call(
            functools.partial(finish_kernel, float(pixels) ** -0.5, zs, spots, len(parts)),
            out_shape=[shape(9, ch, ch, dtype=F32)] + coarse,
            in_specs=[vmem()] * (count + len(parts)) + [hbm() for _ in out],
            out_specs=[hbm()] + [hbm() for _ in coarse],
            input_output_aliases={count + len(parts): 0} if out else {},
            scratch_shapes=[
                pltpu.VMEM((count, tall, 9, depth // 9, half), F32),
                pltpu.SemaphoreType.DMA((count, tall, 3)),
            ]
            + [x for c in coarse for x in (pltpu.VMEM(c.shape, BF), pltpu.SemaphoreType.DMA((1,)))],
            compiler_params=params(8),
            cost_estimate=cost(1 << 20, 4 << 20),
            name="finish",
        )(*pieces, *parts, *out)

    out, others, spots = [], [], ()
    for k, wave in enumerate(waves):
        if k:
            wave[1:], out = lax.optimization_barrier((wave[1:], out))
        swapped = core_swap(jnp.stack(wave))
        here = [(s, k * wave[0].shape[0]) for s in [0] + ways]
        places = [(0, *spot) for spot in here] + [(1, *spot) for spot in spots]
        out = finish(out, wave + others, tuple(places))
        others, spots = [swapped[i] for i in range(len(wave))], here
    grad_weight, grad_coarse = finish(out, others, tuple((1, *spot) for spot in spots), parts)
    return (done[0][None], grad_coarse[None], grad_weight.reshape(3, 3, ch, ch))


def piece_sizes(groups):
    return [groups * 3 // 4, 0, groups - groups * 3 // 4]


def solution(mesh):
    return jax.shard_map(
        per_device,
        mesh=mesh,
        in_specs=(
            P(None, "row", "col", None),
            P(None, ("row", "col"), None, None),
            P(),
            P(),
            P(),
            P(None, "row", "col", None),
        ),
        out_specs=(P(None, "row", "col", None), P(None, ("row", "col"), None, None), P()),
        check_vma=False,
    )
```

```python
import functools
import jax
import jax.numpy as jnp
from jax import lax
from jax.experimental import pallas as pl
from jax.experimental.pallas import tpu as pltpu
from jax.sharding import PartitionSpec as P

BF = jnp.bfloat16
F32 = jnp.float32
MB = 1024 * 1024
START_MIB = 53.7


def smem():
    return pl.BlockSpec(memory_space=pltpu.SMEM)


def vmem():
    return pl.BlockSpec(memory_space=pltpu.VMEM)


def params(mib):
    return pltpu.CompilerParams(vmem_limit_bytes=int(mib * MB))


def cost(flops, nbytes):
    return pl.CostEstimate(flops=flops, bytes_accessed=nbytes, transcendentals=0)


def hbm():
    return pl.BlockSpec(memory_space=pltpu.HBM)


def place():
    row = lax.axis_index("row")
    return lax.rem(row, 2), row // 2, lax.axis_index("col")


def is_edge(s):
    return s & (s + 1) == 0


def start_kernel(n, cot, coarse, *refs):
    outs, (rough, low, high, sems) = refs[:n], refs[n:]
    _, _, me = place()
    cr, _, ch = rough.shape
    rows, width, _ = cot.shape
    cols = rough.shape[1] // n
    pairs = (coarse, rough), (cot.at[:, :16, :], low), (cot.at[:, width - 16 :, :], high)
    copies = [pltpu.make_async_copy(*pair, sems.at[k]) for k, pair in enumerate(pairs)]
    for c in copies:
        c.start()
    copies[0].wait()
    for s, out in enumerate(outs):
        start = pl.multiple_of((me ^ s) * cols, cols)
        for j in range(cr):
            out[j * cols : (j + 1) * cols, :] = rough[j, pl.ds(start, cols), :]
    r = lax.broadcasted_iota(jnp.int32, (rows, rows * 16), 0)
    p = lax.broadcasted_iota(jnp.int32, (rows, rows * 16), 1)
    sides = []
    for c, edge, pick in ((copies[1], low, 0), (copies[2], high, 15)):
        c.wait()
        sel = jnp.where(p == r * 16 + pick, 1.0, 0.0).astype(BF)
        flat = edge[...].reshape(rows * 16, ch)
        sides.append(jnp.dot(sel, flat, preferred_element_type=F32))
    for s in range(1, n):
        if is_edge(s):
            col = jnp.where((me ^ s) > me, sides[1], sides[0])
            outs[s][cr * cols :, :] = col.astype(BF)


def load_kernel(steps, cot, scales, moved, scale):
    rows, width, ch = cot.shape
    by = scales[pl.ds(steps[0], 1), :]
    scale[...] = by
    zero = jnp.zeros((1, ch), F32)

    def group(g, _):
        for q in range(4):
            r = g * 4 + q
            spread(moved, r + 1, (cot[r].astype(F32) * by).astype(BF), zero, zero)
        return 0

    lax.fori_loop(0, rows // 4, group, 0)


def edge_kernel(offset, shifts, scale, moved, *refs):
    blocks, (one, two, left, right) = refs[: len(shifts)], refs[len(shifts) :]
    core, _, me = place()
    _, rows, width, ch = moved.shape
    rows -= 2
    by = scale[...]
    for side, place_of in ((left, me - 1), (right, me + 1)):
        col = jnp.zeros((rows, ch), F32)
        for s, block in zip(shifts, blocks):
            edge = (block[offset:, :].astype(F32) * by).astype(BF).astype(F32)
            col = jnp.where((me ^ s) == place_of, edge, col)
        side[...] = col
    idx = lax.broadcasted_iota(jnp.int32, (16, ch), 0)
    ends = []
    for k in (0, rows - 1):
        tip = jnp.where(idx == 1, right[k : k + 1, :], 0.0)
        tip = jnp.where(idx == 0, left[k : k + 1, :], tip)
        ends.append((moved[1, k + 1].astype(F32), tip))
    (top, top_tip), (bottom, bottom_tip) = ends
    for out, first in ((one, core == 1), (two, core == 0)):
        out[:width, :] = jnp.where(first, top, bottom).astype(BF)
        out[width:, :] = jnp.where(first, top_tip, bottom_tip).astype(BF)


def spread_up(coarse_row, width):
    cols = coarse_row.shape[0]
    a = lax.broadcasted_iota(jnp.int32, (width, cols), 0)
    b = lax.broadcasted_iota(jnp.int32, (width, cols), 1)
    up = jnp.where(a // (width // cols) == b, 1.0, 0.0).astype(BF)
    return jnp.dot(up, coarse_row, preferred_element_type=F32)


def sigmoid(x):
    return 0.5 * jnp.tanh(0.5 * x) + 0.5


def gate(fine, coarse_row):
    hidden = fine.astype(F32) + spread_up(coarse_row, fine.shape[1])[None]
    return hidden, sigmoid(hidden)


def spread(moved, slot, rounded, left, right):
    width = rounded.shape[0]
    row = rounded.astype(F32)
    idx = lax.broadcasted_iota(jnp.int32, row.shape, 0)
    moved[0, slot] = jnp.where(idx == 0, left, pltpu.roll(row, 1, 0)).astype(BF)
    moved[1, slot] = rounded
    moved[2, slot] = jnp.where(idx == width - 1, right, pltpu.roll(row, width - 1, 0)).astype(BF)


def prepare_kernel(n, cr, fine, left, right, moved_in, *refs):
    blocks, (moved, act_t, strip, sums, up) = refs[:n], refs[n:]
    core, _, me = place()
    rows, width, ch = fine.shape
    cols = strip.shape[1]
    for s in range(n):
        for j in range(cr):
            strip[(me ^ s) * cr + j] = blocks[s][j * cols : (j + 1) * cols, :]
    idx = lax.broadcasted_iota(jnp.int32, (16, ch), 0)

    def patch(r, _):
        for k, low, pick, side in ((0, 0, 0, left), (2, width - 16, 15, right)):
            tile = moved[k, r + 1, low : low + 16, :].astype(F32)
            tile = jnp.where(idx == pick, side[pl.ds(r, 1), :], tile)
            moved[k, r + 1, low : low + 16, :] = tile.astype(BF)
        return 0

    lax.fori_loop(0, rows, patch, 0)
    last = rows // 4 - 1

    def build(g):
        up[g] = spread_up(strip[g], width)
        for r in range(4 * g, 4 * g + 4):
            hidden = fine[r].astype(F32) + up[g]
            act = (hidden * sigmoid(hidden)).astype(BF)
            act_t[:, r * width : (r + 1) * width] = act.T

    def share(g):
        for k in range(5):
            got = partial_tap(1 - core, k, 4 * g, 4, act_t, moved)
            sums[k] = got if g == 1 else sums[k] + got

    build(1)
    for g in range(1, last):
        build(g + 1 if g + 1 < last else 0)
        share(g)
    build(last)


def partial_tap(part, k, row, tall, act_t, moved):
    _, _, width, ch = moved.shape
    lhs = act_t[:, row * width : (row + tall) * width]
    t = 4 if isinstance(k, int) and k == 4 else part * 5 + k
    window = moved[2 - lax.rem(t, 3), pl.ds(2 - t // 3 + row, tall)]
    return jnp.dot(lhs, window.reshape(tall * width, ch), preferred_element_type=F32)


def weight_taps(part, act_t, moved, out, sums):
    _, plane, z = place()
    planes, zs, depth, half = out.shape
    rows = moved.shape[1] - 2
    ch = 2 * half
    step = ch // (planes * zs)
    z = lax.rem(z, zs)

    def put(unit, acc):
        at = pl.multiple_of(unit * step, step)
        for p in range(planes):
            for c in range(zs):
                b = (p * zs + c) * step
                out[p ^ plane, c ^ z, pl.ds(at, step), :] = acc[b : b + step].astype(BF)

    def total(k):
        if sums is None:
            return partial_tap(part, k, 0, rows, act_t, moved)
        first = partial_tap(part, k, 0, 4, act_t, moved)
        return sums[k] + first + partial_tap(part, k, rows - 4, 4, act_t, moved)

    def tap(k, _):
        acc = total(k)
        put(k, acc[:, :half])
        put(k + 4, acc[:, half:])
        return 0

    lax.fori_loop(0, 4, tap, 0)
    return put, total


def other_kernel(act_t, two, one, sums, moved_in, out, rest, moved):
    core, _, _ = place()
    _, rows, width, ch = moved.shape
    row = lax.axis_index("row")
    outer = (row == 0) | (row == lax.axis_size("row") - 1)
    next_chip = jnp.where(outer, 0.0, two[...].astype(F32))
    for slot, first in ((0, core == 1), (rows - 1, core == 0)):
        halo = jnp.where(first, one[...].astype(F32), next_chip)
        left, right = halo[width : width + 1], halo[width + 1 : width + 2]
        spread(moved, slot, halo[:width].astype(BF), left, right)
    put, total = weight_taps(1 - core, act_t, moved, out, sums)
    middle = total(4)
    low, high = middle[:, : ch // 2], middle[:, ch // 2 :]
    put(8, jnp.where(core == 1, low, high))
    rest[...] = jnp.where(core == 1, high, low)


def mine_kernel(act_t, rest, moved, out):
    core, _, _ = place()
    put, _ = weight_taps(core, act_t, moved, out, None)
    put(8, rest[...])


def strip_order(n):
    return list(range(n - 1, -1, -1))


def input_kernel(first, size, n, after, moved, fine, strip, weight, *refs):
    gf, gc, fines, pooled, sems = refs[-5:]
    _, _, me = place()
    cr = strip.shape[0] // n
    _, width, ch = fine.shape
    cols = strip.shape[1]
    wide = jnp.concatenate([weight[t] for t in range(9)], axis=1)
    copies = []
    for g in range(size):
        k = (strip_order(n)[(first + g) // cr] ^ me) * cr + (first + g) % cr
        r = 4 * k
        taps = [
            moved[2 - t % 3, pl.ds(2 - t // 3 + r, 4)].reshape(4 * width, ch) for t in range(9)
        ]
        dact = lax.dot_general(
            jnp.concatenate(taps, axis=1),
            wide,
            (((1,), (1,)), ((), ())),
            preferred_element_type=F32,
        ).reshape(4, width, ch)
        hidden, sig = gate(fine[pl.ds(r, 4)], strip[k])
        dhidden = dact * sig * (1.0 + hidden * (1.0 - sig))
        fines[g] = dhidden.astype(BF)
        tall = dhidden[0] + dhidden[1] + dhidden[2] + dhidden[3]
        for h in range(ch // 128):
            pooled[...] = tall[:, 128 * h : 128 * h + 128]
            every = [pooled[pl.ds(k, cols, stride=width // cols), :] for k in range(width // cols)]
            gc[g, h] = functools.reduce(jnp.add, every).astype(BF)
        copies.append(pltpu.make_async_copy(fines.at[g], gf.at[pl.ds(r, 4)], sems.at[g]))
        copies[-1].start()
    for c in copies:
        c.wait()


def finish_kernel(norm, zs, spots, n, *refs):
    pieces, parts = refs[: len(spots)], refs[len(spots) : len(spots) + n]
    if n:
        out, coarse_out, scratch, sems, coarse, coarse_sem = refs[-6:]
    else:
        out, scratch, sems = refs[-3:]
    core, plane, me = place()
    planes = lax.axis_size("row") // 2
    ch = out.shape[1]
    half = ch // 2
    tall = ch // planes
    step = tall // zs
    z = lax.rem(me, zs)
    copies = []
    for k, (flip, s, first) in enumerate(spots):
        part = core ^ flip
        lanes = pl.ds(pl.multiple_of(part * half, half), half)
        for c in range(pieces[k].shape[0]):
            x = pieces[k][c].astype(F32) * norm
            for t in range(9):
                scratch[k, c, t] = x[t * step : (t + 1) * step]
            b = pl.multiple_of((plane ^ s) * tall + ((first + c) ^ z) * step, step)
            span = pl.ds(b, step)
            taps = pl.ds(part * 5, 4)
            pairs = (
                (scratch.at[k, c, :4], out.at[taps, span, :half]),
                (scratch.at[k, c, 4:8], out.at[taps, span, half:]),
                (scratch.at[k, c, 8], out.at[4, span, lanes]),
            )
            for i, pair in enumerate(pairs):
                copies.append(pltpu.make_async_copy(*pair, sems.at[k, c, i]))
                copies[-1].start()
    if n:
        cr = coarse.shape[0]
        cols = coarse.shape[1] // n
        for s in range(n):
            start = pl.multiple_of((me ^ s) * cols, cols)
            for j in range(cr):
                for h in range(2):
                    b = (j * 2 + h) * cols
                    coarse[j, pl.ds(start, cols), pl.ds(h * half, half)] = parts[s][b : b + cols]
        copies.append(pltpu.make_async_copy(coarse, coarse_out, coarse_sem.at[0]))
        copies[-1].start()
    for c in copies:
        c.wait()


def xor_pairs(count, bit):
    return [(i, i ^ bit) for i in range(count)]


def per_device(fine_input, coarse_feat, conv_weight, step_scale, timesteps, cotangent):
    _, rows, width, ch = fine_input.shape
    n = lax.axis_size("col")
    nrow = lax.axis_size("row")
    planes = nrow // 2
    cr = coarse_feat.shape[1]
    cols = width // 4
    fine, cot, coarse = fine_input[0], cotangent[0], coarse_feat[0]
    weight = conv_weight.reshape(9, ch, ch)

    def shape(*dims, dtype=BF):
        return jax.ShapeDtypeStruct(dims, dtype)

    def col_swap(x, s):
        return lax.ppermute(x, "col", xor_pairs(n, s))

    blocks = pl.pallas_call(
        functools.partial(start_kernel, n),
        out_shape=[shape(cr * cols + (rows if s and is_edge(s) else 0), ch) for s in range(n)],
        in_specs=[hbm(), hbm()],
        out_specs=[vmem()] * n,
        scratch_shapes=[
            pltpu.VMEM(coarse.shape, BF),
            pltpu.VMEM((rows, 16, ch), BF),
            pltpu.VMEM((rows, 16, ch), BF),
            pltpu.SemaphoreType.DMA((3,)),
        ],
        compiler_params=params(START_MIB),
        cost_estimate=cost(1 << 31, 4 << 20),
        name="start",
    )(cot, coarse)
    blocks = list(blocks)
    moved, scale = pl.pallas_call(
        load_kernel,
        out_shape=[shape(3, rows + 2, width, ch), shape(1, ch, dtype=F32)],
        in_specs=[smem(), vmem(), vmem()],
        out_specs=[vmem()] * 2,
        compiler_params=params(4),
        cost_estimate=cost(1 << 20, 4 << 20),
        name="load",
    )(timesteps, cot, step_scale)

    shifts = [s for s in range(n - 1, 0, -1) if is_edge(s)]
    for s in shifts + [s for s in range(1, n) if not is_edge(s)]:
        blocks[s] = col_swap(blocks[s], s)

    halo, side = shape(width + 16, ch), shape(rows, ch, dtype=F32)
    one, two, left, right = pl.pallas_call(
        functools.partial(edge_kernel, cr * cols, shifts),
        out_shape=[halo, halo, side, side],
        in_specs=[vmem()] * (2 + len(shifts)),
        out_specs=[vmem()] * 4,
        compiler_params=params(4),
        cost_estimate=cost(1 << 18, 1 << 19),
        name="edges",
    )(scale, moved, *[blocks[s] for s in shifts])
    odd = range(1, nrow, 2)
    two = lax.ppermute(
        two, "row", [(i, (i + 1) % nrow) for i in odd] + [((i + 1) % nrow, i) for i in odd]
    )
    one = lax.ppermute(one, "row", xor_pairs(nrow, 1))

    groups = rows // 4
    moved, act_t, strip, sums = pl.pallas_call(
        functools.partial(prepare_kernel, n, cr),
        out_shape=[
            shape(*moved.shape),
            shape(ch, rows * width),
            shape(groups, cols, ch),
            shape(5, ch, ch, dtype=F32),
        ],
        in_specs=[vmem()] * (4 + n),
        out_specs=[vmem()] * 4,
        input_output_aliases={3: 0},
        scratch_shapes=[pltpu.VMEM((groups, width, ch), F32)],
        compiler_params=params(12),
        cost_estimate=cost(1 << 32, 4 << 20),
        name="prepare",
    )(fine, left, right, moved, *blocks)

    halves = n // 2
    aligned = ch // (planes * halves) % 16 == 0
    zs = halves if aligned else 1
    depth = 9 * ch // (planes * zs)
    half = ch // 2
    part = shape(planes, zs, depth, half)
    send, rest, moved = pl.pallas_call(
        other_kernel,
        out_shape=[part, shape(ch, half, dtype=F32), shape(*moved.shape)],
        in_specs=[vmem()] * 5,
        out_specs=[vmem()] * 3,
        input_output_aliases={4: 2},
        compiler_params=params(8),
        cost_estimate=cost(9 * rows * width * ch * ch // 4, 8 << 20),
        name="weight_other",
    )(act_t, two, one, sums, moved)
    keep = pl.pallas_call(
        mine_kernel,
        out_shape=part,
        in_specs=[vmem()] * 3,
        out_specs=vmem(),
        compiler_params=params(8),
        cost_estimate=cost(8 * rows * width * ch * ch, 8 << 20),
        name="weight_mine",
    )(act_t, rest, moved)

    done, pooled, made = [], [], 0

    def input_piece(size, after):
        nonlocal done, made
        *done, gc = pl.pallas_call(
            functools.partial(input_kernel, made, size, n),
            out_shape=[shape(rows, width, ch), shape(size, 2, cols, ch // 2)],
            in_specs=[pl.BlockSpec(memory_space=pl.ANY)]
            + [vmem()] * 4
            + [pl.BlockSpec(memory_space=pl.ANY) for _ in done],
            out_specs=[pl.BlockSpec(memory_space=pl.ANY), vmem()],
            input_output_aliases={5: 0} if done else {},
            scratch_shapes=[
                pltpu.VMEM((size, 4, width, ch), BF),
                pltpu.VMEM((width, 128), F32),
                pltpu.SemaphoreType.DMA((size,)),
            ],
            compiler_params=params(12),
            cost_estimate=cost(2 * 9 * 4 * size * width * ch * ch, 4 << 20),
            name="input_grad",
        )(after, moved, fine, strip, weight, *done)
        pooled.append(gc)
        made += size

    def beside(got, size, after):
        nonlocal done, pooled
        if size:
            input_piece(size, after)
            got, done, pooled = lax.optimization_barrier((got, done, pooled))
        return got

    def pooled_strip(s):
        at = strip_order(n).index(s) * cr
        groups_done = [x[g] for x in pooled for g in range(x.shape[0])]
        return jnp.concatenate([x.reshape(-1, ch // 2) for x in groups_done[at : at + cr]])

    def add(*terms):
        return functools.reduce(jnp.add, [t.astype(F32) for t in terms]).astype(BF)

    def core_swap(x):
        return lax.ppermute(x, "row", xor_pairs(nrow, 1))

    def plane_swap(x, s):
        return lax.ppermute(x, "row", xor_pairs(nrow, 2 * s))

    held = {s: [] for s in range(n)}

    def hop(bit):
        sent = []
        for s in [s for s in held if s & bit]:
            sent += [(s, src, x) for src, x in held.pop(s) + [(0, pooled_strip(s))]]
        return sent, col_swap(jnp.concatenate([x for _, _, x in sent]), bit)

    def land(bit, sent, got):
        at = 0
        for s, src, x in sent:
            held[s ^ bit].append((src ^ bit, got[at : at + x.shape[0]]))
            at += x.shape[0]

    sizes = piece_sizes(rows // 4)
    total = add(keep, core_swap(send))
    got = [plane_swap(total[s], s) for s in range(1, planes)]
    total = add(total[0], *beside(got, sizes[0], total))
    if not aligned:
        order = jnp.arange(halves) ^ (lax.axis_index("col") % halves)
        total = total.reshape(halves, depth // halves, half)[order]
    bit = halves // 2
    while bit:
        got = [col_swap(total[bit:], bit)]
        if bit == halves // 2:
            sent, far = hop(halves)
        total = add(total[:bit], *beside(got, sizes[1] if bit == 1 else 0, total))
        bit //= 2
    got = [col_swap(total, halves)]
    land(halves, sent, far)
    bit = halves // 2
    while bit:
        sent, near_rows = hop(bit)
        land(bit, sent, near_rows)
        bit //= 2
    got = beside(got, sizes[2], total)
    places = [src for src, _ in held[0]]
    got, strips = lax.optimization_barrier((got, [x for _, x in held[0]]))
    strips = list(zip(places, strips))
    total = add(total, *got)

    bit = 1
    while bit < halves // 2:
        total = jnp.concatenate([total, col_swap(total, bit)])
        bit *= 2
    came = col_swap(total, bit)
    if aligned:
        waves = [total, came]
    else:
        total = jnp.concatenate([total, came])
        waves = [total[order].reshape(1, depth, half)]
    ways = list(range(1, planes))
    waves = [[x] + [plane_swap(x, s) for s in ways] for x in waves]
    if aligned:
        waves[0][1:], waves[1][:2] = lax.optimization_barrier((waves[0][1:], waves[1][:2]))

    parts = strips + [(0, pooled_strip(0))]
    parts = [x for _, x in sorted(parts, key=lambda pair: pair[0])]
    pixels = rows * nrow * width * n

    def finish(out, pieces, spots, parts=()):
        coarse = [shape(cr, n * cols, ch)] if parts else []
        count, tall = len(pieces), pieces[0].shape[0]
        return pl.pallas_call(
            functools.partial(finish_kernel, float(pixels) ** -0.5, zs, spots, len(parts)),
            out_shape=[shape(9, ch, ch, dtype=F32)] + coarse,
            in_specs=[vmem()] * (count + len(parts)) + [hbm() for _ in out],
            out_specs=[hbm()] + [hbm() for _ in coarse],
            input_output_aliases={count + len(parts): 0} if out else {},
            scratch_shapes=[
                pltpu.VMEM((count, tall, 9, depth // 9, half), F32),
                pltpu.SemaphoreType.DMA((count, tall, 3)),
            ]
            + [x for c in coarse for x in (pltpu.VMEM(c.shape, BF), pltpu.SemaphoreType.DMA((1,)))],
            compiler_params=params(8),
            cost_estimate=cost(1 << 20, 4 << 20),
            name="finish",
        )(*pieces, *parts, *out)

    out, others, spots = [], [], ()
    for k, wave in enumerate(waves):
        if k:
            wave[1:], out = lax.optimization_barrier((wave[1:], out))
        swapped = core_swap(jnp.stack(wave))
        here = [(s, k * wave[0].shape[0]) for s in [0] + ways]
        places = [(0, *spot) for spot in here] + [(1, *spot) for spot in spots]
        out = finish(out, wave + others, tuple(places))
        others, spots = [swapped[i] for i in range(len(wave))], here
    grad_weight, grad_coarse = finish(out, others, tuple((1, *spot) for spot in spots), parts)
    return (done[0][None], grad_coarse[None], grad_weight.reshape(3, 3, ch, ch))


def piece_sizes(groups):
    sizes = [groups * 3 // 4, groups // 8]
    return sizes + [groups - sum(sizes)]


def solution(mesh):
    return jax.shard_map(
        per_device,
        mesh=mesh,
        in_specs=(
            P(None, "row", "col", None),
            P(None, ("row", "col"), None, None),
            P(),
            P(),
            P(),
            P(None, "row", "col", None),
        ),
        out_specs=(P(None, "row", "col", None), P(None, ("row", "col"), None, None), P()),
        check_vma=False,
    )
```

```python
import functools
import jax
import jax.numpy as jnp
from jax import lax
from jax.experimental import pallas as pl
from jax.experimental.pallas import tpu as pltpu
from jax.sharding import PartitionSpec as P

BF = jnp.bfloat16
F32 = jnp.float32
MB = 1024 * 1024
START_MIB = 53.7


def smem():
    return pl.BlockSpec(memory_space=pltpu.SMEM)


def vmem():
    return pl.BlockSpec(memory_space=pltpu.VMEM)


def params(mib):
    return pltpu.CompilerParams(vmem_limit_bytes=int(mib * MB))


def cost(flops, nbytes):
    return pl.CostEstimate(flops=flops, bytes_accessed=nbytes, transcendentals=0)


def hbm():
    return pl.BlockSpec(memory_space=pltpu.HBM)


def place():
    row = lax.axis_index("row")
    return lax.rem(row, 2), row // 2, lax.axis_index("col")


def is_edge(s):
    return s & (s + 1) == 0


def start_kernel(n, cot, coarse, *refs):
    outs, (rough, low, high, sems) = refs[:n], refs[n:]
    _, _, me = place()
    cr, _, ch = rough.shape
    rows, width, _ = cot.shape
    cols = rough.shape[1] // n
    pairs = (coarse, rough), (cot.at[:, :16, :], low), (cot.at[:, width - 16 :, :], high)
    copies = [pltpu.make_async_copy(*pair, sems.at[k]) for k, pair in enumerate(pairs)]
    for c in copies:
        c.start()
    copies[0].wait()
    for s, out in enumerate(outs):
        start = pl.multiple_of((me ^ s) * cols, cols)
        for j in range(cr):
            out[j * cols : (j + 1) * cols, :] = rough[j, pl.ds(start, cols), :]
    r = lax.broadcasted_iota(jnp.int32, (rows, rows * 16), 0)
    p = lax.broadcasted_iota(jnp.int32, (rows, rows * 16), 1)
    sides = []
    for c, edge, pick in ((copies[1], low, 0), (copies[2], high, 15)):
        c.wait()
        sel = jnp.where(p == r * 16 + pick, 1.0, 0.0).astype(BF)
        flat = edge[...].reshape(rows * 16, ch)
        sides.append(jnp.dot(sel, flat, preferred_element_type=F32))
    for s in range(1, n):
        if is_edge(s):
            col = jnp.where((me ^ s) > me, sides[1], sides[0])
            outs[s][cr * cols :, :] = col.astype(BF)


def load_kernel(steps, cot, scales, moved, scale):
    rows, width, ch = cot.shape
    by = scales[pl.ds(steps[0], 1), :]
    scale[...] = by
    zero = jnp.zeros((1, ch), F32)

    def group(g, _):
        for q in range(4):
            r = g * 4 + q
            spread(moved, r + 1, (cot[r].astype(F32) * by).astype(BF), zero, zero)
        return 0

    lax.fori_loop(0, rows // 4, group, 0)


def edge_kernel(offset, shifts, scale, moved, *refs):
    blocks, (one, two, left, right) = refs[: len(shifts)], refs[len(shifts) :]
    core, _, me = place()
    _, rows, width, ch = moved.shape
    rows -= 2
    by = scale[...]
    for side, place_of in ((left, me - 1), (right, me + 1)):
        col = jnp.zeros((rows, ch), F32)
        for s, block in zip(shifts, blocks):
            edge = (block[offset:, :].astype(F32) * by).astype(BF).astype(F32)
            col = jnp.where((me ^ s) == place_of, edge, col)
        side[...] = col
    idx = lax.broadcasted_iota(jnp.int32, (16, ch), 0)
    ends = []
    for k in (0, rows - 1):
        tip = jnp.where(idx == 1, right[k : k + 1, :], 0.0)
        tip = jnp.where(idx == 0, left[k : k + 1, :], tip)
        ends.append((moved[1, k + 1].astype(F32), tip))
    (top, top_tip), (bottom, bottom_tip) = ends
    for out, first in ((one, core == 1), (two, core == 0)):
        out[:width, :] = jnp.where(first, top, bottom).astype(BF)
        out[width:, :] = jnp.where(first, top_tip, bottom_tip).astype(BF)


def spread_up(coarse_row, width):
    cols = coarse_row.shape[0]
    a = lax.broadcasted_iota(jnp.int32, (width, cols), 0)
    b = lax.broadcasted_iota(jnp.int32, (width, cols), 1)
    up = jnp.where(a // (width // cols) == b, 1.0, 0.0).astype(BF)
    return jnp.dot(up, coarse_row, preferred_element_type=F32)


def sigmoid(x):
    return 0.5 * jnp.tanh(0.5 * x) + 0.5


def gate(fine, coarse_row):
    hidden = fine.astype(F32) + spread_up(coarse_row, fine.shape[1])[None]
    return hidden, sigmoid(hidden)


def spread(moved, slot, rounded, left, right):
    width = rounded.shape[0]
    row = rounded.astype(F32)
    idx = lax.broadcasted_iota(jnp.int32, row.shape, 0)
    moved[0, slot] = jnp.where(idx == 0, left, pltpu.roll(row, 1, 0)).astype(BF)
    moved[1, slot] = rounded
    moved[2, slot] = jnp.where(idx == width - 1, right, pltpu.roll(row, width - 1, 0)).astype(BF)


def prepare_kernel(n, cr, fine, left, right, moved_in, *refs):
    blocks, (moved, act_t, strip, sums, up) = refs[:n], refs[n:]
    core, _, me = place()
    rows, width, ch = fine.shape
    cols = strip.shape[1]
    for s in range(n):
        for j in range(cr):
            strip[(me ^ s) * cr + j] = blocks[s][j * cols : (j + 1) * cols, :]
    idx = lax.broadcasted_iota(jnp.int32, (16, ch), 0)

    def patch(r, _):
        for k, low, pick, side in ((0, 0, 0, left), (2, width - 16, 15, right)):
            tile = moved[k, r + 1, low : low + 16, :].astype(F32)
            tile = jnp.where(idx == pick, side[pl.ds(r, 1), :], tile)
            moved[k, r + 1, low : low + 16, :] = tile.astype(BF)
        return 0

    lax.fori_loop(0, rows, patch, 0, unroll=8)
    last = rows // 4 - 1

    def build(g):
        up[g] = spread_up(strip[g], width)
        for r in range(4 * g, 4 * g + 4):
            hidden = fine[r].astype(F32) + up[g]
            act = (hidden * sigmoid(hidden)).astype(BF)
            act_t[:, r * width : (r + 1) * width] = act.T

    def share(g):
        for k in range(5):
            got = partial_tap(1 - core, k, 4 * g, 4, act_t, moved)
            sums[k] = got if g == 1 else sums[k] + got

    build(1)
    for g in range(1, last):
        build(g + 1 if g + 1 < last else 0)
        share(g)
    build(last)


def partial_tap(part, k, row, tall, act_t, moved):
    _, _, width, ch = moved.shape
    lhs = act_t[:, row * width : (row + tall) * width]
    t = 4 if isinstance(k, int) and k == 4 else part * 5 + k
    window = moved[2 - lax.rem(t, 3), pl.ds(2 - t // 3 + row, tall)]
    return jnp.dot(lhs, window.reshape(tall * width, ch), preferred_element_type=F32)


def weight_taps(part, act_t, moved, out, sums):
    _, plane, z = place()
    planes, zs, depth, half = out.shape
    rows = moved.shape[1] - 2
    ch = 2 * half
    step = ch // (planes * zs)
    z = lax.rem(z, zs)

    def put(unit, acc):
        at = pl.multiple_of(unit * step, step)
        for p in range(planes):
            for c in range(zs):
                b = (p * zs + c) * step
                out[p ^ plane, c ^ z, pl.ds(at, step), :] = acc[b : b + step].astype(BF)

    def total(k):
        if sums is None:
            return partial_tap(part, k, 0, rows, act_t, moved)
        first = partial_tap(part, k, 0, 4, act_t, moved)
        return sums[k] + first + partial_tap(part, k, rows - 4, 4, act_t, moved)

    def tap(k, _):
        acc = total(k)
        put(k, acc[:, :half])
        put(k + 4, acc[:, half:])
        return 0

    lax.fori_loop(0, 4, tap, 0, unroll=True)
    return put, total


def other_kernel(act_t, two, one, sums, moved_in, out, rest, moved):
    core, _, _ = place()
    _, rows, width, ch = moved.shape
    row = lax.axis_index("row")
    outer = (row == 0) | (row == lax.axis_size("row") - 1)
    next_chip = jnp.where(outer, 0.0, two[...].astype(F32))
    for slot, first in ((0, core == 1), (rows - 1, core == 0)):
        halo = jnp.where(first, one[...].astype(F32), next_chip)
        left, right = halo[width : width + 1], halo[width + 1 : width + 2]
        spread(moved, slot, halo[:width].astype(BF), left, right)
    put, total = weight_taps(1 - core, act_t, moved, out, sums)
    middle = total(4)
    low, high = middle[:, : ch // 2], middle[:, ch // 2 :]
    put(8, jnp.where(core == 1, low, high))
    rest[...] = jnp.where(core == 1, high, low)


def mine_kernel(act_t, rest, moved, out):
    core, _, _ = place()
    put, _ = weight_taps(core, act_t, moved, out, None)
    put(8, rest[...])


def strip_order(n):
    return list(range(n - 1, -1, -1))


def input_kernel(first, size, n, after, moved, fine, strip, weight, *refs):
    gf, gc, fines, pooled, sems = refs[-5:]
    _, _, me = place()
    cr = strip.shape[0] // n
    _, width, ch = fine.shape
    cols = strip.shape[1]
    wide = jnp.concatenate([weight[t] for t in range(9)], axis=1)
    copies = []
    for g in range(size):
        k = (strip_order(n)[(first + g) // cr] ^ me) * cr + (first + g) % cr
        r = 4 * k
        taps = [
            moved[2 - t % 3, pl.ds(2 - t // 3 + r, 4)].reshape(4 * width, ch) for t in range(9)
        ]
        dact = lax.dot_general(
            jnp.concatenate(taps, axis=1),
            wide,
            (((1,), (1,)), ((), ())),
            preferred_element_type=F32,
        ).reshape(4, width, ch)
        hidden, sig = gate(fine[pl.ds(r, 4)], strip[k])
        dhidden = dact * sig * (1.0 + hidden * (1.0 - sig))
        fines[g] = dhidden.astype(BF)
        tall = dhidden[0] + dhidden[1] + dhidden[2] + dhidden[3]
        for h in range(ch // 128):
            pooled[...] = tall[:, 128 * h : 128 * h + 128]
            every = [pooled[pl.ds(k, cols, stride=width // cols), :] for k in range(width // cols)]
            gc[g, h] = functools.reduce(jnp.add, every).astype(BF)
        copies.append(pltpu.make_async_copy(fines.at[g], gf.at[pl.ds(r, 4)], sems.at[g]))
        copies[-1].start()
    for c in copies:
        c.wait()


def finish_kernel(norm, zs, spots, n, *refs):
    pieces, parts = refs[: len(spots)], refs[len(spots) : len(spots) + n]
    if n:
        out, coarse_out, scratch, sems, coarse, coarse_sem = refs[-6:]
    else:
        out, scratch, sems = refs[-3:]
    core, plane, me = place()
    planes = lax.axis_size("row") // 2
    ch = out.shape[1]
    half = ch // 2
    tall = ch // planes
    step = tall // zs
    z = lax.rem(me, zs)
    copies = []
    for k, (flip, s, first) in enumerate(spots):
        part = core ^ flip
        lanes = pl.ds(pl.multiple_of(part * half, half), half)
        for c in range(pieces[k].shape[0]):
            x = pieces[k][c].astype(F32) * norm
            for t in range(9):
                scratch[k, c, t] = x[t * step : (t + 1) * step]
            b = pl.multiple_of((plane ^ s) * tall + ((first + c) ^ z) * step, step)
            span = pl.ds(b, step)
            taps = pl.ds(part * 5, 4)
            pairs = (
                (scratch.at[k, c, :4], out.at[taps, span, :half]),
                (scratch.at[k, c, 4:8], out.at[taps, span, half:]),
                (scratch.at[k, c, 8], out.at[4, span, lanes]),
            )
            for i, pair in enumerate(pairs):
                copies.append(pltpu.make_async_copy(*pair, sems.at[k, c, i]))
                copies[-1].start()
    if n:
        cr = coarse.shape[0]
        cols = coarse.shape[1] // n
        for s in range(n):
            start = pl.multiple_of((me ^ s) * cols, cols)
            for j in range(cr):
                for h in range(2):
                    b = (j * 2 + h) * cols
                    coarse[j, pl.ds(start, cols), pl.ds(h * half, half)] = parts[s][b : b + cols]
        copies.append(pltpu.make_async_copy(coarse, coarse_out, coarse_sem.at[0]))
        copies[-1].start()
    for c in copies:
        c.wait()


def xor_pairs(count, bit):
    return [(i, i ^ bit) for i in range(count)]


def per_device(fine_input, coarse_feat, conv_weight, step_scale, timesteps, cotangent):
    _, rows, width, ch = fine_input.shape
    n = lax.axis_size("col")
    nrow = lax.axis_size("row")
    planes = nrow // 2
    cr = coarse_feat.shape[1]
    cols = width // 4
    fine, cot, coarse = fine_input[0], cotangent[0], coarse_feat[0]
    weight = conv_weight.reshape(9, ch, ch)

    def shape(*dims, dtype=BF):
        return jax.ShapeDtypeStruct(dims, dtype)

    def col_swap(x, s):
        return lax.ppermute(x, "col", xor_pairs(n, s))

    blocks = pl.pallas_call(
        functools.partial(start_kernel, n),
        out_shape=[shape(cr * cols + (rows if s and is_edge(s) else 0), ch) for s in range(n)],
        in_specs=[hbm(), hbm()],
        out_specs=[vmem()] * n,
        scratch_shapes=[
            pltpu.VMEM(coarse.shape, BF),
            pltpu.VMEM((rows, 16, ch), BF),
            pltpu.VMEM((rows, 16, ch), BF),
            pltpu.SemaphoreType.DMA((3,)),
        ],
        compiler_params=params(START_MIB),
        cost_estimate=cost(1 << 31, 4 << 20),
        name="start",
    )(cot, coarse)
    blocks = list(blocks)
    moved, scale = pl.pallas_call(
        load_kernel,
        out_shape=[shape(3, rows + 2, width, ch), shape(1, ch, dtype=F32)],
        in_specs=[smem(), vmem(), vmem()],
        out_specs=[vmem()] * 2,
        compiler_params=params(4),
        cost_estimate=cost(1 << 20, 4 << 20),
        name="load",
    )(timesteps, cot, step_scale)

    shifts = [s for s in range(n - 1, 0, -1) if is_edge(s)]
    for s in shifts + [s for s in range(1, n) if not is_edge(s)]:
        blocks[s] = col_swap(blocks[s], s)

    halo, side = shape(width + 16, ch), shape(rows, ch, dtype=F32)
    one, two, left, right = pl.pallas_call(
        functools.partial(edge_kernel, cr * cols, shifts),
        out_shape=[halo, halo, side, side],
        in_specs=[vmem()] * (2 + len(shifts)),
        out_specs=[vmem()] * 4,
        compiler_params=params(4),
        cost_estimate=cost(1 << 18, 1 << 19),
        name="edges",
    )(scale, moved, *[blocks[s] for s in shifts])
    odd = range(1, nrow, 2)
    two = lax.ppermute(
        two, "row", [(i, (i + 1) % nrow) for i in odd] + [((i + 1) % nrow, i) for i in odd]
    )
    one = lax.ppermute(one, "row", xor_pairs(nrow, 1))

    groups = rows // 4
    moved, act_t, strip, sums = pl.pallas_call(
        functools.partial(prepare_kernel, n, cr),
        out_shape=[
            shape(*moved.shape),
            shape(ch, rows * width),
            shape(groups, cols, ch),
            shape(5, ch, ch, dtype=F32),
        ],
        in_specs=[vmem()] * (4 + n),
        out_specs=[vmem()] * 4,
        input_output_aliases={3: 0},
        scratch_shapes=[pltpu.VMEM((groups, width, ch), F32)],
        compiler_params=params(12),
        cost_estimate=cost(1 << 32, 4 << 20),
        name="prepare",
    )(fine, left, right, moved, *blocks)

    halves = n // 2
    aligned = ch // (planes * halves) % 16 == 0
    zs = halves if aligned else 1
    depth = 9 * ch // (planes * zs)
    half = ch // 2
    part = shape(planes, zs, depth, half)
    send, rest, moved = pl.pallas_call(
        other_kernel,
        out_shape=[part, shape(ch, half, dtype=F32), shape(*moved.shape)],
        in_specs=[vmem()] * 5,
        out_specs=[vmem()] * 3,
        input_output_aliases={4: 2},
        compiler_params=params(8),
        cost_estimate=cost(9 * rows * width * ch * ch // 4, 8 << 20),
        name="weight_other",
    )(act_t, two, one, sums, moved)
    keep = pl.pallas_call(
        mine_kernel,
        out_shape=part,
        in_specs=[vmem()] * 3,
        out_specs=vmem(),
        compiler_params=params(8),
        cost_estimate=cost(8 * rows * width * ch * ch, 8 << 20),
        name="weight_mine",
    )(act_t, rest, moved)

    done, pooled, made = [], [], 0

    def input_piece(size, after):
        nonlocal done, made
        *done, gc = pl.pallas_call(
            functools.partial(input_kernel, made, size, n),
            out_shape=[shape(rows, width, ch), shape(size, 2, cols, ch // 2)],
            in_specs=[pl.BlockSpec(memory_space=pl.ANY)]
            + [vmem()] * 4
            + [pl.BlockSpec(memory_space=pl.ANY) for _ in done],
            out_specs=[pl.BlockSpec(memory_space=pl.ANY), vmem()],
            input_output_aliases={5: 0} if done else {},
            scratch_shapes=[
                pltpu.VMEM((size, 4, width, ch), BF),
                pltpu.VMEM((width, 128), F32),
                pltpu.SemaphoreType.DMA((size,)),
            ],
            compiler_params=params(12),
            cost_estimate=cost(2 * 9 * 4 * size * width * ch * ch, 4 << 20),
            name="input_grad",
        )(after, moved, fine, strip, weight, *done)
        pooled.append(gc)
        made += size

    def beside(got, size, after):
        nonlocal done, pooled
        if size:
            input_piece(size, after)
            got, done, pooled = lax.optimization_barrier((got, done, pooled))
        return got

    def pooled_strip(s):
        at = strip_order(n).index(s) * cr
        groups_done = [x[g] for x in pooled for g in range(x.shape[0])]
        return jnp.concatenate([x.reshape(-1, ch // 2) for x in groups_done[at : at + cr]])

    def add(*terms):
        return functools.reduce(jnp.add, [t.astype(F32) for t in terms]).astype(BF)

    def core_swap(x):
        return lax.ppermute(x, "row", xor_pairs(nrow, 1))

    def plane_swap(x, s):
        return lax.ppermute(x, "row", xor_pairs(nrow, 2 * s))

    held = {s: [] for s in range(n)}

    def hop(bit, extra):
        sent = []
        for s in [s for s in held if s & bit]:
            sent += [(s, src, x) for src, x in held.pop(s) + [(0, pooled_strip(s))]]
        return sent, col_swap(jnp.concatenate(extra + [x for _, _, x in sent]), bit)

    def land(bit, sent, got, at):
        for s, src, x in sent:
            held[s ^ bit].append((src ^ bit, got[at : at + x.shape[0]]))
            at += x.shape[0]

    def ride(bit, total):
        sent, got = hop(bit, [total.reshape(-1, half)])
        at = total.size // half
        land(bit, sent, got, at)
        return got[:at].reshape(total.shape)

    sizes = piece_sizes(rows // 4)
    total = add(keep, core_swap(send))
    got = [plane_swap(total[s], s) for s in range(1, planes)]
    total = add(total[0], *beside(got, sizes[0], total))
    if not aligned:
        order = jnp.arange(halves) ^ (lax.axis_index("col") % halves)
        total = total.reshape(halves, depth // halves, half)[order]
    bit = halves // 2
    while bit:
        got = [col_swap(total[bit:], bit)]
        if bit == halves // 2:
            sent, far = hop(halves, [])
        total = add(total[:bit], *beside(got, sizes[1] if bit == 1 else 0, total))
        bit //= 2
    got = beside([col_swap(total, halves)], sizes[2], total)
    total = add(total, *got)
    land(halves, sent, far, 0)

    bit = 1
    while bit < halves // 2:
        total = jnp.concatenate([total, ride(bit, total)])
        bit *= 2
    came = ride(bit, total)
    if aligned:
        waves = [total, came]
    else:
        total = jnp.concatenate([total, came])
        waves = [total[order].reshape(1, depth, half)]
    ways = list(range(1, planes))
    waves = [[x] + [plane_swap(x, s) for s in ways] for x in waves]
    if aligned:
        waves[0][1:], waves[1][0] = lax.optimization_barrier((waves[0][1:], waves[1][0]))

    parts = held[0] + [(0, pooled_strip(0))]
    parts = [x for _, x in sorted(parts, key=lambda pair: pair[0])]
    pixels = rows * nrow * width * n

    def finish(out, pieces, spots, parts=()):
        coarse = [shape(cr, n * cols, ch)] if parts else []
        count, tall = len(pieces), pieces[0].shape[0]
        return pl.pallas_call(
            functools.partial(finish_kernel, float(pixels) ** -0.5, zs, spots, len(parts)),
            out_shape=[shape(9, ch, ch, dtype=F32)] + coarse,
            in_specs=[vmem()] * (count + len(parts)) + [hbm() for _ in out],
            out_specs=[hbm()] + [hbm() for _ in coarse],
            input_output_aliases={count + len(parts): 0} if out else {},
            scratch_shapes=[
                pltpu.VMEM((count, tall, 9, depth // 9, half), F32),
                pltpu.SemaphoreType.DMA((count, tall, 3)),
            ]
            + [x for c in coarse for x in (pltpu.VMEM(c.shape, BF), pltpu.SemaphoreType.DMA((1,)))],
            compiler_params=params(8),
            cost_estimate=cost(1 << 20, 4 << 20),
            name="finish",
        )(*pieces, *parts, *out)

    out, others, spots = [], [], ()
    for k, wave in enumerate(waves):
        if k:
            wave[1:], out = lax.optimization_barrier((wave[1:], out))
        swapped = core_swap(jnp.stack(wave))
        here = [(s, k * wave[0].shape[0]) for s in [0] + ways]
        places = [(0, *spot) for spot in here] + [(1, *spot) for spot in spots]
        out = finish(out, wave + others, tuple(places))
        others, spots = [swapped[i] for i in range(len(wave))], here
    grad_weight, grad_coarse = finish(out, others, tuple((1, *spot) for spot in spots), parts)
    return (done[0][None], grad_coarse[None], grad_weight.reshape(3, 3, ch, ch))


def piece_sizes(groups):
    sizes = [groups * 3 // 4, groups // 8]
    return sizes + [groups - sum(sizes)]


def solution(mesh):
    return jax.shard_map(
        per_device,
        mesh=mesh,
        in_specs=(
            P(None, "row", "col", None),
            P(None, ("row", "col"), None, None),
            P(),
            P(),
            P(),
            P(None, "row", "col", None),
        ),
        out_specs=(P(None, "row", "col", None), P(None, ("row", "col"), None, None), P()),
        check_vma=False,
    )
```

```python
import functools
import jax
import jax.numpy as jnp
from jax import lax
from jax.experimental import pallas as pl
from jax.experimental.pallas import tpu as pltpu
from jax.sharding import PartitionSpec as P

BF = jnp.bfloat16
F32 = jnp.float32
MB = 1024 * 1024
START_MIB = 53.7


def smem():
    return pl.BlockSpec(memory_space=pltpu.SMEM)


def vmem():
    return pl.BlockSpec(memory_space=pltpu.VMEM)


def params(mib):
    return pltpu.CompilerParams(vmem_limit_bytes=int(mib * MB))


def cost(flops, nbytes):
    return pl.CostEstimate(flops=flops, bytes_accessed=nbytes, transcendentals=0)


def hbm():
    return pl.BlockSpec(memory_space=pltpu.HBM)


def place():
    row = lax.axis_index("row")
    return lax.rem(row, 2), row // 2, lax.axis_index("col")


def is_edge(s):
    return s & (s + 1) == 0


def start_kernel(n, cot, coarse, *refs):
    outs, (rough, low, high, sems) = refs[:n], refs[n:]
    _, _, me = place()
    cr, _, ch = rough.shape
    rows, width, _ = cot.shape
    cols = rough.shape[1] // n
    pairs = (coarse, rough), (cot.at[:, :16, :], low), (cot.at[:, width - 16 :, :], high)
    copies = [pltpu.make_async_copy(*pair, sems.at[k]) for k, pair in enumerate(pairs)]
    for c in copies:
        c.start()
    copies[0].wait()
    for s, out in enumerate(outs):
        start = pl.multiple_of((me ^ s) * cols, cols)
        for j in range(cr):
            out[j * cols : (j + 1) * cols, :] = rough[j, pl.ds(start, cols), :]
    r = lax.broadcasted_iota(jnp.int32, (rows, rows * 16), 0)
    p = lax.broadcasted_iota(jnp.int32, (rows, rows * 16), 1)
    sides = []
    for c, edge, pick in ((copies[1], low, 0), (copies[2], high, 15)):
        c.wait()
        sel = jnp.where(p == r * 16 + pick, 1.0, 0.0).astype(BF)
        flat = edge[...].reshape(rows * 16, ch)
        sides.append(jnp.dot(sel, flat, preferred_element_type=F32))
    for s in range(1, n):
        if is_edge(s):
            col = jnp.where((me ^ s) > me, sides[1], sides[0])
            outs[s][cr * cols :, :] = col.astype(BF)


def load_kernel(steps, cot, scales, moved, scale):
    rows, width, ch = cot.shape
    by = scales[pl.ds(steps[0], 1), :]
    scale[...] = by
    zero = jnp.zeros((1, ch), F32)

    def group(g, _):
        for q in range(4):
            r = g * 4 + q
            spread(moved, r + 1, (cot[r].astype(F32) * by).astype(BF), zero, zero)
        return 0

    lax.fori_loop(0, rows // 4, group, 0, unroll=True)


def edge_kernel(offset, shifts, scale, moved, *refs):
    blocks, (one, two, left, right) = refs[: len(shifts)], refs[len(shifts) :]
    core, _, me = place()
    _, rows, width, ch = moved.shape
    rows -= 2
    by = scale[...]
    for side, place_of in ((left, me - 1), (right, me + 1)):
        col = jnp.zeros((rows, ch), F32)
        for s, block in zip(shifts, blocks):
            edge = (block[offset:, :].astype(F32) * by).astype(BF).astype(F32)
            col = jnp.where((me ^ s) == place_of, edge, col)
        side[...] = col
    idx = lax.broadcasted_iota(jnp.int32, (16, ch), 0)
    ends = []
    for k in (0, rows - 1):
        tip = jnp.where(idx == 1, right[k : k + 1, :], 0.0)
        tip = jnp.where(idx == 0, left[k : k + 1, :], tip)
        ends.append((moved[1, k + 1].astype(F32), tip))
    (top, top_tip), (bottom, bottom_tip) = ends
    for out, first in ((one, core == 1), (two, core == 0)):
        out[:width, :] = jnp.where(first, top, bottom).astype(BF)
        out[width:, :] = jnp.where(first, top_tip, bottom_tip).astype(BF)


def spread_up(coarse_row, width):
    cols = coarse_row.shape[0]
    a = lax.broadcasted_iota(jnp.int32, (width, cols), 0)
    b = lax.broadcasted_iota(jnp.int32, (width, cols), 1)
    up = jnp.where(a // (width // cols) == b, 1.0, 0.0).astype(BF)
    return jnp.dot(up, coarse_row, preferred_element_type=F32)


def sigmoid(x):
    return 0.5 * jnp.tanh(0.5 * x) + 0.5


def gate(fine, coarse_row):
    hidden = fine.astype(F32) + spread_up(coarse_row, fine.shape[1])[None]
    return hidden, sigmoid(hidden)


def spread(moved, slot, rounded, left, right):
    width = rounded.shape[0]
    row = rounded.astype(F32)
    idx = lax.broadcasted_iota(jnp.int32, row.shape, 0)
    moved[0, slot] = jnp.where(idx == 0, left, pltpu.roll(row, 1, 0)).astype(BF)
    moved[1, slot] = rounded
    moved[2, slot] = jnp.where(idx == width - 1, right, pltpu.roll(row, width - 1, 0)).astype(BF)


def prepare_kernel(n, cr, fine, left, right, moved_in, *refs):
    blocks, (moved, act_t, strip, sums, up) = refs[:n], refs[n:]
    core, _, me = place()
    rows, width, ch = fine.shape
    cols = strip.shape[1]
    for s in range(n):
        for j in range(cr):
            strip[(me ^ s) * cr + j] = blocks[s][j * cols : (j + 1) * cols, :]
    idx = lax.broadcasted_iota(jnp.int32, (16, ch), 0)

    def patch(r, _):
        for k, low, pick, side in ((0, 0, 0, left), (2, width - 16, 15, right)):
            tile = moved[k, r + 1, low : low + 16, :].astype(F32)
            tile = jnp.where(idx == pick, side[pl.ds(r, 1), :], tile)
            moved[k, r + 1, low : low + 16, :] = tile.astype(BF)
        return 0

    lax.fori_loop(0, rows, patch, 0, unroll=True)
    last = rows // 4 - 1

    def build(g):
        up[g] = spread_up(strip[g], width)
        for r in range(4 * g, 4 * g + 4):
            hidden = fine[r].astype(F32) + up[g]
            act = (hidden * sigmoid(hidden)).astype(BF)
            act_t[:, r * width : (r + 1) * width] = act.T

    def share(g):
        for k in range(5):
            got = partial_tap(1 - core, k, 4 * g, 4, act_t, moved)
            sums[k] = got if g == 1 else sums[k] + got

    build(1)
    for g in range(1, last):
        build(g + 1 if g + 1 < last else 0)
        share(g)
    build(last)


def partial_tap(part, k, row, tall, act_t, moved):
    _, _, width, ch = moved.shape
    lhs = act_t[:, row * width : (row + tall) * width]
    t = 4 if isinstance(k, int) and k == 4 else part * 5 + k
    window = moved[2 - lax.rem(t, 3), pl.ds(2 - t // 3 + row, tall)]
    return jnp.dot(lhs, window.reshape(tall * width, ch), preferred_element_type=F32)


def weight_taps(part, act_t, moved, out, sums):
    _, plane, z = place()
    planes, zs, depth, half = out.shape
    rows = moved.shape[1] - 2
    ch = 2 * half
    step = ch // (planes * zs)
    z = lax.rem(z, zs)

    def put(unit, acc):
        at = pl.multiple_of(unit * step, step)
        for p in range(planes):
            for c in range(zs):
                b = (p * zs + c) * step
                out[p ^ plane, c ^ z, pl.ds(at, step), :] = acc[b : b + step].astype(BF)

    def total(k):
        if sums is None:
            return partial_tap(part, k, 0, rows, act_t, moved)
        first = partial_tap(part, k, 0, 4, act_t, moved)
        return sums[k] + first + partial_tap(part, k, rows - 4, 4, act_t, moved)

    def tap(k, _):
        acc = total(k)
        put(k, acc[:, :half])
        put(k + 4, acc[:, half:])
        return 0

    lax.fori_loop(0, 4, tap, 0, unroll=True)
    return put, total


def other_kernel(act_t, two, one, sums, moved_in, out, rest, moved):
    core, _, _ = place()
    _, rows, width, ch = moved.shape
    row = lax.axis_index("row")
    outer = (row == 0) | (row == lax.axis_size("row") - 1)
    next_chip = jnp.where(outer, 0.0, two[...].astype(F32))
    for slot, first in ((0, core == 1), (rows - 1, core == 0)):
        halo = jnp.where(first, one[...].astype(F32), next_chip)
        left, right = halo[width : width + 1], halo[width + 1 : width + 2]
        spread(moved, slot, halo[:width].astype(BF), left, right)
    put, total = weight_taps(1 - core, act_t, moved, out, sums)
    middle = total(4)
    low, high = middle[:, : ch // 2], middle[:, ch // 2 :]
    put(8, jnp.where(core == 1, low, high))
    rest[...] = jnp.where(core == 1, high, low)


def mine_kernel(act_t, rest, moved, out):
    core, _, _ = place()
    put, _ = weight_taps(core, act_t, moved, out, None)
    put(8, rest[...])


def strip_order(n):
    return list(range(n - 1, -1, -1))


def input_kernel(first, size, n, after, moved, fine, strip, weight, *refs):
    gf, gc, fines, pooled, sems = refs[-5:]
    _, _, me = place()
    cr = strip.shape[0] // n
    _, width, ch = fine.shape
    cols = strip.shape[1]
    wide = jnp.concatenate([weight[t] for t in range(9)], axis=1)
    copies = []
    for g in range(size):
        k = (strip_order(n)[(first + g) // cr] ^ me) * cr + (first + g) % cr
        r = 4 * k
        taps = [
            moved[2 - t % 3, pl.ds(2 - t // 3 + r, 4)].reshape(4 * width, ch) for t in range(9)
        ]
        dact = lax.dot_general(
            jnp.concatenate(taps, axis=1),
            wide,
            (((1,), (1,)), ((), ())),
            preferred_element_type=F32,
        ).reshape(4, width, ch)
        hidden, sig = gate(fine[pl.ds(r, 4)], strip[k])
        dhidden = dact * sig * (1.0 + hidden * (1.0 - sig))
        fines[g] = dhidden.astype(BF)
        tall = dhidden[0] + dhidden[1] + dhidden[2] + dhidden[3]
        for h in range(ch // 128):
            pooled[...] = tall[:, 128 * h : 128 * h + 128]
            every = [pooled[pl.ds(k, cols, stride=width // cols), :] for k in range(width // cols)]
            gc[g, h] = functools.reduce(jnp.add, every).astype(BF)
        copies.append(pltpu.make_async_copy(fines.at[g], gf.at[pl.ds(r, 4)], sems.at[g]))
        copies[-1].start()
    for c in copies:
        c.wait()


def finish_kernel(norm, zs, spots, n, *refs):
    pieces, parts = refs[: len(spots)], refs[len(spots) : len(spots) + n]
    if n:
        out, coarse_out, scratch, sems, coarse, coarse_sem = refs[-6:]
    else:
        out, scratch, sems = refs[-3:]
    core, plane, me = place()
    planes = lax.axis_size("row") // 2
    ch = out.shape[1]
    half = ch // 2
    tall = ch // planes
    step = tall // zs
    z = lax.rem(me, zs)
    copies = []
    for k, (flip, s, first) in enumerate(spots):
        part = core ^ flip
        lanes = pl.ds(pl.multiple_of(part * half, half), half)
        for c in range(pieces[k].shape[0]):
            x = pieces[k][c].astype(F32) * norm
            for t in range(9):
                scratch[k, c, t] = x[t * step : (t + 1) * step]
            b = pl.multiple_of((plane ^ s) * tall + ((first + c) ^ z) * step, step)
            span = pl.ds(b, step)
            taps = pl.ds(part * 5, 4)
            pairs = (
                (scratch.at[k, c, :4], out.at[taps, span, :half]),
                (scratch.at[k, c, 4:8], out.at[taps, span, half:]),
                (scratch.at[k, c, 8], out.at[4, span, lanes]),
            )
            for i, pair in enumerate(pairs):
                copies.append(pltpu.make_async_copy(*pair, sems.at[k, c, i]))
                copies[-1].start()
    if n:
        cr = coarse.shape[0]
        cols = coarse.shape[1] // n
        for s in range(n):
            start = pl.multiple_of((me ^ s) * cols, cols)
            for j in range(cr):
                for h in range(2):
                    b = (j * 2 + h) * cols
                    coarse[j, pl.ds(start, cols), pl.ds(h * half, half)] = parts[s][b : b + cols]
        copies.append(pltpu.make_async_copy(coarse, coarse_out, coarse_sem.at[0]))
        copies[-1].start()
    for c in copies:
        c.wait()


def xor_pairs(count, bit):
    return [(i, i ^ bit) for i in range(count)]


def per_device(fine_input, coarse_feat, conv_weight, step_scale, timesteps, cotangent):
    _, rows, width, ch = fine_input.shape
    n = lax.axis_size("col")
    nrow = lax.axis_size("row")
    planes = nrow // 2
    cr = coarse_feat.shape[1]
    cols = width // 4
    fine, cot, coarse = fine_input[0], cotangent[0], coarse_feat[0]
    weight = conv_weight.reshape(9, ch, ch)

    def shape(*dims, dtype=BF):
        return jax.ShapeDtypeStruct(dims, dtype)

    def col_swap(x, s):
        return lax.ppermute(x, "col", xor_pairs(n, s))

    blocks = pl.pallas_call(
        functools.partial(start_kernel, n),
        out_shape=[shape(cr * cols + (rows if s and is_edge(s) else 0), ch) for s in range(n)],
        in_specs=[hbm(), hbm()],
        out_specs=[vmem()] * n,
        scratch_shapes=[
            pltpu.VMEM(coarse.shape, BF),
            pltpu.VMEM((rows, 16, ch), BF),
            pltpu.VMEM((rows, 16, ch), BF),
            pltpu.SemaphoreType.DMA((3,)),
        ],
        compiler_params=params(START_MIB),
        cost_estimate=cost(1 << 31, 4 << 20),
        name="start",
    )(cot, coarse)
    blocks = list(blocks)
    moved, scale = pl.pallas_call(
        load_kernel,
        out_shape=[shape(3, rows + 2, width, ch), shape(1, ch, dtype=F32)],
        in_specs=[smem(), vmem(), vmem()],
        out_specs=[vmem()] * 2,
        compiler_params=params(4),
        cost_estimate=cost(1 << 20, 4 << 20),
        name="load",
    )(timesteps, cot, step_scale)

    shifts = [s for s in range(n - 1, 0, -1) if is_edge(s)]
    for s in shifts + [s for s in range(1, n) if not is_edge(s)]:
        blocks[s] = col_swap(blocks[s], s)

    halo, side = shape(width + 16, ch), shape(rows, ch, dtype=F32)
    one, two, left, right = pl.pallas_call(
        functools.partial(edge_kernel, cr * cols, shifts),
        out_shape=[halo, halo, side, side],
        in_specs=[vmem()] * (2 + len(shifts)),
        out_specs=[vmem()] * 4,
        compiler_params=params(4),
        cost_estimate=cost(1 << 18, 1 << 19),
        name="edges",
    )(scale, moved, *[blocks[s] for s in shifts])
    odd = range(1, nrow, 2)
    two = lax.ppermute(
        two, "row", [(i, (i + 1) % nrow) for i in odd] + [((i + 1) % nrow, i) for i in odd]
    )
    one = lax.ppermute(one, "row", xor_pairs(nrow, 1))

    groups = rows // 4
    moved, act_t, strip, sums = pl.pallas_call(
        functools.partial(prepare_kernel, n, cr),
        out_shape=[
            shape(*moved.shape),
            shape(ch, rows * width),
            shape(groups, cols, ch),
            shape(5, ch, ch, dtype=F32),
        ],
        in_specs=[vmem()] * (4 + n),
        out_specs=[vmem()] * 4,
        input_output_aliases={3: 0},
        scratch_shapes=[pltpu.VMEM((groups, width, ch), F32)],
        compiler_params=params(12),
        cost_estimate=cost(1 << 32, 4 << 20),
        name="prepare",
    )(fine, left, right, moved, *blocks)

    halves = n // 2
    aligned = ch // (planes * halves) % 16 == 0
    zs = halves if aligned else 1
    depth = 9 * ch // (planes * zs)
    half = ch // 2
    part = shape(planes, zs, depth, half)
    send, rest, moved = pl.pallas_call(
        other_kernel,
        out_shape=[part, shape(ch, half, dtype=F32), shape(*moved.shape)],
        in_specs=[vmem()] * 5,
        out_specs=[vmem()] * 3,
        input_output_aliases={4: 2},
        compiler_params=params(8),
        cost_estimate=cost(9 * rows * width * ch * ch // 4, 8 << 20),
        name="weight_other",
    )(act_t, two, one, sums, moved)
    keep = pl.pallas_call(
        mine_kernel,
        out_shape=part,
        in_specs=[vmem()] * 3,
        out_specs=vmem(),
        compiler_params=params(8),
        cost_estimate=cost(8 * rows * width * ch * ch, 8 << 20),
        name="weight_mine",
    )(act_t, rest, moved)

    done, pooled, made = [], [], 0

    def input_piece(size, after):
        nonlocal done, made
        *done, gc = pl.pallas_call(
            functools.partial(input_kernel, made, size, n),
            out_shape=[shape(rows, width, ch), shape(size, 2, cols, ch // 2)],
            in_specs=[pl.BlockSpec(memory_space=pl.ANY)]
            + [vmem()] * 4
            + [pl.BlockSpec(memory_space=pl.ANY) for _ in done],
            out_specs=[pl.BlockSpec(memory_space=pl.ANY), vmem()],
            input_output_aliases={5: 0} if done else {},
            scratch_shapes=[
                pltpu.VMEM((size, 4, width, ch), BF),
                pltpu.VMEM((width, 128), F32),
                pltpu.SemaphoreType.DMA((size,)),
            ],
            compiler_params=params(12),
            cost_estimate=cost(2 * 9 * 4 * size * width * ch * ch, 4 << 20),
            name="input_grad",
        )(after, moved, fine, strip, weight, *done)
        pooled.append(gc)
        made += size

    def beside(got, size, after):
        nonlocal done, pooled
        if size:
            input_piece(size, after)
            got, done, pooled = lax.optimization_barrier((got, done, pooled))
        return got

    def pooled_strip(s):
        at = strip_order(n).index(s) * cr
        groups_done = [x[g] for x in pooled for g in range(x.shape[0])]
        return jnp.concatenate([x.reshape(-1, ch // 2) for x in groups_done[at : at + cr]])

    def add(*terms):
        return functools.reduce(jnp.add, [t.astype(F32) for t in terms]).astype(BF)

    def core_swap(x):
        return lax.ppermute(x, "row", xor_pairs(nrow, 1))

    def plane_swap(x, s):
        return lax.ppermute(x, "row", xor_pairs(nrow, 2 * s))

    held = {s: [] for s in range(n)}

    def hop(bit, extra):
        sent = []
        for s in [s for s in held if s & bit]:
            sent += [(s, src, x) for src, x in held.pop(s) + [(0, pooled_strip(s))]]
        return sent, col_swap(jnp.concatenate(extra + [x for _, _, x in sent]), bit)

    def land(bit, sent, got, at):
        for s, src, x in sent:
            held[s ^ bit].append((src ^ bit, got[at : at + x.shape[0]]))
            at += x.shape[0]

    def ride(bit, total):
        sent, got = hop(bit, [total.reshape(-1, half)])
        at = total.size // half
        land(bit, sent, got, at)
        return got[:at].reshape(total.shape)

    sizes = piece_sizes(rows // 4)
    total = add(keep, core_swap(send))
    got = [plane_swap(total[s], s) for s in range(1, planes)]
    total = add(total[0], *beside(got, sizes[0], total))
    if not aligned:
        order = jnp.arange(halves) ^ (lax.axis_index("col") % halves)
        total = total.reshape(halves, depth // halves, half)[order]
    bit = halves // 2
    while bit:
        got = [col_swap(total[bit:], bit)]
        if bit == halves // 2:
            sent, far = hop(halves, [])
        total = add(total[:bit], *beside(got, sizes[1] if bit == 1 else 0, total))
        bit //= 2
    got = beside([col_swap(total, halves)], sizes[2], total)
    total = add(total, *got)
    land(halves, sent, far, 0)

    bit = 1
    while bit < halves // 2:
        total = jnp.concatenate([total, ride(bit, total)])
        bit *= 2
    came = ride(bit, total)
    if aligned:
        waves = [total, came]
    else:
        total = jnp.concatenate([total, came])
        waves = [total[order].reshape(1, depth, half)]
    ways = list(range(1, planes))
    waves = [[x] + [plane_swap(x, s) for s in ways] for x in waves]
    if aligned:
        waves[0][1:], waves[1][0] = lax.optimization_barrier((waves[0][1:], waves[1][0]))

    parts = held[0] + [(0, pooled_strip(0))]
    parts = [x for _, x in sorted(parts, key=lambda pair: pair[0])]
    pixels = rows * nrow * width * n

    def finish(out, pieces, spots, parts=()):
        coarse = [shape(cr, n * cols, ch)] if parts else []
        count, tall = len(pieces), pieces[0].shape[0]
        return pl.pallas_call(
            functools.partial(finish_kernel, float(pixels) ** -0.5, zs, spots, len(parts)),
            out_shape=[shape(9, ch, ch, dtype=F32)] + coarse,
            in_specs=[vmem()] * (count + len(parts)) + [hbm() for _ in out],
            out_specs=[hbm()] + [hbm() for _ in coarse],
            input_output_aliases={count + len(parts): 0} if out else {},
            scratch_shapes=[
                pltpu.VMEM((count, tall, 9, depth // 9, half), F32),
                pltpu.SemaphoreType.DMA((count, tall, 3)),
            ]
            + [x for c in coarse for x in (pltpu.VMEM(c.shape, BF), pltpu.SemaphoreType.DMA((1,)))],
            compiler_params=params(8),
            cost_estimate=cost(1 << 20, 4 << 20),
            name="finish",
        )(*pieces, *parts, *out)

    out, others, spots = [], [], ()
    for k, wave in enumerate(waves):
        if k:
            wave[1:], out = lax.optimization_barrier((wave[1:], out))
        swapped = core_swap(jnp.stack(wave))
        here = [(s, k * wave[0].shape[0]) for s in [0] + ways]
        places = [(0, *spot) for spot in here] + [(1, *spot) for spot in spots]
        out = finish(out, wave + others, tuple(places))
        others, spots = [swapped[i] for i in range(len(wave))], here
    grad_weight, grad_coarse = finish(out, others, tuple((1, *spot) for spot in spots), parts)
    return (done[0][None], grad_coarse[None], grad_weight.reshape(3, 3, ch, ch))


def piece_sizes(groups):
    sizes = [groups * 3 // 4, groups // 8]
    return sizes + [groups - sum(sizes)]


def solution(mesh):
    return jax.shard_map(
        per_device,
        mesh=mesh,
        in_specs=(
            P(None, "row", "col", None),
            P(None, ("row", "col"), None, None),
            P(),
            P(),
            P(),
            P(None, "row", "col", None),
        ),
        out_specs=(P(None, "row", "col", None), P(None, ("row", "col"), None, None), P()),
        check_vma=False,
    )
```
